32 devices in a mesh: trow: 4 (over y, core), tcol: 8 (over z, x).
Axes of the slice: x: 2, y: 2, z: 4, core: 2. Of those that a mesh axis runs over, the one named last changes fastest.
Arguments:
- object_planes: float32 [2, 1024, 2048], P(None, 'trow', 'tcol'), may hold values from -5 to 5
- probe: float32 [2, 128, 128], replicated, may hold values from -5 to 5
- intensities: bfloat16 [4, 8, 48, 128, 128], P('trow', 'tcol'), may hold values from 0 to 2
- row_offsets: int32 [4, 8, 48], P('trow', 'tcol'), may hold values from -64 to 192
- col_offsets: int32 [4, 8, 48], P('trow', 'tcol'), may hold values from -64 to 192
- counts: int32 [32], P(('trow', 'tcol')), may hold values from 1 to 48, 960 in all
Outputs:
- object_grad: float32 [2, 1024, 2048], P(None, 'trow', 'tcol')
- probe_grad: float32 [2, 128, 128], replicated
The draws below stay inside these ranges and needn't reach their ends.
All inputs are finite; a program needn't handle non-finite values. No bound on the sum of `counts` on one device may be relied on, other than what follows from the above.
Results may differ from the reference program's by a relative error of at most 0.0003.
Values sent between devices are 32-bit elements; how exact they have to be, the bound alone decides.
No kernel may reach another device: no remote copies, remote signals or barrier semaphores. Data moves between devices by JAX's collectives and lax.ppermute only.
A program may use at most 64 MiB of HBM per device.

```python
import math
import jax
import jax.numpy as jnp
import numpy as np
from jax import lax

P_SIZE = 128
TH = 256
TW = 256
POS_DEV = 48
NR = 1024
NC = 2048
N_TROW = 4
N_TCOL = 8


def touch_ends(entries, key, least, high):
    longest = entries.shape.index(max(entries.shape))
    spots = []
    for shift in (0, 1):
        where = [jax.random.randint(jax.random.fold_in(key, axis), (), 0, length) for axis, length in enumerate(entries.shape)]
        where[longest] = (where[longest] + shift) % entries.shape[longest]
        spots.append(tuple(where))
    return entries.at[spots[0]].set(least).at[spots[1]].set(high)


def levels(own_key, shape, shards, low, high):
    factor_of, own = 1.0, jax.random.fold_in(own_key, 6)
    for position, blocks in shards:
        steps = jnp.exp(jax.random.uniform(jax.random.fold_in(own, position), (blocks,), jnp.float32, low / len(shards), high / len(shards)))
        factor_of = factor_of * jnp.repeat(steps, shape[position] // blocks).reshape([-1 if axis == position else 1 for axis in range(len(shape))])
    return factor_of


def split_up(count, total, bound, slope):
    loads = [(1 << 20) // math.isqrt(grade ** slope) + 1 for grade in range(2, count + 1)]
    rest, given = total - bound - (count - 1), [1] * (count - 1)
    while rest > 0:
        free = [i for i in range(count - 1) if given[i] < bound]
        mass, remaining = sum([loads[i] for i in free]), rest
        for i in free:
            addition = min(bound - given[i], max(1, remaining * loads[i] // mass), rest)
            given[i] = given[i] + addition
            rest = rest - addition
    return np.array([bound] + given)


def ragged(own_key, number_of, total, bound, lean):
    if number_of == 2:
        one = jax.random.randint(own_key, (), max(1, total - bound), min(bound, total - 1) + 1)
        return jnp.stack([one, total - one])
    lengths = jnp.asarray(split_up(number_of, total, bound, lean), jnp.int32)
    couples = (number_of - 1) // 2
    source_of, receiver = lengths[1:1 + 2 * couples:2], lengths[2:2 + 2 * couples:2]
    slack = jnp.minimum(source_of - 1, bound - receiver)
    shifted = jax.random.randint(jax.random.fold_in(own_key, 1), (couples,), 0, 1 << 20) % (slack + 1)
    lengths = lengths.at[1:1 + 2 * couples:2].set(source_of - shifted).at[2:2 + 2 * couples:2].set(receiver + shifted)
    return lengths[jax.random.permutation(jax.random.fold_in(own_key, 2), number_of)]


def gaussian(own_key, extent, scale, reach, cuts=(), kind=jnp.bfloat16):
    result = jax.random.normal(own_key, extent, jnp.float32) * scale
    if len(cuts) > 0:
        result = levels(own_key, extent, cuts, -0.22, 0.18) * result
    return jnp.clip(result, min=-reach, max=reach).astype(kind)


def setup_inputs(seed: int = 0) -> dict:
    key_of = jax.random.split(jax.random.key(seed), 7)
    return {
        "object_planes": gaussian(key_of[0], (2, NR, NC), 0.7, 5.0, ((1, 4), (2, 8)), jnp.float32),
        "probe": gaussian(key_of[1], (2, P_SIZE, P_SIZE), 0.7, 5.0, (), jnp.float32),
        "intensities": jnp.clip(2.0 * jax.random.uniform(key_of[2], (N_TROW, N_TCOL, POS_DEV, P_SIZE, P_SIZE), jnp.float32) ** levels(key_of[2], (N_TROW, N_TCOL, POS_DEV, P_SIZE, P_SIZE), ((0, 4), (1, 8)), -0.2, 0.2), 0.0, 2.0).astype(jnp.bfloat16),
        "row_offsets": touch_ends(jax.random.randint(key_of[3], (N_TROW, N_TCOL, POS_DEV), 0 - P_SIZE // 2, TH - P_SIZE // 2 + 1), jax.random.fold_in(key_of[3], 1), 0 - P_SIZE // 2, (TH - P_SIZE // 2 + 1) - 1).astype(jnp.int32),
        "col_offsets": touch_ends(jax.random.randint(key_of[4], (N_TROW, N_TCOL, POS_DEV), 0 - P_SIZE // 2, TW - P_SIZE // 2 + 1), jax.random.fold_in(key_of[4], 1), 0 - P_SIZE // 2, (TW - P_SIZE // 2 + 1) - 1).astype(jnp.int32),
        "counts": ragged(key_of[5], N_TROW * N_TCOL, POS_DEV * N_TROW * N_TCOL * 5 // 8, POS_DEV, 2).astype(jnp.int32),
    }


def reference(object_planes, probe, intensities, row_offsets, col_offsets, counts):
    margin = P_SIZE // 2
    field = object_planes[0] + 1j * object_planes[1]
    probe_wave = probe[0] + 1j * probe[1]
    padded = jnp.pad(field, margin)
    row_table = row_offsets.reshape(N_TROW * N_TCOL, POS_DEV)
    col_table = col_offsets.reshape(N_TROW * N_TCOL, POS_DEV)
    measured_all = intensities.reshape(N_TROW * N_TCOL, POS_DEV, P_SIZE, P_SIZE)
    slots = jnp.arange(POS_DEV, dtype=jnp.int32)

    def device_step(carry, device):
        grad_pad, probe_sum = carry
        tile_row = (device // N_TCOL).astype(jnp.int32)
        tile_col = (device % N_TCOL).astype(jnp.int32)
        row_start = (tile_row * TH).astype(jnp.int32)
        col_start = (tile_col * TW).astype(jnp.int32)
        window = lax.dynamic_slice(padded, (row_start, col_start), (TH + P_SIZE, TW + P_SIZE))
        row_list = row_table[device].astype(jnp.int32)
        col_list = col_table[device].astype(jnp.int32)

        def take_patch(row_at, col_at):
            return lax.dynamic_slice(window, (row_at + margin, col_at + margin), (P_SIZE, P_SIZE))
        patches = jax.vmap(take_patch)(row_list, col_list)
        exit_wave = probe_wave[None] * patches
        psi = jnp.fft.fft2(exit_wave, norm='ortho')
        measured = measured_all[device].astype(jnp.float32)
        live = (slots < counts[device]).astype(jnp.float32)
        fourier_grad = 2.0 * (jnp.abs(psi) ** 2 - measured) * psi
        exit_grad = jnp.fft.ifft2(fourier_grad, norm='ortho') * live[:, None, None]
        probe_sum = probe_sum + lax.optimization_barrier(jnp.sum(jnp.conj(patches) * exit_grad, axis=0))
        contrib = jnp.conj(probe_wave)[None] * exit_grad

        def add_patch(index, local):
            row_at = row_list[index] + margin
            col_at = col_list[index] + margin
            current = lax.dynamic_slice(local, (row_at, col_at), (P_SIZE, P_SIZE))
            return lax.dynamic_update_slice(local, current + contrib[index], (row_at, col_at))
        local = lax.fori_loop(0, POS_DEV, add_patch, jnp.zeros((TH + P_SIZE, TW + P_SIZE), padded.dtype))
        current = lax.dynamic_slice(grad_pad, (row_start, col_start), (TH + P_SIZE, TW + P_SIZE))
        grad_pad = lax.dynamic_update_slice(grad_pad, current + local, (row_start, col_start))
        return ((grad_pad, probe_sum), None)
    start = (jnp.zeros(padded.shape, padded.dtype), jnp.zeros((P_SIZE, P_SIZE), padded.dtype))
    devices = jnp.arange(N_TROW * N_TCOL, dtype=jnp.int32)
    (grad_pad, probe_sum), _ = lax.scan(device_step, start, devices)
    grad_field = grad_pad[margin:margin + NR, margin:margin + NC]
    object_grad = jnp.stack([jnp.real(grad_field), jnp.imag(grad_field)]).astype(jnp.float32)
    probe_sum = probe_sum / jnp.sqrt(jnp.float32(POS_DEV * N_TROW * N_TCOL))
    probe_grad = jnp.stack([jnp.real(probe_sum), jnp.imag(probe_sum)]).astype(jnp.float32)
    return (object_grad, probe_grad)
```

```python
import functools

import jax
import jax.numpy as jnp
import numpy as np
from jax import lax
from jax.experimental import pallas as pl
from jax.experimental.pallas import tpu as pltpu
from jax.sharding import PartitionSpec as P

LANES = 128
VMEM_BYTES = 48 * 1024 * 1024
GROUP = 4


def dft_tables(length):
    index = np.arange(length)
    angle = -2.0 * np.pi * (np.outer(index, index) % length) / length
    cosine, sine = np.cos(angle) / np.sqrt(length), np.sin(angle) / np.sqrt(length)
    right = np.block([[cosine, sine], [-sine, cosine]])
    tables = []
    for table in (right, right.T):
        high = table.astype(jnp.bfloat16)
        low = (table - high.astype(np.float64)).astype(jnp.bfloat16)
        tables += [high, low]
    return np.stack(tables)


def split(value):
    high = value.astype(jnp.bfloat16)
    low = (value - high.astype(jnp.float32)).astype(jnp.bfloat16)
    return high, low


def dot(a, b):
    return jnp.dot(a, b, preferred_element_type=jnp.float32)


def times_table(value, high, low):
    big, small = split(value)
    return dot(big, high) + (dot(small, high) + dot(big, low))


def table_times(high, low, value):
    big, small = split(value)
    return dot(high, big) + (dot(high, small) + dot(low, big))


def main_kernel(
    rows_ref, cols_ref, count_ref,
    centre_ref, top_ref, bottom_ref, left_ref, right_ref, probe_ref, measured_ref, table_ref,
    grad_centre_ref, grad_top_ref, grad_bottom_ref, probe_sum_ref,
    window, grad,
):
    size = probe_ref.shape[1]
    margin = size // 2
    height, width = centre_ref.shape[1:]
    tiles = width // LANES
    columns = tiles + 2
    slots = measured_ref.shape[0]
    half = (height + size) // 2

    for plane in range(2):
        base = plane * columns
        for tile in range(tiles):
            lanes = slice(tile * LANES, (tile + 1) * LANES)
            window[base + 1 + tile, :margin] = top_ref[plane, :, lanes]
            window[base + 1 + tile, margin : margin + height] = centre_ref[plane, :, lanes]
            window[base + 1 + tile, margin + height :] = bottom_ref[plane, :, lanes]
        window[base, :half] = left_ref[plane]
        window[base, half:] = pltpu.roll(left_ref[plane], margin, axis=1)
        window[base + tiles + 1, :half] = right_ref[plane]
        window[base + tiles + 1, half:] = pltpu.roll(right_ref[plane], margin, axis=1)
    grad[...] = jnp.zeros_like(grad)
    probe_sum_ref[...] = jnp.zeros_like(probe_sum_ref)

    lane = lax.broadcasted_iota(jnp.int32, (size, LANES), 1)
    count = count_ref[0]

    def place(slot):
        row = rows_ref[slot] + margin
        col = cols_ref[slot] + LANES
        tile = lax.shift_right_logical(col, 7)
        return row, tile, col & (LANES - 1)

    def one_pair(first):
        patches, waves = [], []
        for slot in (first, first + 1):
            row, tile, turn = place(slot)
            here = lane >= turn
            patch = [
                jnp.where(
                    here,
                    window[plane * columns + tile, pl.ds(row, size), :],
                    window[plane * columns + tile + 1, pl.ds(row, size), :],
                )
                for plane in range(2)
            ]
            probe = [pltpu.roll(probe_ref[plane], turn, axis=1) for plane in range(2)]
            wave = jnp.concatenate(
                [
                    probe[0] * patch[0] - probe[1] * patch[1],
                    probe[0] * patch[1] + probe[1] * patch[0],
                ],
                axis=1,
            )
            patches.append((patch, probe))
            waves.append(wave)
        rows = jnp.concatenate(waves, axis=0)
        middle = times_table(rows, table_ref[0], table_ref[1])
        beside = jnp.concatenate(
            [
                jnp.concatenate([middle[:size, :size], middle[size:, :size]], axis=1),
                jnp.concatenate([middle[:size, size:], middle[size:, size:]], axis=1),
            ],
            axis=0,
        )
        psi = table_times(table_ref[2], table_ref[3], beside)
        real, imag = psi[:size], psi[size:]
        weights = []
        for member, slot in enumerate((first, first + 1)):
            lanes = slice(member * size, (member + 1) * size)
            scale = jnp.where(slot < count, 2.0, 0.0).astype(jnp.float32)
            power = real[:, lanes] * real[:, lanes] + imag[:, lanes] * imag[:, lanes]
            weights.append((power - measured_ref[slot].astype(jnp.float32)) * scale)
        weight = jnp.concatenate(weights, axis=1)
        psi = jnp.concatenate([weight * real, weight * imag], axis=0)
        back = table_times(table_ref[0], table_ref[1], psi)
        rows = jnp.concatenate(
            [
                jnp.concatenate([back[:size, :size], back[size:, :size]], axis=1),
                jnp.concatenate([back[:size, size:], back[size:, size:]], axis=1),
            ],
            axis=0,
        )
        exits = times_table(rows, table_ref[2], table_ref[3])
        for member, slot in enumerate((first, first + 1)):
            patch, probe = patches[member]
            row, tile, turn = place(slot)
            here = lane >= turn
            exit_real = exits[member * size : (member + 1) * size, :size]
            exit_imag = exits[member * size : (member + 1) * size, size:]
            terms = (
                patch[0] * exit_real + patch[1] * exit_imag,
                patch[0] * exit_imag - patch[1] * exit_real,
            )
            adds = (
                probe[0] * exit_real + probe[1] * exit_imag,
                probe[0] * exit_imag - probe[1] * exit_real,
            )
            back_turn = (LANES - turn) & (LANES - 1)
            for plane in range(2):
                probe_sum_ref[plane] += pltpu.roll(terms[plane], back_turn, axis=1)
                at = plane * columns + tile
                grad[at, pl.ds(row, size), :] += jnp.where(here, adds[plane], 0.0)
                grad[at + 1, pl.ds(row, size), :] += jnp.where(here, 0.0, adds[plane])

    def step(index, carry):
        for member in range(0, GROUP, 2):
            one_pair(index * GROUP + member)
        return carry

    lax.fori_loop(0, (count + GROUP - 1) // GROUP, step, 0)

    for plane in range(2):
        base = plane * columns
        for tile in range(columns):
            lanes = slice(tile * LANES, (tile + 1) * LANES)
            grad_top_ref[plane, :, lanes] = grad[base + tile, :margin]
            grad_centre_ref[plane, :, lanes] = grad[base + tile, margin : margin + height]
            grad_bottom_ref[plane, :, lanes] = grad[base + tile, margin + height :]


def main_call(rows, cols, count, centre, top, bottom, left, right, probe, measured, tables):
    height, width = centre.shape[1:]
    size = probe.shape[1]
    margin = size // 2
    columns = width // LANES + 2
    wide = columns * LANES
    smem = pl.BlockSpec(memory_space=pltpu.SMEM)
    vmem = pl.BlockSpec(memory_space=pltpu.VMEM)
    f32 = jnp.float32
    return pl.pallas_call(
        main_kernel,
        out_shape=(
            jax.ShapeDtypeStruct((2, height, wide), f32),
            jax.ShapeDtypeStruct((2, margin, wide), f32),
            jax.ShapeDtypeStruct((2, margin, wide), f32),
            jax.ShapeDtypeStruct((2, size, size), f32),
        ),
        in_specs=[smem] * 3 + [vmem] * 8,
        out_specs=(vmem,) * 4,
        scratch_shapes=[
            pltpu.VMEM((2 * columns, height + size, LANES), f32),
            pltpu.VMEM((2 * columns, height + size, LANES), f32),
        ],
        compiler_params=pltpu.CompilerParams(vmem_limit_bytes=VMEM_BYTES),
        name="slots",
    )(rows, cols, count, centre, top, bottom, left, right, probe, measured, tables)


def shifted(value, axis, steps):
    count = lax.axis_size(axis)
    first, last = max(0, -steps), min(count, count - steps)
    return lax.ppermute(value, axis, [(source, source + steps) for source in range(first, last)])


def swapped(value, axis, bit):
    return lax.ppermute(value, axis, [(i, i ^ bit) for i in range(lax.axis_size(axis))])


def sum_over_all(value):
    n_row, n_col = lax.axis_size("trow"), lax.axis_size("tcol")
    odd = lax.axis_index("trow") % 2
    mine = lax.dynamic_index_in_dim(value, odd, 0, keepdims=False)
    other = lax.dynamic_index_in_dim(value, 1 - odd, 0, keepdims=False)
    mine = mine + swapped(other, "trow", 1)
    bit = 2
    while bit < n_row:
        mine = mine + swapped(mine, "trow", bit)
        bit *= 2
    bit = 1
    while bit < n_col:
        mine = mine + swapped(mine, "tcol", bit)
        bit *= 2
    other = swapped(mine, "trow", 1)
    return jnp.where(odd == 0, jnp.stack([mine, other]), jnp.stack([other, mine]))


def body(tables, object_planes, probe, intensities, row_offsets, col_offsets, counts):
    size = probe.shape[1]
    margin = size // 2
    height, width = object_planes.shape[1:]
    half = (height + size) // 2

    top = shifted(object_planes[:, height - margin :], "trow", 1)
    bottom = shifted(object_planes[:, :margin], "trow", -1)
    tall = jnp.concatenate([top, object_planes, bottom], axis=1)
    last, first = tall[:, :, width - margin :], tall[:, :, :margin]
    left = shifted(jnp.concatenate([last[:, half:], last[:, :half]], axis=2), "tcol", 1)
    right = shifted(jnp.concatenate([first[:, :half], first[:, half:]], axis=2), "tcol", -1)

    centre, upper, lower, probe_sum = main_call(
        row_offsets.reshape(-1), col_offsets.reshape(-1), counts,
        object_planes, top, bottom, left, right, probe,
        intensities.reshape(-1, size, size), tables,
    )
    probe_total = sum_over_all(probe_sum)
    devices = lax.axis_size("trow") * lax.axis_size("tcol")
    probe_grad = probe_total / jnp.sqrt(jnp.float32(intensities.shape[2] * devices))

    from_below = shifted(upper, "trow", -1)
    from_above = shifted(lower, "trow", 1)
    centre = centre.at[:, height - margin :].add(from_below)
    centre = centre.at[:, :margin].add(from_above)
    start = LANES
    from_right = shifted(centre[:, :, start - margin : start], "tcol", -1)
    from_left = shifted(centre[:, :, start + width : start + width + margin], "tcol", 1)
    result = centre[:, :, start : start + width]
    result = result.at[:, :, width - margin :].add(from_right)
    result = result.at[:, :, :margin].add(from_left)
    return (result, probe_grad)


def solution(mesh):
    tables = dft_tables(LANES)
    inner = jax.shard_map(
        body,
        mesh=mesh,
        in_specs=(
            P(),
            P(None, "trow", "tcol"),
            P(),
            P("trow", "tcol", None, None, None),
            P("trow", "tcol", None),
            P("trow", "tcol", None),
            P(("trow", "tcol")),
        ),
        out_specs=(P(None, "trow", "tcol"), P()),
        check_vma=False,
    )

    def run(*args):
        return inner(jnp.asarray(tables), *args)

    return run
```

```python
import jax
import jax.numpy as jnp
import numpy as np
from jax import lax
from jax.experimental import pallas as pl
from jax.experimental.pallas import tpu as pltpu
from jax.sharding import PartitionSpec as P

LANES = 128
VMEM_BYTES = 56 * 1024 * 1024
GROUP = 8
F32 = jnp.float32
ANY = pl.BlockSpec(memory_space=pl.ANY)
VMEM = pl.BlockSpec(memory_space=pltpu.VMEM)
SMEM = pl.BlockSpec(memory_space=pltpu.SMEM)


def dft_tables(length):
    index = np.arange(length)
    angle = -2.0 * np.pi * (np.outer(index, index) % length) / length
    cosine, sine = np.cos(angle) / np.sqrt(length), np.sin(angle) / np.sqrt(length)
    right = np.block([[cosine, sine], [-sine, cosine]])
    tables = []
    for table in (right, right.T):
        high = table.astype(jnp.bfloat16)
        low = (table - high.astype(np.float64)).astype(jnp.bfloat16)
        tables += [high, low]
    return np.stack(tables)


def split(value):
    high = value.astype(jnp.bfloat16)
    low = (value - high.astype(F32)).astype(jnp.bfloat16)
    return high, low


def dot(a, b):
    return jnp.dot(a, b, preferred_element_type=F32)


def times_table(value, high, low):
    big, small = split(value)
    return dot(jnp.concatenate([big, small, big], axis=1), jnp.concatenate([high, high, low], axis=0))


def table_times(high, low, value):
    big, small = split(value)
    return dot(jnp.concatenate([high, high, low], axis=1), jnp.concatenate([big, small, big], axis=0))


def folded(tall, low_lanes):
    half = tall.shape[0] // 2
    lane = lax.broadcasted_iota(jnp.int32, (half, LANES), 1)
    here = (lane < LANES // 2) == low_lanes
    return jnp.where(here, tall[:half], pltpu.roll(tall[half:], LANES // 2, axis=1))


def side_kernel(centre_ref, near_ref, far_ref, near_out, far_out, tall, sem):
    height, width = centre_ref.shape[1:]
    margin = near_ref.shape[1]
    odd_row = lax.axis_index("trow") % 2
    odd_col = lax.axis_index("tcol") % 2
    copies = []
    for index in range(2):
        right = (odd_col == 0) if index == 0 else (odd_col == 1)
        lanes = pl.ds(pl.multiple_of(jnp.where(right, width - LANES, 0), LANES), LANES)
        near_at = pl.multiple_of(jnp.where(odd_row == 1, 0, margin + height), 8)
        far_at = pl.multiple_of(jnp.where(odd_row == 1, margin + height, 0), 8)
        for plane in range(2):
            copies += [
                (centre_ref.at[plane, :, lanes], tall.at[index, plane, pl.ds(margin, height)]),
                (near_ref.at[plane, :, lanes], tall.at[index, plane, pl.ds(near_at, margin)]),
                (far_ref.at[plane, :, lanes], tall.at[index, plane, pl.ds(far_at, margin)]),
            ]
    copies = [pltpu.make_async_copy(a, b, sem.at[i]) for i, (a, b) in enumerate(copies)]
    for copy in copies:
        copy.start()
    for copy in copies:
        copy.wait()
    for plane in range(2):
        near_out[plane] = folded(tall[0, plane], odd_col == 1)
        far_out[plane] = folded(tall[1, plane], odd_col == 0)


def side_call(centre, near, far):
    height = centre.shape[1] + 2 * near.shape[1]
    shape = jax.ShapeDtypeStruct((2, height // 2, LANES), F32)
    return pl.pallas_call(
        side_kernel,
        out_shape=(shape, shape),
        in_specs=[ANY] * 3,
        out_specs=(VMEM, VMEM),
        scratch_shapes=[pltpu.VMEM((2, 2, height, LANES), F32), pltpu.SemaphoreType.DMA((12,))],
        name="side_columns",
    )(centre, near, far)


def main_kernel(
    rows_ref, cols_ref, count_ref,
    centre_ref, near_row_ref, far_row_ref, near_col_ref, far_col_ref, probe_ref, measured_ref, table_ref,
    centre_out, near_row_out, far_row_out, side_out, mine_out, other_out,
    window, grad, sides, probe, measured, table, probe_sum, rows_out, side, centre_sem, edge_sem, small_sem, measured_sem, out_sem,
):
    size = probe.shape[1]
    margin = size // 2
    height, width = centre_ref.shape[1:]
    tiles = width // LANES
    columns = tiles + 2
    slots = measured_ref.shape[0]
    half = (height + size) // 2
    odd_row = lax.axis_index("trow") % 2
    odd_col = lax.axis_index("tcol") % 2
    near_at = pl.multiple_of(jnp.where(odd_row == 1, 0, margin + height), 8)
    far_at = pl.multiple_of(jnp.where(odd_row == 1, margin + height, 0), 8)
    count = count_ref[0]
    groups = (count + GROUP - 1) // GROUP

    small = [
        pltpu.make_async_copy(probe_ref, probe, small_sem.at[0]),
        pltpu.make_async_copy(table_ref, table, small_sem.at[1]),
        pltpu.make_async_copy(near_col_ref, sides.at[0], small_sem.at[2]),
        pltpu.make_async_copy(far_col_ref, sides.at[1], small_sem.at[3]),
    ]
    for plane in range(2):
        for tile in range(tiles):
            lanes = slice(tile * LANES, (tile + 1) * LANES)
            to = window.at[plane * columns + 1 + tile]
            index = plane * tiles + tile
            small += [
                pltpu.make_async_copy(centre_ref.at[plane, :, lanes], to.at[pl.ds(margin, height)], centre_sem.at[index]),
                pltpu.make_async_copy(near_row_ref.at[plane, :, lanes], to.at[pl.ds(near_at, margin)], edge_sem.at[2 * index]),
                pltpu.make_async_copy(far_row_ref.at[plane, :, lanes], to.at[pl.ds(far_at, margin)], edge_sem.at[2 * index + 1]),
            ]

    def measured_copy(group):
        some = pl.ds(group * GROUP, GROUP)
        return pltpu.make_async_copy(measured_ref.at[some], measured.at[some], measured_sem.at[group])

    for copy in small:
        copy.start()
    for group in range(slots // GROUP):
        @pl.when(group < groups)
        def _():
            measured_copy(group).start()
    grad[...] = jnp.zeros_like(grad)
    probe_sum[...] = jnp.zeros_like(probe_sum)
    for copy in small:
        copy.wait()
    near_tile = jnp.where(odd_col == 1, 0, tiles + 1)
    far_tile = jnp.where(odd_col == 1, tiles + 1, 0)
    for plane in range(2):
        for index, tile in enumerate((near_tile, far_tile)):
            window[plane * columns + tile, :half] = sides[index, plane]
            window[plane * columns + tile, half:] = pltpu.roll(sides[index, plane], margin, axis=1)

    lane = lax.broadcasted_iota(jnp.int32, (size, LANES), 1)

    def place(slot):
        row = rows_ref[slot] + margin
        col = cols_ref[slot] + LANES
        tile = lax.shift_right_logical(col, 7)
        return row, tile, col & (LANES - 1)

    def load(first):
        kept, waves = [], []
        for slot in (first, first + 1):
            row, tile, turn = place(slot)
            here = lane >= turn
            patch = [
                jnp.where(
                    here,
                    window[plane * columns + tile, pl.ds(row, size), :],
                    window[plane * columns + tile + 1, pl.ds(row, size), :],
                )
                for plane in range(2)
            ]
            turned = [pltpu.roll(probe[plane], turn, axis=1) for plane in range(2)]
            wave_real = turned[0] * patch[0] - turned[1] * patch[1]
            wave_imag = turned[0] * patch[1] + turned[1] * patch[0]
            kept.append((patch, turned))
            waves.append(jnp.concatenate([wave_real, wave_imag], axis=1))
        return kept, jnp.concatenate(waves, axis=0)

    def regroup(pair):
        return jnp.concatenate(
            [
                jnp.concatenate([pair[:size, :size], pair[size:, :size]], axis=1),
                jnp.concatenate([pair[:size, size:], pair[size:, size:]], axis=1),
            ],
            axis=0,
        )

    def weigh(first, psi):
        real, imag = psi[:size], psi[size:]
        weights = []
        for member, slot in enumerate((first, first + 1)):
            lanes = slice(member * size, (member + 1) * size)
            scale = jnp.where(slot < count, 2.0, 0.0).astype(F32)
            power = real[:, lanes] * real[:, lanes] + imag[:, lanes] * imag[:, lanes]
            weights.append((power - measured[slot].astype(F32)) * scale)
        weight = jnp.concatenate(weights, axis=1)
        return jnp.concatenate([weight * real, weight * imag], axis=0)

    def add_up(first, kept, exits):
        for member, slot in enumerate((first, first + 1)):
            patch, turned = kept[member]
            row, tile, turn = place(slot)
            here = lane >= turn
            exit_real = exits[member * size : (member + 1) * size, :size]
            exit_imag = exits[member * size : (member + 1) * size, size:]
            terms = (patch[0] * exit_real + patch[1] * exit_imag, patch[0] * exit_imag - patch[1] * exit_real)
            adds = (turned[0] * exit_real + turned[1] * exit_imag, turned[0] * exit_imag - turned[1] * exit_real)
            back = (LANES - turn) & (LANES - 1)
            for plane in range(2):
                probe_sum[plane] += pltpu.roll(terms[plane], back, axis=1)
                at = plane * columns + tile
                grad[at, pl.ds(row, size), :] += jnp.where(here, adds[plane], 0.0)
                grad[at + 1, pl.ds(row, size), :] += jnp.where(here, 0.0, adds[plane])

    def step(group, carry):
        measured_copy(group).wait()
        firsts = [group * GROUP + member for member in range(0, GROUP, 2)]
        loaded = [load(first) for first in firsts]
        pairs = [regroup(times_table(wave, table[0], table[1])) for _, wave in loaded]
        pairs = [weigh(first, table_times(table[2], table[3], pair)) for first, pair in zip(firsts, pairs)]
        pairs = [regroup(table_times(table[0], table[1], pair)) for pair in pairs]
        pairs = [times_table(pair, table[2], table[3]) for pair in pairs]
        for first, (kept, _), pair in zip(firsts, loaded, pairs):
            add_up(first, kept, pair)
        return carry

    lax.fori_loop(0, groups, step, 0)

    total = lax.axis_size("trow") * lax.axis_size("tcol") * slots
    probe_sum[...] *= 1.0 / np.sqrt(np.float32(total))
    narrow = lax.broadcasted_iota(jnp.int32, (height + size, LANES), 1) < margin
    for plane in range(2):
        side[plane] = jnp.where(narrow, grad[plane * columns + tiles + 1], grad[plane * columns])
    outs = [
        pltpu.make_async_copy(probe_sum.at[odd_row], mine_out, out_sem.at[0]),
        pltpu.make_async_copy(probe_sum.at[1 - odd_row], other_out, out_sem.at[1]),
        pltpu.make_async_copy(side.at[:, pl.ds(margin, height)], side_out, out_sem.at[2]),
    ]
    for plane in range(2):
        for tile in range(tiles):
            lanes = slice(tile * LANES, (tile + 1) * LANES)
            at = grad.at[plane * columns + 1 + tile]
            outs += [
                (at.at[pl.ds(near_at, margin)], near_row_out.at[plane, :, lanes]),
                (at.at[pl.ds(far_at, margin)], far_row_out.at[plane, :, lanes]),
                (at.at[pl.ds(margin, height)], centre_out.at[plane, :, lanes]),
            ]
        lanes = slice(width, width + LANES)
        outs += [
            (side.at[plane, pl.ds(near_at, margin)], near_row_out.at[plane, :, lanes]),
            (side.at[plane, pl.ds(far_at, margin)], far_row_out.at[plane, :, lanes]),
        ]
    outs = outs[:3] + [pltpu.make_async_copy(a, b, out_sem.at[3 + i]) for i, (a, b) in enumerate(outs[3:])]
    for copy in outs:
        copy.start()
    for copy in outs:
        copy.wait()


def main_call(rows, cols, count, centre, near_row, far_row, near_col, far_col, probe, measured, tables):
    height, width = centre.shape[1:]
    size = probe.shape[1]
    margin = size // 2
    tiles = width // LANES
    columns = tiles + 2
    slots = measured.shape[0]
    return pl.pallas_call(
        main_kernel,
        out_shape=(
            jax.ShapeDtypeStruct((2, height, width), F32),
            jax.ShapeDtypeStruct((2, margin, width + LANES), F32),
            jax.ShapeDtypeStruct((2, margin, width + LANES), F32),
            jax.ShapeDtypeStruct((2, height, LANES), F32),
            jax.ShapeDtypeStruct((size, size), F32),
            jax.ShapeDtypeStruct((size, size), F32),
        ),
        in_specs=[SMEM] * 3 + [ANY] * 8,
        out_specs=(ANY,) * 6,
        scratch_shapes=[
            pltpu.VMEM((2 * columns, height + size, LANES), F32),
            pltpu.VMEM((2 * columns, height + size, LANES), F32),
            pltpu.VMEM((2,) + near_col.shape, F32),
            pltpu.VMEM(probe.shape, F32),
            pltpu.VMEM(measured.shape, measured.dtype),
            pltpu.VMEM(tables.shape, tables.dtype),
            pltpu.VMEM(probe.shape, F32),
            pltpu.VMEM((2, margin, LANES), F32),
            pltpu.VMEM((2, height + size, LANES), F32),
            pltpu.SemaphoreType.DMA((2 * tiles,)),
            pltpu.SemaphoreType.DMA((4 * tiles,)),
            pltpu.SemaphoreType.DMA((4,)),
            pltpu.SemaphoreType.DMA((slots // GROUP,)),
            pltpu.SemaphoreType.DMA((3 + 2 * (3 * tiles + 2),)),
        ],
        compiler_params=pltpu.CompilerParams(vmem_limit_bytes=VMEM_BYTES),
        name="slots",
    )(rows, cols, count, centre, near_row, far_row, near_col, far_col, probe, measured, tables)


def side_sum_kernel(side_ref, near_ref, far_ref, near_out, far_out, side):
    margin = near_ref.shape[1]
    height = side_ref.shape[1]
    odd_row = lax.axis_index("trow") % 2
    odd_col = lax.axis_index("tcol") % 2
    near_at = pl.multiple_of(jnp.where(odd_row == 1, 0, height - margin), 8)
    far_at = pl.multiple_of(jnp.where(odd_row == 1, height - margin, 0), 8)
    wide = near_ref.shape[2]
    side[...] = side_ref[...]
    for plane in range(2):
        side[plane, pl.ds(near_at, margin), :] += near_ref[plane, :, wide - LANES :]
        side[plane, pl.ds(far_at, margin), :] += far_ref[plane, :, wide - LANES :]
    for plane in range(2):
        near_out[plane] = folded(side[plane], odd_col == 0)
        far_out[plane] = folded(side[plane], odd_col == 1)


def side_sum_call(side, near, far):
    shape = jax.ShapeDtypeStruct((2, side.shape[1] // 2, LANES), F32)
    return pl.pallas_call(
        side_sum_kernel,
        out_shape=(shape, shape),
        in_specs=[VMEM] * 3,
        out_specs=(VMEM, VMEM),
        scratch_shapes=[pltpu.VMEM(side.shape, F32)],
        name="side_sums",
    )(side, near, far)


def final_kernel(centre_ref, near_row_ref, far_row_ref, near_col_ref, far_col_ref, out_ref):
    height, width = centre_ref.shape[1:]
    margin = near_row_ref.shape[1]
    half = height // 2
    odd_row = lax.axis_index("trow") % 2
    odd_col = lax.axis_index("tcol") % 2
    near_at = pl.multiple_of(jnp.where(odd_row == 1, 0, height - margin), 8)
    far_at = pl.multiple_of(jnp.where(odd_row == 1, height - margin, 0), 8)
    narrow = lax.broadcasted_iota(jnp.int32, (half, LANES), 1) < LANES // 2
    out_ref[...] = centre_ref[...]
    for plane in range(2):
        near = jnp.where(odd_col == 1, near_col_ref[plane], far_col_ref[plane])
        far = jnp.where(odd_col == 1, far_col_ref[plane], near_col_ref[plane])
        for first, left, right in (
            (0, near, far),
            (half, pltpu.roll(near, LANES // 2, axis=1), pltpu.roll(far, LANES // 2, axis=1)),
        ):
            rows = slice(first, first + half)
            out_ref[plane, rows, :LANES] += jnp.where(narrow, left, 0.0)
            out_ref[plane, rows, width - LANES :] += jnp.where(narrow, 0.0, right)
        out_ref[plane, pl.ds(near_at, margin), :] += near_row_ref[plane, :, :width]
        out_ref[plane, pl.ds(far_at, margin), :] += far_row_ref[plane, :, :width]


def final_call(centre, near_row, far_row, near_col, far_col):
    return pl.pallas_call(
        final_kernel,
        out_shape=jax.ShapeDtypeStruct(centre.shape, F32),
        in_specs=[VMEM] * 5,
        out_specs=VMEM,
        name="final_sums",
    )(centre, near_row, far_row, near_col, far_col)


def near_swap(value, axis):
    return lax.ppermute(value, axis, [(i, i ^ 1) for i in range(lax.axis_size(axis))])


def far_swap(value, axis):
    pairs = [(i, i + 1) for i in range(1, lax.axis_size(axis) - 1, 2)]
    return lax.ppermute(value, axis, pairs + [(j, i) for i, j in pairs])


def sum_over_all(mine, other):
    n_row, n_col = lax.axis_size("trow"), lax.axis_size("tcol")
    steps = [(1 << k, 0) for k in range(1, n_row.bit_length() - 1)] + [(0, 1 << k) for k in range(n_col.bit_length() - 1)]
    mine = mine + near_swap(other, "trow")
    turned = list(steps)
    for k in range(0, len(steps) - 1, 2):
        turned[k], turned[k + 1] = steps[k + 1], steps[k]
    for even, odd in zip(steps, turned):
        pairs = []
        for r in range(n_row):
            for c in range(n_col):
                dr, dc = odd if r % 2 else even
                pairs.append((r * n_col + c, (r ^ dr) * n_col + (c ^ dc)))
        mine = mine + lax.ppermute(mine, ("trow", "tcol"), pairs)
    other = near_swap(mine, "trow")
    odd = lax.axis_index("trow") % 2
    return jnp.where(odd == 0, jnp.stack([mine, other]), jnp.stack([other, mine]))


def body(tables, object_planes, probe, intensities, row_offsets, col_offsets, counts):
    size = probe.shape[1]
    margin = size // 2
    height, width = object_planes.shape[1:]
    odd = lax.axis_index("trow") % 2
    last, first = object_planes[:, height - margin :], object_planes[:, :margin]
    near_row = near_swap(jnp.where(odd == 0, last, first), "trow")
    far_row = far_swap(jnp.where(odd == 0, first, last), "trow")
    near_side, far_side = side_call(object_planes, near_row, far_row)
    near_col = near_swap(near_side, "tcol")
    far_col = far_swap(far_side, "tcol")

    centre, near_row, far_row, side, mine, other = main_call(
        row_offsets.reshape(-1), col_offsets.reshape(-1), counts,
        object_planes, near_row, far_row, near_col, far_col, probe,
        intensities.reshape(-1, size, size), tables,
    )
    probe_grad = sum_over_all(mine, other)
    near_row = near_swap(near_row, "trow")
    far_row = far_swap(far_row, "trow")
    near_side, far_side = side_sum_call(side, near_row, far_row)
    near_col = near_swap(near_side, "tcol")
    far_col = far_swap(far_side, "tcol")
    return (final_call(centre, near_row, far_row, near_col, far_col), probe_grad)


def solution(mesh):
    tables = dft_tables(LANES)
    inner = jax.shard_map(
        body,
        mesh=mesh,
        in_specs=(
            P(),
            P(None, "trow", "tcol"),
            P(),
            P("trow", "tcol", None, None, None),
            P("trow", "tcol", None),
            P("trow", "tcol", None),
            P(("trow", "tcol")),
        ),
        out_specs=(P(None, "trow", "tcol"), P()),
        check_vma=False,
    )

    def run(*args):
        return inner(jnp.asarray(tables), *args)

    return run
```

```python
import jax
import jax.numpy as jnp
import numpy as np
from jax import lax
from jax.experimental import pallas as pl
from jax.experimental.pallas import tpu as pltpu
from jax.sharding import PartitionSpec as P

LANES = 128
VMEM_BYTES = 24 * 1024 * 1024
GROUP = 8
F32 = jnp.float32
HBM = pl.BlockSpec(memory_space=pltpu.HBM)
VMEM = pl.BlockSpec(memory_space=pltpu.VMEM)
SMEM = pl.BlockSpec(memory_space=pltpu.SMEM)
PARAMS = pltpu.CompilerParams(vmem_limit_bytes=VMEM_BYTES)


def in_hbm(*arrays):
    return [pltpu.with_memory_space_constraint(array, pltpu.HBM) for array in arrays]


def in_vmem(*arrays):
    return [pltpu.with_memory_space_constraint(array, pltpu.VMEM) for array in arrays]


def near(shape, dtype=F32):
    return pltpu.VMEM(tuple(shape), dtype)


def dft_tables(length):
    index = np.arange(length)
    angle = -2.0 * np.pi * (np.outer(index, index) % length) / length
    cosine, sine = np.cos(angle) / np.sqrt(length), np.sin(angle) / np.sqrt(length)
    right = np.block([[cosine, sine], [-sine, cosine]])
    return np.stack([right, right.T]).astype(np.float32)


def split(value):
    high = value.astype(jnp.bfloat16)
    low = (value - high.astype(F32)).astype(jnp.bfloat16)
    return high, low


def dot(a, b):
    return jnp.dot(a, b, preferred_element_type=F32)


def times_table(value, high, low):
    big, small = split(value)
    return dot(jnp.concatenate([big, small, big], axis=1), jnp.concatenate([high, high, low], axis=0))


def table_times(high, low, value):
    big, small = split(value)
    return dot(jnp.concatenate([high, high, low], axis=1), jnp.concatenate([big, small, big], axis=0))


def folded(tall, low_lanes):
    half = tall.shape[0] // 2
    lane = lax.broadcasted_iota(jnp.int32, (half, LANES), 1)
    here = (lane < LANES // 2) == low_lanes
    return jnp.where(here, tall[:half], pltpu.roll(tall[half:], LANES // 2, axis=1))


def parities():
    return lax.axis_index("trow") % 2, lax.axis_index("tcol") % 2


def place_of(odd, low, high):
    near = pl.multiple_of(jnp.where(odd == 1, low, high), 8)
    far = pl.multiple_of(jnp.where(odd == 1, high, low), 8)
    return near, far


def edge_kernel(centre_ref, window, near_out, far_out, sem):
    height, width = centre_ref.shape[1:]
    margin = near_out.shape[1]
    columns = window.shape[0] // 2
    odd_row, _ = parities()
    near, far = place_of(odd_row, 0, height - margin)
    copies = [
        (centre_ref.at[:, pl.ds(near, margin)], near_out),
        (centre_ref.at[:, pl.ds(far, margin)], far_out),
    ]
    for plane in range(2):
        for tile in range(width // LANES):
            lanes = slice(tile * LANES, (tile + 1) * LANES)
            copies.append((centre_ref.at[plane, :, lanes], window.at[plane * columns + 1 + tile, pl.ds(margin, height)]))
    copies = [pltpu.make_async_copy(a, b, sem.at[i]) for i, (a, b) in enumerate(copies)]
    for copy in copies:
        copy.start()
    for copy in copies:
        copy.wait()


def edge_call(centre, margin):
    height, width = centre.shape[1:]
    tiles = width // LANES
    edge = near((2, margin, width))
    return pl.pallas_call(
        edge_kernel,
        out_shape=(near((2 * (tiles + 2), height + 2 * margin, LANES)), edge, edge),
        in_specs=[HBM],
        out_specs=(VMEM,) * 3,
        scratch_shapes=[pltpu.SemaphoreType.DMA((2 + 2 * tiles,))],
        compiler_params=PARAMS,
        name="edge_rows",
    )(*in_hbm(centre))


def ready_kernel(probe_ref, measured_ref, table_ref, probe, measured, tables, table, sem):
    copies = [(table_ref, table), (probe_ref, probe), (measured_ref, measured)]
    copies = [pltpu.make_async_copy(a, b, sem.at[i]) for i, (a, b) in enumerate(copies)]
    for copy in copies:
        copy.start()
    copies[0].wait()
    for index in range(2):
        tables[2 * index], tables[2 * index + 1] = split(table[index])
    copies[1].wait()
    copies[2].wait()


def ready_call(probe, measured, table):
    return pl.pallas_call(
        ready_kernel,
        out_shape=(
            near(probe.shape),
            near(measured.shape, measured.dtype),
            near((4,) + table.shape[1:], jnp.bfloat16),
        ),
        in_specs=[HBM] * 3,
        out_specs=(VMEM,) * 3,
        scratch_shapes=[pltpu.VMEM(table.shape, F32), pltpu.SemaphoreType.DMA((3,))],
        compiler_params=PARAMS,
        name="ready",
    )(*in_hbm(probe, measured, table))


def side_kernel(tile_ref, near_ref, far_ref, window, near_out, far_out):
    margin = near_ref.shape[1]
    columns = window.shape[0] // 2
    odd_row, odd_col = parities()
    bottom = window.shape[1] - margin
    near, far = place_of(odd_row, 0, bottom)
    for plane in range(2):
        for tile in range(columns - 2):
            lanes = slice(tile * LANES, (tile + 1) * LANES)
            window[plane * columns + 1 + tile, margin:bottom] = tile_ref[plane * columns + 1 + tile, margin:bottom]
            window[plane * columns + 1 + tile, pl.ds(near, margin), :] = near_ref[plane, :, lanes]
            window[plane * columns + 1 + tile, pl.ds(far, margin), :] = far_ref[plane, :, lanes]
    for plane in range(2):
        near_tile = plane * columns + jnp.where(odd_col == 1, 1, columns - 2)
        far_tile = plane * columns + jnp.where(odd_col == 1, columns - 2, 1)
        near_out[plane] = folded(window[near_tile], odd_col == 1)
        far_out[plane] = folded(window[far_tile], odd_col == 0)


def side_call(window, near_row, far_row):
    shape = near((2, window.shape[1] // 2, LANES))
    return pl.pallas_call(
        side_kernel,
        out_shape=(near(window.shape), shape, shape),
        in_specs=[VMEM] * 3,
        out_specs=(VMEM,) * 3,
        compiler_params=PARAMS,
        name="side_columns",
    )(*in_vmem(window, near_row, far_row))


def sort_slots(cols_ref, count, inner_width, order):
    def visit(slot, inner):
        col = cols_ref[slot]
        is_inner = jnp.logical_and(col >= 0, col <= inner_width)
        order[jnp.where(is_inner, inner, order.shape[0] - 1 - (slot - inner))] = slot
        return inner + is_inner.astype(jnp.int32)

    return lax.fori_loop(0, count, visit, jnp.int32(0))


def run_slots(first_group, last_group, inner, count, order, rows_ref, cols_ref, window, probe, measured, table, grad, probe_sum):
    size = probe.shape[1]
    margin = size // 2
    columns = window.shape[0] // 2
    lane = lax.broadcasted_iota(jnp.int32, (size, LANES), 1)

    def find(index):
        at = jnp.where(index < inner, index, jnp.maximum(order.shape[0] - 1 - (index - inner), 0))
        live = index < count
        slot = jnp.where(live, order[at], 0)
        row = rows_ref[slot] + margin
        col = cols_ref[slot] + LANES
        scale = jnp.where(live, 2.0, 0.0).astype(F32)
        return slot, row, lax.shift_right_logical(col, 7), col & (LANES - 1), scale

    def load(pair):
        kept, waves = [], []
        for _, row, tile, turn, _ in pair:
            here = lane >= turn
            patch = [
                jnp.where(
                    here,
                    window[plane * columns + tile, pl.ds(row, size), :],
                    window[plane * columns + tile + 1, pl.ds(row, size), :],
                )
                for plane in range(2)
            ]
            turned = [pltpu.roll(probe[plane], turn, axis=1) for plane in range(2)]
            wave_real = turned[0] * patch[0] - turned[1] * patch[1]
            wave_imag = turned[0] * patch[1] + turned[1] * patch[0]
            kept.append((patch, turned))
            waves.append(jnp.concatenate([wave_real, wave_imag], axis=1))
        return kept, jnp.concatenate(waves, axis=0)

    def regroup(pair):
        return jnp.concatenate(
            [
                jnp.concatenate([pair[:size, :size], pair[size:, :size]], axis=1),
                jnp.concatenate([pair[:size, size:], pair[size:, size:]], axis=1),
            ],
            axis=0,
        )

    def weigh(pair, psi):
        real, imag = psi[:size], psi[size:]
        weights = []
        for member, (slot, _, _, _, scale) in enumerate(pair):
            lanes = slice(member * size, (member + 1) * size)
            power = real[:, lanes] * real[:, lanes] + imag[:, lanes] * imag[:, lanes]
            weights.append((power - measured[slot].astype(F32)) * scale)
        weight = jnp.concatenate(weights, axis=1)
        return jnp.concatenate([weight * real, weight * imag], axis=0)

    def add_up(pair, kept, exits):
        for member, (_, row, tile, turn, _) in enumerate(pair):
            patch, turned = kept[member]
            here = lane >= turn
            exit_real = exits[member * size : (member + 1) * size, :size]
            exit_imag = exits[member * size : (member + 1) * size, size:]
            terms = (patch[0] * exit_real + patch[1] * exit_imag, patch[0] * exit_imag - patch[1] * exit_real)
            adds = (turned[0] * exit_real + turned[1] * exit_imag, turned[0] * exit_imag - turned[1] * exit_real)
            back = (LANES - turn) & (LANES - 1)
            for plane in range(2):
                probe_sum[plane] += pltpu.roll(terms[plane], back, axis=1)
                at = plane * columns + tile
                grad[at, pl.ds(row, size), :] += jnp.where(here, adds[plane], 0.0)
                grad[at + 1, pl.ds(row, size), :] += jnp.where(here, 0.0, adds[plane])

    def step(group, carry):
        slots = [find(group * GROUP + member) for member in range(GROUP)]
        pairs = [slots[member : member + 2] for member in range(0, GROUP, 2)]
        loaded = [load(pair) for pair in pairs]
        waves = [regroup(times_table(wave, table[0], table[1])) for _, wave in loaded]
        waves = [weigh(pair, table_times(table[2], table[3], wave)) for pair, wave in zip(pairs, waves)]
        waves = [regroup(table_times(table[0], table[1], wave)) for wave in waves]
        waves = [times_table(wave, table[2], table[3]) for wave in waves]
        for pair, (kept, _), wave in zip(pairs, loaded, waves):
            add_up(pair, kept, wave)
        return carry

    lax.fori_loop(first_group, last_group, step, 0)


def inner_kernel(rows_ref, cols_ref, count_ref, window, probe, measured, table, grad, probe_sum, order):
    count = count_ref[0]
    grad[...] = jnp.zeros_like(grad)
    probe_sum[...] = jnp.zeros_like(probe_sum)
    inner_width = (window.shape[0] // 2 - 2) * LANES - probe.shape[1]
    inner = sort_slots(cols_ref, count, inner_width, order)
    run_slots(0, inner // GROUP, inner, count, order, rows_ref, cols_ref, window, probe, measured, table, grad, probe_sum)


def inner_call(rows, cols, count, window, probe, measured, tables):
    return pl.pallas_call(
        inner_kernel,
        out_shape=(near(window.shape), near(probe.shape)),
        in_specs=[SMEM] * 3 + [VMEM] * 4,
        out_specs=(VMEM,) * 2,
        scratch_shapes=[pltpu.SMEM((measured.shape[0],), jnp.int32)],
        compiler_params=PARAMS,
        cost_estimate=pl.CostEstimate(flops=10**10, bytes_accessed=2 * 10**7, transcendentals=0),
        name="slots_inside",
    )(rows, cols, count, *in_vmem(window, probe, measured, tables))


def outer_kernel(
    rows_ref, cols_ref, count_ref, window_ref, near_col_ref, far_col_ref, probe, measured, table, grad_ref, probe_ref,
    grad, near_row_out, far_row_out, side_out, mine_out, other_out, window, probe_sum, order,
):
    size = probe.shape[1]
    margin = size // 2
    columns = window.shape[0] // 2
    tall = window.shape[1]
    half = tall // 2
    odd_row, odd_col = parities()
    near, far = place_of(odd_row, 0, tall - margin)
    count = count_ref[0]
    inner_width = (columns - 2) * LANES - size
    inner = sort_slots(cols_ref, count, inner_width, order)
    probe_sum[...] = probe_ref[...]
    grad[...] = grad_ref[...]
    for plane in range(2):
        own = slice(plane * columns + 1, (plane + 1) * columns - 1)
        window[own] = window_ref[own]
        near_tile = plane * columns + jnp.where(odd_col == 1, 0, columns - 1)
        far_tile = plane * columns + jnp.where(odd_col == 1, columns - 1, 0)
        for tile, ref in ((near_tile, near_col_ref), (far_tile, far_col_ref)):
            window[tile, :half] = ref[plane]
            window[tile, half:] = pltpu.roll(ref[plane], margin, axis=1)
    groups = (count + GROUP - 1) // GROUP
    run_slots(
        inner // GROUP, groups, inner, count, order, rows_ref, cols_ref, window, probe, measured, table, grad, probe_sum
    )
    total = lax.axis_size("trow") * lax.axis_size("tcol") * measured.shape[0]
    factor = 1.0 / np.sqrt(np.float32(total))
    mine_out[...] = probe_sum[odd_row] * factor
    other_out[...] = probe_sum[1 - odd_row] * factor
    narrow = lax.broadcasted_iota(jnp.int32, (margin, LANES), 1) < margin
    for plane in range(2):
        base = plane * columns
        left, right = base, base + columns - 1
        for at, out in ((near, near_row_out), (far, far_row_out)):
            rows = pl.ds(at, margin)
            for tile in range(columns - 2):
                out[plane, :, tile * LANES : (tile + 1) * LANES] = grad[base + 1 + tile, rows, :]
            out[plane, :, (columns - 2) * LANES :] = jnp.where(narrow, grad[right, rows, :], grad[left, rows, :])
        for row in range(margin, tall - margin, margin):
            rows = slice(row, row + margin)
            side_out[plane, row - margin : row] = jnp.where(narrow, grad[right, rows, :], grad[left, rows, :])


def outer_call(rows, cols, count, window, near_col, far_col, probe, measured, tables, grad, probe_sum):
    size = probe.shape[1]
    margin = size // 2
    columns = window.shape[0] // 2
    height = window.shape[1] - size
    row = near((2, margin, (columns - 1) * LANES))
    part = near((size, size))
    return pl.pallas_call(
        outer_kernel,
        out_shape=(near(grad.shape), row, row, near((2, height, LANES)), part, part),
        in_specs=[SMEM] * 3 + [VMEM] * 8,
        out_specs=(VMEM,) * 6,
        scratch_shapes=[
            pltpu.VMEM(window.shape, F32),
            pltpu.VMEM(probe.shape, F32),
            pltpu.SMEM((measured.shape[0],), jnp.int32),
        ],
        compiler_params=PARAMS,
        name="slots_across",
    )(rows, cols, count, *in_vmem(window, near_col, far_col, probe, measured, tables, grad, probe_sum))


def side_sum_kernel(side_ref, near_ref, far_ref, near_out, far_out, side):
    margin = near_ref.shape[1]
    height = side_ref.shape[1]
    odd_row, odd_col = parities()
    near_at, far_at = place_of(odd_row, 0, height - margin)
    wide = near_ref.shape[2]
    side[...] = side_ref[...]
    for plane in range(2):
        side[plane, pl.ds(near_at, margin), :] += near_ref[plane, :, wide - LANES :]
        side[plane, pl.ds(far_at, margin), :] += far_ref[plane, :, wide - LANES :]
    for plane in range(2):
        near_out[plane] = folded(side[plane], odd_col == 0)
        far_out[plane] = folded(side[plane], odd_col == 1)


def side_sum_call(side, near_row, far_row):
    shape = near((2, side.shape[1] // 2, LANES))
    return pl.pallas_call(
        side_sum_kernel,
        out_shape=(shape, shape),
        in_specs=[VMEM] * 3,
        out_specs=(VMEM, VMEM),
        scratch_shapes=[pltpu.VMEM(side.shape, F32)],
        compiler_params=PARAMS,
        name="side_sums",
    )(*in_vmem(side, near_row, far_row))


def final_kernel(grad, near_row_ref, far_row_ref, near_col_ref, far_col_ref, out_ref):
    height, width = out_ref.shape[1:]
    columns = grad.shape[0] // 2
    margin = near_row_ref.shape[1]
    half = height // 2
    odd_row, odd_col = parities()
    near_at, far_at = place_of(odd_row, 0, height - margin)
    narrow = lax.broadcasted_iota(jnp.int32, (half, LANES), 1) < LANES // 2
    for plane in range(2):
        for tile in range(columns - 2):
            lanes = slice(tile * LANES, (tile + 1) * LANES)
            out_ref[plane, :, lanes] = grad[plane * columns + 1 + tile, margin : margin + height]
        near = jnp.where(odd_col == 1, near_col_ref[plane], far_col_ref[plane])
        far = jnp.where(odd_col == 1, far_col_ref[plane], near_col_ref[plane])
        for first, left, right in (
            (0, near, far),
            (half, pltpu.roll(near, LANES // 2, axis=1), pltpu.roll(far, LANES // 2, axis=1)),
        ):
            rows = slice(first, first + half)
            out_ref[plane, rows, :LANES] += jnp.where(narrow, left, 0.0)
            out_ref[plane, rows, width - LANES :] += jnp.where(narrow, 0.0, right)
        out_ref[plane, pl.ds(near_at, margin), :] += near_row_ref[plane, :, :width]
        out_ref[plane, pl.ds(far_at, margin), :] += far_row_ref[plane, :, :width]


def final_call(grad, near_row, far_row, near_col, far_col):
    margin = near_row.shape[1]
    shape = (2, grad.shape[1] - 2 * margin, near_row.shape[2] - LANES)
    return pl.pallas_call(
        final_kernel,
        out_shape=jax.ShapeDtypeStruct(shape, F32),
        in_specs=[VMEM] * 5,
        out_specs=VMEM,
        compiler_params=PARAMS,
        name="final_sums",
    )(*in_vmem(grad, near_row, far_row, near_col, far_col))


def near_swap(value, axis):
    return lax.ppermute(value, axis, [(i, i ^ 1) for i in range(lax.axis_size(axis))])


def far_swap(value, axis):
    pairs = [(i, i + 1) for i in range(1, lax.axis_size(axis) - 1, 2)]
    return lax.ppermute(value, axis, pairs + [(j, i) for i, j in pairs])


def doubling_steps(n_row, n_col):
    steps = [(0, 1)] + [(1 << k, 0) for k in range(1, n_row.bit_length() - 1)]
    rest = [(0, 1 << k) for k in range(1, n_col.bit_length() - 1)]
    turned = list(rest)
    for k in range(0, len(rest) - 1, 2):
        turned[k], turned[k + 1] = rest[k + 1], rest[k]
    return list(zip(steps, steps)) + list(zip(rest, turned))


def add_partner(mine, even, odd):
    n_row, n_col = lax.axis_size("trow"), lax.axis_size("tcol")
    pairs = []
    for r in range(n_row):
        for c in range(n_col):
            dr, dc = odd if r % 2 else even
            pairs.append((r * n_col + c, (r ^ dr) * n_col + (c ^ dc)))
    return mine + lax.ppermute(mine, ("trow", "tcol"), pairs)


def body(table, object_planes, probe, intensities, row_offsets, col_offsets, counts):
    size = probe.shape[1]
    rows, cols = row_offsets.reshape(-1), col_offsets.reshape(-1)
    window, near_row, far_row = edge_call(object_planes, size // 2)
    near_row = near_swap(near_row, "trow")
    far_row = far_swap(far_row, "trow")
    probe, measured, tables = ready_call(probe, intensities.reshape(-1, size, size), table)
    window, near_side, far_side = side_call(window, near_row, far_row)
    near_col = near_swap(near_side, "tcol")
    far_col = far_swap(far_side, "tcol")
    grad, probe_sum = inner_call(rows, cols, counts, window, probe, measured, tables)
    grad, near_row, far_row, side, mine, other = outer_call(
        rows, cols, counts, window, near_col, far_col, probe, measured, tables, grad, probe_sum
    )

    steps = doubling_steps(lax.axis_size("trow"), lax.axis_size("tcol"))
    mine = mine + near_swap(other, "trow")
    mine, near_row, far_row = lax.optimization_barrier((mine, near_row, far_row))
    near_row = near_swap(near_row, "trow")
    far_row = far_swap(far_row, "trow")
    mine = add_partner(mine, *steps[0])
    near_side, far_side = side_sum_call(side, near_row, far_row)
    mine, near_side, far_side = lax.optimization_barrier((mine, near_side, far_side))
    near_col = near_swap(near_side, "tcol")
    far_col = far_swap(far_side, "tcol")
    for even, odd in steps[1:]:
        mine = add_partner(mine, even, odd)
    object_grad = final_call(grad, near_row, far_row, near_col, far_col)
    mine, object_grad = lax.optimization_barrier((mine, object_grad))
    other = near_swap(mine, "trow")
    odd_row, _ = parities()
    probe_grad = jnp.where(odd_row == 0, jnp.stack([mine, other]), jnp.stack([other, mine]))
    return (object_grad, probe_grad)


def solution(mesh):
    table = dft_tables(LANES)
    inner = jax.shard_map(
        body,
        mesh=mesh,
        in_specs=(
            P(),
            P(None, "trow", "tcol"),
            P(),
            P("trow", "tcol", None, None, None),
            P("trow", "tcol", None),
            P("trow", "tcol", None),
            P(("trow", "tcol")),
        ),
        out_specs=(P(None, "trow", "tcol"), P()),
        check_vma=False,
    )

    def run(*args):
        return inner(jnp.asarray(table), *args)

    return run
```

```python
import functools

import jax
import jax.numpy as jnp
import numpy as np
from jax import lax
from jax.experimental import pallas as pl
from jax.experimental.pallas import tpu as pltpu
from jax.sharding import PartitionSpec as P

LANES = 128
VMEM_BYTES = 24 * 1024 * 1024
GROUP = 8
F32 = jnp.float32
HBM = pl.BlockSpec(memory_space=pltpu.HBM)
VMEM = pl.BlockSpec(memory_space=pltpu.VMEM)
SMEM = pl.BlockSpec(memory_space=pltpu.SMEM)
PARAMS = pltpu.CompilerParams(vmem_limit_bytes=VMEM_BYTES)


def in_hbm(*arrays):
    return [pltpu.with_memory_space_constraint(array, pltpu.HBM) for array in arrays]


def in_vmem(*arrays):
    return [pltpu.with_memory_space_constraint(array, pltpu.VMEM) for array in arrays]


def in_smem(*arrays):
    return [pltpu.with_memory_space_constraint(array, pltpu.SMEM) for array in arrays]


def near(shape, dtype=F32):
    return pltpu.VMEM(tuple(shape), dtype)


def dft_tables(length):
    index = np.arange(length)
    angle = -2.0 * np.pi * (np.outer(index, index) % length) / length
    cosine, sine = np.cos(angle) / np.sqrt(length), np.sin(angle) / np.sqrt(length)
    right = np.block([[cosine, sine], [-sine, cosine]])
    return np.stack([right, right.T]).astype(np.float32)


def split(value):
    high = value.astype(jnp.bfloat16)
    low = (value - high.astype(F32)).astype(jnp.bfloat16)
    return high, low


def dot(a, b):
    return jnp.dot(a, b, preferred_element_type=F32)


def times_table(value, high, low):
    big, small = split(value)
    return dot(jnp.concatenate([big, small, big], axis=1), jnp.concatenate([high, high, low], axis=0))


def table_times(high, low, value):
    big, small = split(value)
    return dot(jnp.concatenate([high, high, low], axis=1), jnp.concatenate([big, small, big], axis=0))


def folded(tall, low_lanes):
    half = tall.shape[0] // 2
    lane = lax.broadcasted_iota(jnp.int32, (half, LANES), 1)
    here = (lane < LANES // 2) == low_lanes
    return jnp.where(here, tall[:half], pltpu.roll(tall[half:], LANES // 2, axis=1))


def parities():
    return lax.axis_index("trow") % 2, lax.axis_index("tcol") % 2


def place_of(odd, low, high):
    near = pl.multiple_of(jnp.where(odd == 1, low, high), 8)
    far = pl.multiple_of(jnp.where(odd == 1, high, low), 8)
    return near, far


def edge_kernel(centre_ref, window, near_out, far_out, sem):
    height, width = centre_ref.shape[1:]
    margin = near_out.shape[1]
    columns = window.shape[0] // 2
    odd_row, _ = parities()
    near, far = place_of(odd_row, 0, height - margin)
    copies = [
        (centre_ref.at[:, pl.ds(near, margin)], near_out),
        (centre_ref.at[:, pl.ds(far, margin)], far_out),
    ]
    for plane in range(2):
        for tile in range(width // LANES):
            lanes = slice(tile * LANES, (tile + 1) * LANES)
            copies.append((centre_ref.at[plane, :, lanes], window.at[plane * columns + 1 + tile, pl.ds(margin, height)]))
    copies = [pltpu.make_async_copy(a, b, sem.at[i]) for i, (a, b) in enumerate(copies)]
    for copy in copies:
        copy.start()
    for copy in copies:
        copy.wait()


def edge_call(centre, margin):
    height, width = centre.shape[1:]
    tiles = width // LANES
    edge = near((2, margin, width))
    return pl.pallas_call(
        edge_kernel,
        out_shape=(near((2 * (tiles + 2), height + 2 * margin, LANES)), edge, edge),
        in_specs=[HBM],
        out_specs=(VMEM,) * 3,
        scratch_shapes=[pltpu.SemaphoreType.DMA((2 + 2 * tiles,))],
        compiler_params=PARAMS,
        name="edge_rows",
    )(*in_hbm(centre))


def ready_kernel(
    inner_columns, rows_ref, cols_ref, count_ref, probe_ref, measured_ref, table_ref, plan, turned, measured, tables,
    row_list, col_list, probe, table, sem,
):
    slots = measured.shape[0]
    margin = probe.shape[1] // 2
    pairs = ((rows_ref, row_list), (cols_ref, col_list), (probe_ref, probe), (table_ref, table))
    copies = [pltpu.make_async_copy(a, b, sem.at[i]) for i, (a, b) in enumerate(pairs + ((measured_ref, measured),))]
    for copy in copies:
        copy.start()
    for copy in copies[:3]:
        copy.wait()
    count = count_ref[0]
    inner = jnp.int32(0)
    for slot in range(slots):
        first = col_list[slot]
        live = slot < count
        is_inner = jnp.logical_and(jnp.logical_and(first >= 0, first <= inner_columns), live)
        at = jnp.where(is_inner, inner, slots - 1 - (slot - inner))
        plan[jnp.where(live, at, 5 * slots + 1)] = slot
        inner = inner + is_inner.astype(jnp.int32)
        col = first + LANES
        turn = col & (LANES - 1)
        place = slots + 2 + 3 * slot
        plan[place] = row_list[slot] + margin
        plan[place + 1] = lax.shift_right_logical(col, 7)
        plan[place + 2] = turn
        for plane in range(2):
            turned[slot, plane] = pltpu.roll(probe[plane], turn, axis=1)
    plan[slots] = inner
    plan[slots + 1] = count
    copies[3].wait()
    for index in range(2):
        tables[2 * index], tables[2 * index + 1] = split(table[index])
    copies[4].wait()


def ready_call(rows, cols, count, probe, measured, table, width):
    slots = measured.shape[0]
    return pl.pallas_call(
        functools.partial(ready_kernel, width - probe.shape[1]),
        out_shape=(
            pltpu.SMEM((5 * slots + 2,), jnp.int32),
            near((slots,) + probe.shape),
            near(measured.shape, measured.dtype),
            near((4,) + table.shape[1:], jnp.bfloat16),
        ),
        in_specs=[HBM] * 2 + [SMEM] + [HBM] * 3,
        out_specs=(SMEM,) + (VMEM,) * 3,
        scratch_shapes=[
            pltpu.SMEM(rows.shape, jnp.int32),
            pltpu.SMEM(cols.shape, jnp.int32),
            pltpu.VMEM(probe.shape, F32),
            pltpu.VMEM(table.shape, F32),
            pltpu.SemaphoreType.DMA((5,)),
        ],
        compiler_params=PARAMS,
        name="ready",
    )(*in_hbm(rows, cols), count, *in_hbm(probe, measured, table))


def side_kernel(tile_ref, near_ref, far_ref, window, near_out, far_out):
    margin = near_ref.shape[1]
    columns = window.shape[0] // 2
    odd_row, odd_col = parities()
    bottom = window.shape[1] - margin
    near, far = place_of(odd_row, 0, bottom)
    for plane in range(2):
        for tile in range(columns - 2):
            lanes = slice(tile * LANES, (tile + 1) * LANES)
            window[plane * columns + 1 + tile, margin:bottom] = tile_ref[plane * columns + 1 + tile, margin:bottom]
            window[plane * columns + 1 + tile, pl.ds(near, margin), :] = near_ref[plane, :, lanes]
            window[plane * columns + 1 + tile, pl.ds(far, margin), :] = far_ref[plane, :, lanes]
    for plane in range(2):
        near_tile = plane * columns + jnp.where(odd_col == 1, 1, columns - 2)
        far_tile = plane * columns + jnp.where(odd_col == 1, columns - 2, 1)
        near_out[plane] = folded(window[near_tile], odd_col == 1)
        far_out[plane] = folded(window[far_tile], odd_col == 0)


def side_call(window, near_row, far_row):
    shape = near((2, window.shape[1] // 2, LANES))
    return pl.pallas_call(
        side_kernel,
        out_shape=(near(window.shape), shape, shape),
        in_specs=[VMEM] * 3,
        out_specs=(VMEM,) * 3,
        compiler_params=PARAMS,
        name="side_columns",
    )(*in_vmem(window, near_row, far_row))


def run_slots(groups, start, inner, live, plan, window, turned, measured, table, grad, probe_sum):
    slots = measured.shape[0]
    size = turned.shape[2]
    columns = window.shape[0] // 2
    lane = lax.broadcasted_iota(jnp.int32, (size, LANES), 1)

    def find(index):
        at = jnp.where(index < inner, start + index, jnp.maximum(slots - 1 - (index - inner), 0))
        is_live = index < live
        slot = plan[jnp.where(is_live, at, jnp.where(inner > 0, start, slots - 1))]
        place = slots + 2 + 3 * slot
        scale = jnp.where(is_live, 2.0, 0.0).astype(F32)
        return slot, plan[place], plan[place + 1], plan[place + 2], scale

    def load(pair):
        kept, waves = [], []
        for slot, row, tile, turn, _ in pair:
            here = lane >= turn
            patch = [
                jnp.where(
                    here,
                    window[plane * columns + tile, pl.ds(row, size), :],
                    window[plane * columns + tile + 1, pl.ds(row, size), :],
                )
                for plane in range(2)
            ]
            probe = [turned[slot, plane] for plane in range(2)]
            wave_real = probe[0] * patch[0] - probe[1] * patch[1]
            wave_imag = probe[0] * patch[1] + probe[1] * patch[0]
            kept.append(patch)
            waves.append(jnp.concatenate([wave_real, wave_imag], axis=1))
        return kept, jnp.concatenate(waves, axis=0)

    def regroup(pair):
        return jnp.concatenate(
            [
                jnp.concatenate([pair[:size, :size], pair[size:, :size]], axis=1),
                jnp.concatenate([pair[:size, size:], pair[size:, size:]], axis=1),
            ],
            axis=0,
        )

    def weigh(pair, psi):
        real, imag = psi[:size], psi[size:]
        weights = []
        for member, (slot, _, _, _, scale) in enumerate(pair):
            lanes = slice(member * size, (member + 1) * size)
            power = real[:, lanes] * real[:, lanes] + imag[:, lanes] * imag[:, lanes]
            weights.append((power - measured[slot].astype(F32)) * scale)
        weight = jnp.concatenate(weights, axis=1)
        return jnp.concatenate([weight * real, weight * imag], axis=0)

    def add_up(pair, kept, exits):
        for member, (slot, row, tile, turn, _) in enumerate(pair):
            patch = kept[member]
            probe = [turned[slot, plane] for plane in range(2)]
            here = lane >= turn
            exit_real = exits[member * size : (member + 1) * size, :size]
            exit_imag = exits[member * size : (member + 1) * size, size:]
            terms = (patch[0] * exit_real + patch[1] * exit_imag, patch[0] * exit_imag - patch[1] * exit_real)
            adds = (probe[0] * exit_real + probe[1] * exit_imag, probe[0] * exit_imag - probe[1] * exit_real)
            back = (LANES - turn) & (LANES - 1)
            for plane in range(2):
                probe_sum[plane] += pltpu.roll(terms[plane], back, axis=1)
                at = plane * columns + tile
                grad[at, pl.ds(row, size), :] += jnp.where(here, adds[plane], 0.0)
                grad[at + 1, pl.ds(row, size), :] += jnp.where(here, 0.0, adds[plane])

    def step(group, carry):
        slots = [find(group * GROUP + member) for member in range(GROUP)]
        pairs = [slots[member : member + 2] for member in range(0, GROUP, 2)]
        loaded = [load(pair) for pair in pairs]
        waves = [regroup(times_table(wave, table[0], table[1])) for _, wave in loaded]
        waves = [weigh(pair, table_times(table[2], table[3], wave)) for pair, wave in zip(pairs, waves)]
        waves = [regroup(table_times(table[0], table[1], wave)) for wave in waves]
        waves = [times_table(wave, table[2], table[3]) for wave in waves]
        for pair, (kept, _), wave in zip(pairs, loaded, waves):
            add_up(pair, kept, wave)
        return carry

    lax.fori_loop(0, groups, step, 0)


def inner_kernel(plan, window, turned, measured, table, grad, probe_sum):
    grad[...] = jnp.zeros_like(grad)
    probe_sum[...] = jnp.zeros_like(probe_sum)
    groups = plan[measured.shape[0]] // GROUP
    here = groups * GROUP
    run_slots(groups, 0, here, here, plan, window, turned, measured, table, grad, probe_sum)


def inner_call(plan, window, turned, measured, tables):
    return pl.pallas_call(
        inner_kernel,
        out_shape=(near(window.shape), near(turned.shape[1:])),
        in_specs=[SMEM] + [VMEM] * 4,
        out_specs=(VMEM,) * 2,
        compiler_params=PARAMS,
        cost_estimate=pl.CostEstimate(flops=10**10, bytes_accessed=2 * 10**7, transcendentals=0),
        name="slots_inside",
    )(*in_smem(plan), *in_vmem(window, turned, measured, tables))


def outer_kernel(
    plan, window_ref, near_col_ref, far_col_ref, turned, measured, table, grad_ref, probe_ref,
    grad, near_row_out, far_row_out, side_out, mine_out, other_out, window, probe_sum,
):
    slots = measured.shape[0]
    margin = turned.shape[2] // 2
    columns = window.shape[0] // 2
    tall = window.shape[1]
    half = tall // 2
    odd_row, odd_col = parities()
    near, far = place_of(odd_row, 0, tall - margin)
    probe_sum[...] = probe_ref[...]
    grad[...] = grad_ref[...]
    for plane in range(2):
        own = slice(plane * columns + 1, (plane + 1) * columns - 1)
        window[own] = window_ref[own]
        near_tile = plane * columns + jnp.where(odd_col == 1, 0, columns - 1)
        far_tile = plane * columns + jnp.where(odd_col == 1, columns - 1, 0)
        for tile, ref in ((near_tile, near_col_ref), (far_tile, far_col_ref)):
            window[tile, :half] = ref[plane]
            window[tile, half:] = pltpu.roll(ref[plane], margin, axis=1)
    start = plan[slots] // GROUP * GROUP
    inner = plan[slots] - start
    live = plan[slots + 1] - start
    run_slots(
        (live + GROUP - 1) // GROUP, start, inner, live, plan, window, turned, measured, table, grad, probe_sum
    )
    factor = 1.0 / np.sqrt(np.float32(lax.axis_size("trow") * lax.axis_size("tcol") * slots))
    mine_out[...] = probe_sum[odd_row] * factor
    other_out[...] = probe_sum[1 - odd_row] * factor
    narrow = lax.broadcasted_iota(jnp.int32, (margin, LANES), 1) < margin
    for plane in range(2):
        base = plane * columns
        left, right = base, base + columns - 1
        for at, out in ((near, near_row_out), (far, far_row_out)):
            rows = pl.ds(at, margin)
            for tile in range(columns - 2):
                out[plane, :, tile * LANES : (tile + 1) * LANES] = grad[base + 1 + tile, rows, :]
            out[plane, :, (columns - 2) * LANES :] = jnp.where(narrow, grad[right, rows, :], grad[left, rows, :])
        for row in range(margin, tall - margin, margin):
            rows = slice(row, row + margin)
            side_out[plane, row - margin : row] = jnp.where(narrow, grad[right, rows, :], grad[left, rows, :])


def outer_call(plan, window, near_col, far_col, turned, measured, tables, grad, probe_sum):
    size = turned.shape[2]
    margin = size // 2
    columns = window.shape[0] // 2
    row = near((2, margin, (columns - 1) * LANES))
    part = near((size, size))
    return pl.pallas_call(
        outer_kernel,
        out_shape=(near(grad.shape), row, row, near((2, window.shape[1] - size, LANES)), part, part),
        in_specs=[SMEM] + [VMEM] * 8,
        out_specs=(VMEM,) * 6,
        scratch_shapes=[pltpu.VMEM(window.shape, F32), pltpu.VMEM(probe_sum.shape, F32)],
        compiler_params=PARAMS,
        cost_estimate=pl.CostEstimate(flops=10**10, bytes_accessed=2 * 10**7, transcendentals=0),
        name="slots_across",
    )(*in_smem(plan), *in_vmem(window, near_col, far_col, turned, measured, tables, grad, probe_sum))


def side_sum_kernel(side_ref, near_ref, far_ref, near_out, far_out, side):
    margin = near_ref.shape[1]
    height = side_ref.shape[1]
    odd_row, odd_col = parities()
    near_at, far_at = place_of(odd_row, 0, height - margin)
    wide = near_ref.shape[2]
    side[...] = side_ref[...]
    for plane in range(2):
        side[plane, pl.ds(near_at, margin), :] += near_ref[plane, :, wide - LANES :]
        side[plane, pl.ds(far_at, margin), :] += far_ref[plane, :, wide - LANES :]
    for plane in range(2):
        near_out[plane] = folded(side[plane], odd_col == 0)
        far_out[plane] = folded(side[plane], odd_col == 1)


def side_sum_call(side, near_row, far_row):
    shape = near((2, side.shape[1] // 2, LANES))
    return pl.pallas_call(
        side_sum_kernel,
        out_shape=(shape, shape),
        in_specs=[VMEM] * 3,
        out_specs=(VMEM, VMEM),
        scratch_shapes=[pltpu.VMEM(side.shape, F32)],
        compiler_params=PARAMS,
        name="side_sums",
    )(*in_vmem(side, near_row, far_row))


def final_kernel(grad, near_row_ref, far_row_ref, near_col_ref, far_col_ref, out_ref):
    height, width = out_ref.shape[1:]
    columns = grad.shape[0] // 2
    margin = near_row_ref.shape[1]
    half = height // 2
    odd_row, odd_col = parities()
    near_at, far_at = place_of(odd_row, 0, height - margin)
    narrow = lax.broadcasted_iota(jnp.int32, (half, LANES), 1) < LANES // 2
    for plane in range(2):
        for tile in range(columns - 2):
            lanes = slice(tile * LANES, (tile + 1) * LANES)
            out_ref[plane, :, lanes] = grad[plane * columns + 1 + tile, margin : margin + height]
        near = jnp.where(odd_col == 1, near_col_ref[plane], far_col_ref[plane])
        far = jnp.where(odd_col == 1, far_col_ref[plane], near_col_ref[plane])
        for first, left, right in (
            (0, near, far),
            (half, pltpu.roll(near, LANES // 2, axis=1), pltpu.roll(far, LANES // 2, axis=1)),
        ):
            rows = slice(first, first + half)
            out_ref[plane, rows, :LANES] += jnp.where(narrow, left, 0.0)
            out_ref[plane, rows, width - LANES :] += jnp.where(narrow, 0.0, right)
        out_ref[plane, pl.ds(near_at, margin), :] += near_row_ref[plane, :, :width]
        out_ref[plane, pl.ds(far_at, margin), :] += far_row_ref[plane, :, :width]


def final_call(grad, near_row, far_row, near_col, far_col):
    margin = near_row.shape[1]
    shape = (2, grad.shape[1] - 2 * margin, near_row.shape[2] - LANES)
    return pl.pallas_call(
        final_kernel,
        out_shape=jax.ShapeDtypeStruct(shape, F32),
        in_specs=[VMEM] * 5,
        out_specs=VMEM,
        compiler_params=PARAMS,
        name="final_sums",
    )(*in_vmem(grad, near_row, far_row, near_col, far_col))


def near_swap(value, axis):
    return lax.ppermute(value, axis, [(i, i ^ 1) for i in range(lax.axis_size(axis))])


def far_swap(value, axis):
    pairs = [(i, i + 1) for i in range(1, lax.axis_size(axis) - 1, 2)]
    return lax.ppermute(value, axis, pairs + [(j, i) for i, j in pairs])


def doubling_steps(n_row, n_col):
    steps = [(0, 1)] + [(1 << k, 0) for k in range(1, n_row.bit_length() - 1)]
    rest = [(0, 1 << k) for k in range(1, n_col.bit_length() - 1)]
    turned = list(rest)
    for k in range(0, len(rest) - 1, 2):
        turned[k], turned[k + 1] = rest[k + 1], rest[k]
    return list(zip(steps, steps)) + list(zip(rest, turned))


def add_partner(mine, even, odd):
    n_row, n_col = lax.axis_size("trow"), lax.axis_size("tcol")
    pairs = []
    for r in range(n_row):
        for c in range(n_col):
            dr, dc = odd if r % 2 else even
            pairs.append((r * n_col + c, (r ^ dr) * n_col + (c ^ dc)))
    return mine + lax.ppermute(mine, ("trow", "tcol"), pairs)


def body(table, object_planes, probe, intensities, row_offsets, col_offsets, counts):
    size = probe.shape[1]
    rows, cols = row_offsets.reshape(-1), col_offsets.reshape(-1)
    measured = intensities.reshape(-1, size, size)
    window, near_row, far_row = edge_call(object_planes, size // 2)
    near_row = near_swap(near_row, "trow")
    far_row = far_swap(far_row, "trow")
    plan, turned, measured, tables = ready_call(rows, cols, counts, probe, measured, table, object_planes.shape[2])
    window, near_side, far_side = side_call(window, near_row, far_row)
    near_col = near_swap(near_side, "tcol")
    far_col = far_swap(far_side, "tcol")
    grad, probe_sum = inner_call(plan, window, turned, measured, tables)
    grad, near_row, far_row, side, mine, other = outer_call(
        plan, window, near_col, far_col, turned, measured, tables, grad, probe_sum
    )

    steps = doubling_steps(lax.axis_size("trow"), lax.axis_size("tcol"))
    mine = mine + near_swap(other, "trow")
    mine, near_row, far_row = lax.optimization_barrier((mine, near_row, far_row))
    near_row = near_swap(near_row, "trow")
    far_row = far_swap(far_row, "trow")
    mine = add_partner(mine, *steps[0])
    near_side, far_side = side_sum_call(side, near_row, far_row)
    mine, near_side, far_side = lax.optimization_barrier((mine, near_side, far_side))
    near_col = near_swap(near_side, "tcol")
    far_col = far_swap(far_side, "tcol")
    for even, odd in steps[1:]:
        mine = add_partner(mine, even, odd)
    object_grad = final_call(grad, near_row, far_row, near_col, far_col)
    mine, object_grad = lax.optimization_barrier((mine, object_grad))
    other = near_swap(mine, "trow")
    odd_row, _ = parities()
    probe_grad = jnp.where(odd_row == 0, jnp.stack([mine, other]), jnp.stack([other, mine]))
    return (object_grad, probe_grad)


def solution(mesh):
    table = dft_tables(LANES)
    inner = jax.shard_map(
        body,
        mesh=mesh,
        in_specs=(
            P(),
            P(None, "trow", "tcol"),
            P(),
            P("trow", "tcol", None, None, None),
            P("trow", "tcol", None),
            P("trow", "tcol", None),
            P(("trow", "tcol")),
        ),
        out_specs=(P(None, "trow", "tcol"), P()),
        check_vma=False,
    )

    def run(*args):
        return inner(jnp.asarray(table), *args)

    return run
```

```python
import jax
import jax.numpy as jnp
import numpy as np
from jax import lax
from jax.experimental import pallas as pl
from jax.experimental.pallas import tpu as pltpu
from jax.sharding import PartitionSpec as P

LANES = 128
VMEM_BYTES = 24 * 1024 * 1024
GROUP = 8
F32 = jnp.float32
HBM = pl.BlockSpec(memory_space=pltpu.HBM)
VMEM = pl.BlockSpec(memory_space=pltpu.VMEM)
SMEM = pl.BlockSpec(memory_space=pltpu.SMEM)
PARAMS = pltpu.CompilerParams(vmem_limit_bytes=VMEM_BYTES)


def in_hbm(*arrays):
    return [pltpu.with_memory_space_constraint(array, pltpu.HBM) for array in arrays]


def in_vmem(*arrays):
    return [pltpu.with_memory_space_constraint(array, pltpu.VMEM) for array in arrays]


def in_smem(*arrays):
    return [pltpu.with_memory_space_constraint(array, pltpu.SMEM) for array in arrays]


def near(shape, dtype=F32):
    return pltpu.VMEM(tuple(shape), dtype)


def dft_tables(length):
    index = np.arange(length)
    angle = -2.0 * np.pi * (np.outer(index, index) % length) / length
    cosine, sine = np.cos(angle) / np.sqrt(length), np.sin(angle) / np.sqrt(length)
    right = np.block([[cosine, sine], [-sine, cosine]])
    return np.stack([right, right.T]).astype(np.float32)


def split(value):
    high = value.astype(jnp.bfloat16)
    low = (value - high.astype(F32)).astype(jnp.bfloat16)
    return high, low


def dot(a, b):
    return jnp.dot(a, b, preferred_element_type=F32)


def times_table(value, high, low):
    big, small = split(value)
    return dot(jnp.concatenate([big, small, big], axis=1), jnp.concatenate([high, high, low], axis=0))


def table_times(high, low, value):
    big, small = split(value)
    return dot(jnp.concatenate([high, high, low], axis=1), jnp.concatenate([big, small, big], axis=0))


def folded(tall, low_lanes):
    half = tall.shape[0] // 2
    lane = lax.broadcasted_iota(jnp.int32, (half, LANES), 1)
    here = (lane < LANES // 2) == low_lanes
    return jnp.where(here, tall[:half], pltpu.roll(tall[half:], LANES // 2, axis=1))


def parities():
    return lax.axis_index("trow") % 2, lax.axis_index("tcol") % 2


def place_of(odd, low, high):
    near = pl.multiple_of(jnp.where(odd == 1, low, high), 8)
    far = pl.multiple_of(jnp.where(odd == 1, high, low), 8)
    return near, far


def edge_kernel(centre_ref, near_out, far_out, sem):
    margin = near_out.shape[1]
    odd_row, _ = parities()
    near, far = place_of(odd_row, 0, centre_ref.shape[1] - margin)
    copies = [
        pltpu.make_async_copy(centre_ref.at[:, pl.ds(far, margin)], far_out, sem.at[0]),
        pltpu.make_async_copy(centre_ref.at[:, pl.ds(near, margin)], near_out, sem.at[1]),
    ]
    for copy in copies:
        copy.start()
    for copy in copies:
        copy.wait()


def edge_call(centre, margin):
    edge = near((2, margin, centre.shape[2]))
    return pl.pallas_call(
        edge_kernel,
        out_shape=(edge, edge),
        in_specs=[HBM],
        out_specs=(VMEM,) * 2,
        scratch_shapes=[pltpu.SemaphoreType.DMA((2,))],
        compiler_params=PARAMS,
        name="edge_rows",
    )(*in_hbm(centre))


def ready_kernel(
    rows_ref, cols_ref, count_ref, probe_ref, measured_ref, table_ref, centre_ref, plan, turned, measured, tables, window,
    row_list, col_list, probe, table, sem,
):
    slots = measured.shape[0]
    margin = probe.shape[1] // 2
    height, width = centre_ref.shape[1:]
    columns = window.shape[0] // 2
    inner_columns = width - probe.shape[2]
    copies = [(rows_ref, row_list), (cols_ref, col_list), (probe_ref, probe), (table_ref, table)]
    for plane in range(2):
        for tile in range(columns - 2):
            lanes = slice(tile * LANES, (tile + 1) * LANES)
            copies.append((centre_ref.at[plane, :, lanes], window.at[plane * columns + 1 + tile, pl.ds(margin, height)]))
    copies.append((measured_ref, measured))
    copies = [pltpu.make_async_copy(a, b, sem.at[i]) for i, (a, b) in enumerate(copies)]
    for copy in copies:
        copy.start()
    for copy in copies[:3]:
        copy.wait()
    count = count_ref[0, 0]
    inner = jnp.int32(0)
    for slot in range(slots):
        first = col_list[slot]
        live = slot < count
        is_inner = jnp.logical_and(jnp.logical_and(first >= 0, first <= inner_columns), live)
        at = jnp.where(is_inner, inner, slots - 1 - (slot - inner))
        plan[jnp.where(live, at, 5 * slots + 1)] = slot
        inner = inner + is_inner.astype(jnp.int32)
        col = first + LANES
        turn = col & (LANES - 1)
        place = slots + 2 + 3 * slot
        plan[place] = row_list[slot] + margin
        plan[place + 1] = lax.shift_right_logical(col, 7)
        plan[place + 2] = turn
        for plane in range(2):
            turned[slot, plane] = pltpu.roll(probe[plane], turn, axis=1)
    plan[slots] = inner
    plan[slots + 1] = count
    copies[3].wait()
    for index in range(2):
        tables[2 * index], tables[2 * index + 1] = split(table[index])
    for copy in copies[4:]:
        copy.wait()


def ready_call(rows, cols, count, probe, measured, table, centre):
    slots = measured.shape[0]
    height, width = centre.shape[1:]
    tiles = width // LANES
    return pl.pallas_call(
        ready_kernel,
        out_shape=(
            pltpu.SMEM((5 * slots + 2,), jnp.int32),
            near((slots,) + probe.shape),
            near(measured.shape, measured.dtype),
            near((4,) + table.shape[1:], jnp.bfloat16),
            near((2 * (tiles + 2), height + probe.shape[1], LANES)),
        ),
        in_specs=[HBM] * 2 + [VMEM] + [HBM] * 4,
        out_specs=(SMEM,) + (VMEM,) * 4,
        scratch_shapes=[
            pltpu.SMEM(rows.shape, jnp.int32),
            pltpu.SMEM(cols.shape, jnp.int32),
            pltpu.VMEM(probe.shape, F32),
            pltpu.VMEM(table.shape, F32),
            pltpu.SemaphoreType.DMA((5 + 2 * tiles,)),
        ],
        compiler_params=PARAMS,
        name="ready",
    )(*in_hbm(rows, cols), *in_vmem(jnp.broadcast_to(count, (8, LANES))), *in_hbm(probe, measured, table, centre))


def side_kernel(tile_ref, near_ref, far_ref, window, near_out, far_out):
    margin = near_ref.shape[1]
    columns = window.shape[0] // 2
    odd_row, odd_col = parities()
    bottom = window.shape[1] - margin
    near, far = place_of(odd_row, 0, bottom)
    for plane in range(2):
        for tile in range(columns - 2):
            lanes = slice(tile * LANES, (tile + 1) * LANES)
            window[plane * columns + 1 + tile, margin:bottom] = tile_ref[plane * columns + 1 + tile, margin:bottom]
            window[plane * columns + 1 + tile, pl.ds(near, margin), :] = near_ref[plane, :, lanes]
            window[plane * columns + 1 + tile, pl.ds(far, margin), :] = far_ref[plane, :, lanes]
    for plane in range(2):
        near_tile = plane * columns + jnp.where(odd_col == 1, 1, columns - 2)
        far_tile = plane * columns + jnp.where(odd_col == 1, columns - 2, 1)
        near_out[plane] = folded(window[near_tile], odd_col == 1)
        far_out[plane] = folded(window[far_tile], odd_col == 0)


def side_call(window, near_row, far_row):
    shape = near((2, window.shape[1] // 2, LANES))
    return pl.pallas_call(
        side_kernel,
        out_shape=(near(window.shape), shape, shape),
        in_specs=[VMEM] * 3,
        out_specs=(VMEM,) * 3,
        compiler_params=PARAMS,
        name="side_columns",
    )(*in_vmem(window, near_row, far_row))


def run_slots(groups, start, inner, live, plan, window, turned, measured, table, grad, probe_sum):
    slots = measured.shape[0]
    size = turned.shape[2]
    columns = window.shape[0] // 2
    lane = lax.broadcasted_iota(jnp.int32, (size, LANES), 1)

    def find(index):
        at = jnp.where(index < inner, start + index, jnp.maximum(slots - 1 - (index - inner), 0))
        is_live = index < live
        slot = plan[jnp.where(is_live, at, jnp.where(inner > 0, start, slots - 1))]
        place = slots + 2 + 3 * slot
        scale = jnp.where(is_live, 2.0, 0.0).astype(F32)
        return slot, plan[place], plan[place + 1], plan[place + 2], scale

    def load(pair):
        kept, waves = [], []
        for slot, row, tile, turn, _ in pair:
            here = lane >= turn
            patch = [
                jnp.where(
                    here,
                    window[plane * columns + tile, pl.ds(row, size), :],
                    window[plane * columns + tile + 1, pl.ds(row, size), :],
                )
                for plane in range(2)
            ]
            probe = [turned[slot, plane] for plane in range(2)]
            wave_real = probe[0] * patch[0] - probe[1] * patch[1]
            wave_imag = probe[0] * patch[1] + probe[1] * patch[0]
            kept.append(patch)
            waves.append(jnp.concatenate([wave_real, wave_imag], axis=1))
        return kept, jnp.concatenate(waves, axis=0)

    def regroup(pair):
        return jnp.concatenate(
            [
                jnp.concatenate([pair[:size, :size], pair[size:, :size]], axis=1),
                jnp.concatenate([pair[:size, size:], pair[size:, size:]], axis=1),
            ],
            axis=0,
        )

    def weigh(pair, psi):
        real, imag = psi[:size], psi[size:]
        weights = []
        for member, (slot, _, _, _, scale) in enumerate(pair):
            lanes = slice(member * size, (member + 1) * size)
            power = real[:, lanes] * real[:, lanes] + imag[:, lanes] * imag[:, lanes]
            weights.append((power - measured[slot].astype(F32)) * scale)
        weight = jnp.concatenate(weights, axis=1)
        return jnp.concatenate([weight * real, weight * imag], axis=0)

    def add_up(pair, kept, exits):
        for member, (slot, row, tile, turn, _) in enumerate(pair):
            patch = kept[member]
            probe = [turned[slot, plane] for plane in range(2)]
            here = lane >= turn
            exit_real = exits[member * size : (member + 1) * size, :size]
            exit_imag = exits[member * size : (member + 1) * size, size:]
            terms = (patch[0] * exit_real + patch[1] * exit_imag, patch[0] * exit_imag - patch[1] * exit_real)
            adds = (probe[0] * exit_real + probe[1] * exit_imag, probe[0] * exit_imag - probe[1] * exit_real)
            back = (LANES - turn) & (LANES - 1)
            for plane in range(2):
                probe_sum[plane] += pltpu.roll(terms[plane], back, axis=1)
                at = plane * columns + tile
                grad[at, pl.ds(row, size), :] += jnp.where(here, adds[plane], 0.0)
                grad[at + 1, pl.ds(row, size), :] += jnp.where(here, 0.0, adds[plane])

    def step(group, carry):
        slots = [find(group * GROUP + member) for member in range(GROUP)]
        pairs = [slots[member : member + 2] for member in range(0, GROUP, 2)]
        loaded = [load(pair) for pair in pairs]
        waves = [regroup(times_table(wave, table[0], table[1])) for _, wave in loaded]
        waves = [weigh(pair, table_times(table[2], table[3], wave)) for pair, wave in zip(pairs, waves)]
        waves = [regroup(table_times(table[0], table[1], wave)) for wave in waves]
        waves = [times_table(wave, table[2], table[3]) for wave in waves]
        for pair, (kept, _), wave in zip(pairs, loaded, waves):
            add_up(pair, kept, wave)
        return carry

    lax.fori_loop(0, groups, step, 0)


def inner_kernel(plan, window, turned, measured, table, grad, probe_sum):
    grad[...] = jnp.zeros_like(grad)
    probe_sum[...] = jnp.zeros_like(probe_sum)
    groups = plan[measured.shape[0]] // GROUP
    here = groups * GROUP
    run_slots(groups, 0, here, here, plan, window, turned, measured, table, grad, probe_sum)


def inner_call(plan, window, turned, measured, tables):
    return pl.pallas_call(
        inner_kernel,
        out_shape=(near(window.shape), near(turned.shape[1:])),
        in_specs=[SMEM] + [VMEM] * 4,
        out_specs=(VMEM,) * 2,
        compiler_params=PARAMS,
        cost_estimate=pl.CostEstimate(flops=10**10, bytes_accessed=2 * 10**7, transcendentals=0),
        name="slots_inside",
    )(*in_smem(plan), *in_vmem(window, turned, measured, tables))


def outer_kernel(
    plan, window_ref, near_col_ref, far_col_ref, turned, measured, table, grad_ref, probe_ref,
    grad, near_row_out, far_row_out, side_out, mine_out, other_out, window, probe_sum,
):
    slots = measured.shape[0]
    margin = turned.shape[2] // 2
    columns = window.shape[0] // 2
    tall = window.shape[1]
    half = tall // 2
    odd_row, odd_col = parities()
    near, far = place_of(odd_row, 0, tall - margin)
    probe_sum[...] = probe_ref[...]
    grad[...] = grad_ref[...]
    for plane in range(2):
        own = slice(plane * columns + 1, (plane + 1) * columns - 1)
        window[own] = window_ref[own]
        near_tile = plane * columns + jnp.where(odd_col == 1, 0, columns - 1)
        far_tile = plane * columns + jnp.where(odd_col == 1, columns - 1, 0)
        for tile, ref in ((near_tile, near_col_ref), (far_tile, far_col_ref)):
            window[tile, :half] = ref[plane]
            window[tile, half:] = pltpu.roll(ref[plane], margin, axis=1)
    start = plan[slots] // GROUP * GROUP
    inner = plan[slots] - start
    live = plan[slots + 1] - start
    run_slots(
        (live + GROUP - 1) // GROUP, start, inner, live, plan, window, turned, measured, table, grad, probe_sum
    )
    factor = 1.0 / np.sqrt(np.float32(lax.axis_size("trow") * lax.axis_size("tcol") * slots))
    mine_out[...] = probe_sum[odd_row] * factor
    other_out[...] = probe_sum[1 - odd_row] * factor
    narrow = lax.broadcasted_iota(jnp.int32, (margin, LANES), 1) < margin
    for plane in range(2):
        base = plane * columns
        left, right = base, base + columns - 1
        for at, out in ((near, near_row_out), (far, far_row_out)):
            rows = pl.ds(at, margin)
            for tile in range(columns - 2):
                out[plane, :, tile * LANES : (tile + 1) * LANES] = grad[base + 1 + tile, rows, :]
            out[plane, :, (columns - 2) * LANES :] = jnp.where(narrow, grad[right, rows, :], grad[left, rows, :])
        for row in range(margin, tall - margin, margin):
            rows = slice(row, row + margin)
            side_out[plane, row - margin : row] = jnp.where(narrow, grad[right, rows, :], grad[left, rows, :])


def outer_call(plan, window, near_col, far_col, turned, measured, tables, grad, probe_sum):
    size = turned.shape[2]
    margin = size // 2
    columns = window.shape[0] // 2
    row = near((2, margin, (columns - 1) * LANES))
    part = near((size, size))
    return pl.pallas_call(
        outer_kernel,
        out_shape=(near(grad.shape), row, row, near((2, window.shape[1] - size, LANES)), part, part),
        in_specs=[SMEM] + [VMEM] * 8,
        out_specs=(VMEM,) * 6,
        scratch_shapes=[pltpu.VMEM(window.shape, F32), pltpu.VMEM(probe_sum.shape, F32)],
        compiler_params=PARAMS,
        cost_estimate=pl.CostEstimate(flops=10**10, bytes_accessed=2 * 10**7, transcendentals=0),
        name="slots_across",
    )(*in_smem(plan), *in_vmem(window, near_col, far_col, turned, measured, tables, grad, probe_sum))


def side_sum_kernel(side_ref, near_ref, far_ref, near_out, far_out, side):
    margin = near_ref.shape[1]
    height = side_ref.shape[1]
    odd_row, odd_col = parities()
    near_at, far_at = place_of(odd_row, 0, height - margin)
    wide = near_ref.shape[2]
    side[...] = side_ref[...]
    for plane in range(2):
        side[plane, pl.ds(near_at, margin), :] += near_ref[plane, :, wide - LANES :]
        side[plane, pl.ds(far_at, margin), :] += far_ref[plane, :, wide - LANES :]
    for plane in range(2):
        near_out[plane] = folded(side[plane], odd_col == 0)
        far_out[plane] = folded(side[plane], odd_col == 1)


def side_sum_call(side, near_row, far_row):
    shape = near((2, side.shape[1] // 2, LANES))
    return pl.pallas_call(
        side_sum_kernel,
        out_shape=(shape, shape),
        in_specs=[VMEM] * 3,
        out_specs=(VMEM, VMEM),
        scratch_shapes=[pltpu.VMEM(side.shape, F32)],
        compiler_params=PARAMS,
        name="side_sums",
    )(*in_vmem(side, near_row, far_row))


def final_kernel(grad, near_row_ref, far_row_ref, near_col_ref, far_col_ref, out_ref):
    height, width = out_ref.shape[1:]
    columns = grad.shape[0] // 2
    margin = near_row_ref.shape[1]
    half = height // 2
    odd_row, odd_col = parities()
    near_at, far_at = place_of(odd_row, 0, height - margin)
    narrow = lax.broadcasted_iota(jnp.int32, (half, LANES), 1) < LANES // 2
    for plane in range(2):
        for tile in range(columns - 2):
            lanes = slice(tile * LANES, (tile + 1) * LANES)
            out_ref[plane, :, lanes] = grad[plane * columns + 1 + tile, margin : margin + height]
        near = jnp.where(odd_col == 1, near_col_ref[plane], far_col_ref[plane])
        far = jnp.where(odd_col == 1, far_col_ref[plane], near_col_ref[plane])
        for first, left, right in (
            (0, near, far),
            (half, pltpu.roll(near, LANES // 2, axis=1), pltpu.roll(far, LANES // 2, axis=1)),
        ):
            rows = slice(first, first + half)
            out_ref[plane, rows, :LANES] += jnp.where(narrow, left, 0.0)
            out_ref[plane, rows, width - LANES :] += jnp.where(narrow, 0.0, right)
        out_ref[plane, pl.ds(near_at, margin), :] += near_row_ref[plane, :, :width]
        out_ref[plane, pl.ds(far_at, margin), :] += far_row_ref[plane, :, :width]


def final_call(grad, near_row, far_row, near_col, far_col):
    margin = near_row.shape[1]
    shape = (2, grad.shape[1] - 2 * margin, near_row.shape[2] - LANES)
    return pl.pallas_call(
        final_kernel,
        out_shape=jax.ShapeDtypeStruct(shape, F32),
        in_specs=[VMEM] * 5,
        out_specs=VMEM,
        compiler_params=PARAMS,
        name="final_sums",
    )(*in_vmem(grad, near_row, far_row, near_col, far_col))


def near_swap(value, axis):
    return lax.ppermute(value, axis, [(i, i ^ 1) for i in range(lax.axis_size(axis))])


def far_swap(value, axis):
    pairs = [(i, i + 1) for i in range(1, lax.axis_size(axis) - 1, 2)]
    return lax.ppermute(value, axis, pairs + [(j, i) for i, j in pairs])


def doubling_steps(n_row, n_col):
    rest = [(0, 1 << k) for k in range(1, n_col.bit_length() - 1)]
    turned = list(rest)
    for k in range(0, len(rest) - 1, 2):
        turned[k], turned[k + 1] = rest[k + 1], rest[k]
    rows = [(1 << k, 0) for k in range(1, n_row.bit_length() - 1)]
    return list(zip(rows, rows)), list(zip(rest, turned)) + [((0, 1), (0, 1))]


def add_kernel(a_ref, b_ref, out_ref):
    out_ref[...] = a_ref[...] + b_ref[...]


def add_call(a, b):
    return pl.pallas_call(
        add_kernel,
        out_shape=near(a.shape),
        in_specs=[VMEM] * 2,
        out_specs=VMEM,
        compiler_params=PARAMS,
        cost_estimate=pl.CostEstimate(flops=2 * 10**9, bytes_accessed=10**5, transcendentals=0),
        name="add",
    )(*in_vmem(a, b))


def add_partner(mine, even, odd, add=jnp.add):
    n_row, n_col = lax.axis_size("trow"), lax.axis_size("tcol")
    pairs = []
    for r in range(n_row):
        for c in range(n_col):
            dr, dc = odd if r % 2 else even
            pairs.append((r * n_col + c, (r ^ dr) * n_col + (c ^ dc)))
    return add(mine, lax.ppermute(mine, ("trow", "tcol"), pairs))


def body(table, object_planes, probe, intensities, row_offsets, col_offsets, counts):
    size = probe.shape[1]
    rows, cols = row_offsets.reshape(-1), col_offsets.reshape(-1)
    measured = intensities.reshape(-1, size, size)
    near_row, far_row = edge_call(object_planes, size // 2)
    far_row = far_swap(far_row, "trow")
    near_row = near_swap(near_row, "trow")
    plan, turned, measured, tables, window = ready_call(rows, cols, counts, probe, measured, table, object_planes)
    window, near_side, far_side = side_call(window, near_row, far_row)
    far_col = far_swap(far_side, "tcol")
    near_col = near_swap(near_side, "tcol")
    grad, probe_sum = inner_call(plan, window, turned, measured, tables)
    grad, near_row, far_row, side, mine, other = outer_call(
        plan, window, near_col, far_col, turned, measured, tables, grad, probe_sum
    )

    along_rows, along_cols = doubling_steps(lax.axis_size("trow"), lax.axis_size("tcol"))
    mine = mine + near_swap(other, "trow")
    mine, near_row, far_row = lax.optimization_barrier((mine, near_row, far_row))
    near_row = near_swap(near_row, "trow")
    far_row = far_swap(far_row, "trow")
    for step in along_rows:
        mine = add_partner(mine, *step, add=add_call)
    near_side, far_side = side_sum_call(side, near_row, far_row)
    mine, near_side, far_side = lax.optimization_barrier((mine, near_side, far_side))
    near_col = near_swap(near_side, "tcol")
    far_col = far_swap(far_side, "tcol")
    for step in along_cols:
        mine = add_partner(mine, *step)
    object_grad = final_call(grad, near_row, far_row, near_col, far_col)
    other = near_swap(mine, "trow")
    odd_row, _ = parities()
    probe_grad = jnp.where(odd_row == 0, jnp.stack([mine, other]), jnp.stack([other, mine]))
    return (object_grad, probe_grad)


def solution(mesh):
    table = dft_tables(LANES)
    inner = jax.shard_map(
        body,
        mesh=mesh,
        in_specs=(
            P(),
            P(None, "trow", "tcol"),
            P(),
            P("trow", "tcol", None, None, None),
            P("trow", "tcol", None),
            P("trow", "tcol", None),
            P(("trow", "tcol")),
        ),
        out_specs=(P(None, "trow", "tcol"), P()),
        check_vma=False,
    )

    def run(*args):
        return inner(jnp.asarray(table), *args)

    return run
```

```python
import jax
import jax.numpy as jnp
import numpy as np
from jax import lax
from jax.experimental import pallas as pl
from jax.experimental.pallas import tpu as pltpu
from jax.sharding import PartitionSpec as P

LANES = 128
VMEM_BYTES = 24 * 1024 * 1024
GROUP = 8
F32 = jnp.float32
HBM = pl.BlockSpec(memory_space=pltpu.HBM)
VMEM = pl.BlockSpec(memory_space=pltpu.VMEM)
SMEM = pl.BlockSpec(memory_space=pltpu.SMEM)
PARAMS = pltpu.CompilerParams(vmem_limit_bytes=VMEM_BYTES)


def in_hbm(*arrays):
    return [pltpu.with_memory_space_constraint(array, pltpu.HBM) for array in arrays]


def in_vmem(*arrays):
    return [pltpu.with_memory_space_constraint(array, pltpu.VMEM) for array in arrays]


def in_smem(*arrays):
    return [pltpu.with_memory_space_constraint(array, pltpu.SMEM) for array in arrays]


def near(shape, dtype=F32):
    return pltpu.VMEM(tuple(shape), dtype)


def dft_tables(length):
    index = np.arange(length)
    angle = -2.0 * np.pi * (np.outer(index, index) % length) / length
    cosine, sine = np.cos(angle) / np.sqrt(length), np.sin(angle) / np.sqrt(length)
    right = np.block([[cosine, sine], [-sine, cosine]])
    return np.stack([right, right.T]).astype(np.float32)


def split(value):
    high = value.astype(jnp.bfloat16)
    low = (value - high.astype(F32)).astype(jnp.bfloat16)
    return high, low


def dot(a, b):
    return jnp.dot(a, b, preferred_element_type=F32)


def times_table(value, high, low):
    big, small = split(value)
    return dot(jnp.concatenate([big, small, big], axis=1), jnp.concatenate([high, high, low], axis=0))


def table_times(high, low, value):
    big, small = split(value)
    return dot(jnp.concatenate([high, high, low], axis=1), jnp.concatenate([big, small, big], axis=0))


def folded(tall, low_lanes):
    half = tall.shape[0] // 2
    lane = lax.broadcasted_iota(jnp.int32, (half, LANES), 1)
    here = (lane < LANES // 2) == low_lanes
    return jnp.where(here, tall[:half], pltpu.roll(tall[half:], LANES // 2, axis=1))


def parities():
    return lax.axis_index("trow") % 2, lax.axis_index("tcol") % 2


def place_of(odd, low, high):
    near = pl.multiple_of(jnp.where(odd == 1, low, high), 8)
    far = pl.multiple_of(jnp.where(odd == 1, high, low), 8)
    return near, far


def edge_kernel(centre_ref, near_out, far_out, sem):
    margin = near_out.shape[1]
    odd_row, _ = parities()
    near, far = place_of(odd_row, 0, centre_ref.shape[1] - margin)
    copies = [
        pltpu.make_async_copy(centre_ref.at[:, pl.ds(far, margin)], far_out, sem.at[0]),
        pltpu.make_async_copy(centre_ref.at[:, pl.ds(near, margin)], near_out, sem.at[1]),
    ]
    for copy in copies:
        copy.start()
    for copy in copies:
        copy.wait()


def edge_call(centre, margin):
    edge = near((2, margin, centre.shape[2]))
    return pl.pallas_call(
        edge_kernel,
        out_shape=(edge, edge),
        in_specs=[HBM],
        out_specs=(VMEM,) * 2,
        scratch_shapes=[pltpu.SemaphoreType.DMA((2,))],
        compiler_params=PARAMS,
        name="edge_rows",
    )(*in_hbm(centre))


def ready_kernel(
    rows_ref, cols_ref, count_ref, probe_ref, measured_ref, table_ref, centre_ref, plan, turned, measured, tables, window,
    row_list, col_list, probe, table, sem,
):
    slots = measured.shape[0]
    margin = probe.shape[1] // 2
    height, width = centre_ref.shape[1:]
    columns = window.shape[0] // 2
    inner_columns = width - probe.shape[2]
    copies = [(rows_ref, row_list), (cols_ref, col_list), (probe_ref, probe), (table_ref, table)]
    for plane in range(2):
        for tile in range(columns - 2):
            lanes = slice(tile * LANES, (tile + 1) * LANES)
            copies.append((centre_ref.at[plane, :, lanes], window.at[plane * columns + 1 + tile, pl.ds(margin, height)]))
    copies.append((measured_ref, measured))
    copies = [pltpu.make_async_copy(a, b, sem.at[i]) for i, (a, b) in enumerate(copies)]
    for copy in copies:
        copy.start()
    for copy in copies[:3]:
        copy.wait()
    count = count_ref[0, 0]
    inner = jnp.int32(0)
    for slot in range(slots):
        first = col_list[slot]
        live = slot < count
        is_inner = jnp.logical_and(jnp.logical_and(first >= 0, first <= inner_columns), live)
        at = jnp.where(is_inner, inner, slots - 1 - (slot - inner))
        plan[jnp.where(live, at, 5 * slots + 1)] = slot
        inner = inner + is_inner.astype(jnp.int32)
        col = first + LANES
        turn = col & (LANES - 1)
        place = slots + 2 + 3 * slot
        plan[place] = row_list[slot] + margin
        plan[place + 1] = lax.shift_right_logical(col, 7)
        plan[place + 2] = turn
        for plane in range(2):
            turned[slot, plane] = pltpu.roll(probe[plane], turn, axis=1)
    plan[slots] = inner
    plan[slots + 1] = count
    copies[3].wait()
    for index in range(2):
        tables[2 * index], tables[2 * index + 1] = split(table[index])
    for copy in copies[4:]:
        copy.wait()


def ready_call(rows, cols, count, probe, measured, table, centre):
    slots = measured.shape[0]
    height, width = centre.shape[1:]
    tiles = width // LANES
    return pl.pallas_call(
        ready_kernel,
        out_shape=(
            pltpu.SMEM((5 * slots + 2,), jnp.int32),
            near((slots,) + probe.shape),
            near(measured.shape, measured.dtype),
            near((4,) + table.shape[1:], jnp.bfloat16),
            near((2 * (tiles + 2), height + probe.shape[1], LANES)),
        ),
        in_specs=[HBM] * 2 + [VMEM] + [HBM] * 4,
        out_specs=(SMEM,) + (VMEM,) * 4,
        scratch_shapes=[
            pltpu.SMEM(rows.shape, jnp.int32),
            pltpu.SMEM(cols.shape, jnp.int32),
            pltpu.VMEM(probe.shape, F32),
            pltpu.VMEM(table.shape, F32),
            pltpu.SemaphoreType.DMA((5 + 2 * tiles,)),
        ],
        compiler_params=PARAMS,
        name="ready",
    )(*in_hbm(rows, cols), *in_vmem(jnp.broadcast_to(count, (8, LANES))), *in_hbm(probe, measured, table, centre))


def side_kernel(tile_ref, near_ref, far_ref, window, near_out, far_out):
    margin = near_ref.shape[1]
    columns = window.shape[0] // 2
    odd_row, odd_col = parities()
    bottom = window.shape[1] - margin
    near, far = place_of(odd_row, 0, bottom)
    for plane in range(2):
        for tile in range(columns - 2):
            lanes = slice(tile * LANES, (tile + 1) * LANES)
            window[plane * columns + 1 + tile, margin:bottom] = tile_ref[plane * columns + 1 + tile, margin:bottom]
            window[plane * columns + 1 + tile, pl.ds(near, margin), :] = near_ref[plane, :, lanes]
            window[plane * columns + 1 + tile, pl.ds(far, margin), :] = far_ref[plane, :, lanes]
    for plane in range(2):
        near_tile = plane * columns + jnp.where(odd_col == 1, 1, columns - 2)
        far_tile = plane * columns + jnp.where(odd_col == 1, columns - 2, 1)
        near_out[plane] = folded(window[near_tile], odd_col == 1)
        far_out[plane] = folded(window[far_tile], odd_col == 0)


def side_call(window, near_row, far_row):
    shape = near((2, window.shape[1] // 2, LANES))
    return pl.pallas_call(
        side_kernel,
        out_shape=(near(window.shape), shape, shape),
        in_specs=[VMEM] * 3,
        out_specs=(VMEM,) * 3,
        compiler_params=PARAMS,
        name="side_columns",
    )(*in_vmem(window, near_row, far_row))


def run_slots(groups, start, inner, live, plan, window, turned, measured, table, grad, probe_sum):
    slots = measured.shape[0]
    size = turned.shape[2]
    columns = window.shape[0] // 2
    lane = lax.broadcasted_iota(jnp.int32, (size, LANES), 1)

    def find(index):
        at = jnp.where(index < inner, start + index, jnp.maximum(slots - 1 - (index - inner), 0))
        is_live = index < live
        slot = plan[jnp.where(is_live, at, jnp.where(inner > 0, start, slots - 1))]
        place = slots + 2 + 3 * slot
        scale = jnp.where(is_live, 2.0, 0.0).astype(F32)
        return slot, plan[place], plan[place + 1], plan[place + 2], scale

    def load(pair):
        kept, waves = [], []
        for slot, row, tile, turn, _ in pair:
            here = lane >= turn
            patch = [
                jnp.where(
                    here,
                    window[plane * columns + tile, pl.ds(row, size), :],
                    window[plane * columns + tile + 1, pl.ds(row, size), :],
                )
                for plane in range(2)
            ]
            probe = [turned[slot, plane] for plane in range(2)]
            wave_real = probe[0] * patch[0] - probe[1] * patch[1]
            wave_imag = probe[0] * patch[1] + probe[1] * patch[0]
            kept.append(patch)
            waves.append(jnp.concatenate([wave_real, wave_imag], axis=1))
        return kept, jnp.concatenate(waves, axis=0)

    def regroup(pair):
        return jnp.concatenate(
            [
                jnp.concatenate([pair[:size, :size], pair[size:, :size]], axis=1),
                jnp.concatenate([pair[:size, size:], pair[size:, size:]], axis=1),
            ],
            axis=0,
        )

    def weigh(pair, psi):
        real, imag = psi[:size], psi[size:]
        weights = []
        for member, (slot, _, _, _, scale) in enumerate(pair):
            lanes = slice(member * size, (member + 1) * size)
            power = real[:, lanes] * real[:, lanes] + imag[:, lanes] * imag[:, lanes]
            weights.append((power - measured[slot].astype(F32)) * scale)
        weight = jnp.concatenate(weights, axis=1)
        return jnp.concatenate([weight * real, weight * imag], axis=0)

    def add_up(pair, kept, exits):
        for member, (slot, row, tile, turn, _) in enumerate(pair):
            patch = kept[member]
            probe = [turned[slot, plane] for plane in range(2)]
            here = lane >= turn
            exit_real = exits[member * size : (member + 1) * size, :size]
            exit_imag = exits[member * size : (member + 1) * size, size:]
            terms = (patch[0] * exit_real + patch[1] * exit_imag, patch[0] * exit_imag - patch[1] * exit_real)
            adds = (probe[0] * exit_real + probe[1] * exit_imag, probe[0] * exit_imag - probe[1] * exit_real)
            back = (LANES - turn) & (LANES - 1)
            for plane in range(2):
                probe_sum[plane] += pltpu.roll(terms[plane], back, axis=1)
                at = plane * columns + tile
                grad[at, pl.ds(row, size), :] += jnp.where(here, adds[plane], 0.0)
                grad[at + 1, pl.ds(row, size), :] += jnp.where(here, 0.0, adds[plane])

    def step(group, carry):
        slots = [find(group * GROUP + member) for member in range(GROUP)]
        pairs = [slots[member : member + 2] for member in range(0, GROUP, 2)]
        loaded = [load(pair) for pair in pairs]
        waves = [regroup(times_table(wave, table[0], table[1])) for _, wave in loaded]
        waves = [weigh(pair, table_times(table[2], table[3], wave)) for pair, wave in zip(pairs, waves)]
        waves = [regroup(table_times(table[0], table[1], wave)) for wave in waves]
        waves = [times_table(wave, table[2], table[3]) for wave in waves]
        for pair, (kept, _), wave in zip(pairs, loaded, waves):
            add_up(pair, kept, wave)
        return carry

    lax.fori_loop(0, groups, step, 0)


def inner_kernel(plan, window, turned, measured, table, grad, probe_sum):
    grad[...] = jnp.zeros_like(grad)
    probe_sum[...] = jnp.zeros_like(probe_sum)
    groups = plan[measured.shape[0]] // GROUP
    here = groups * GROUP
    run_slots(groups, 0, here, here, plan, window, turned, measured, table, grad, probe_sum)


def inner_call(plan, window, turned, measured, tables):
    return pl.pallas_call(
        inner_kernel,
        out_shape=(near(window.shape), near(turned.shape[1:])),
        in_specs=[SMEM] + [VMEM] * 4,
        out_specs=(VMEM,) * 2,
        compiler_params=PARAMS,
        cost_estimate=pl.CostEstimate(flops=10**10, bytes_accessed=2 * 10**7, transcendentals=0),
        name="slots_inside",
    )(*in_smem(plan), *in_vmem(window, turned, measured, tables))


def outer_kernel(
    plan, window_ref, near_col_ref, far_col_ref, turned, measured, table, grad_ref, probe_ref,
    grad, near_row_out, far_row_out, side_out, mine_out, other_out, window, probe_sum,
):
    slots = measured.shape[0]
    margin = turned.shape[2] // 2
    columns = window.shape[0] // 2
    tall = window.shape[1]
    half = tall // 2
    odd_row, odd_col = parities()
    near, far = place_of(odd_row, 0, tall - margin)
    probe_sum[...] = probe_ref[...]
    grad[...] = grad_ref[...]
    for plane in range(2):
        own = slice(plane * columns + 1, (plane + 1) * columns - 1)
        window[own] = window_ref[own]
        near_tile = plane * columns + jnp.where(odd_col == 1, 0, columns - 1)
        far_tile = plane * columns + jnp.where(odd_col == 1, columns - 1, 0)
        for tile, ref in ((near_tile, near_col_ref), (far_tile, far_col_ref)):
            window[tile, :half] = ref[plane]
            window[tile, half:] = pltpu.roll(ref[plane], margin, axis=1)
    start = plan[slots] // GROUP * GROUP
    inner = plan[slots] - start
    live = plan[slots + 1] - start
    run_slots(
        (live + GROUP - 1) // GROUP, start, inner, live, plan, window, turned, measured, table, grad, probe_sum
    )
    factor = 1.0 / np.sqrt(np.float32(lax.axis_size("trow") * lax.axis_size("tcol") * slots))
    mine_out[...] = probe_sum[odd_row] * factor
    other_out[...] = probe_sum[1 - odd_row] * factor
    narrow = lax.broadcasted_iota(jnp.int32, (margin, LANES), 1) < margin
    for plane in range(2):
        base = plane * columns
        left, right = base, base + columns - 1
        for at, out in ((near, near_row_out), (far, far_row_out)):
            rows = pl.ds(at, margin)
            for tile in range(columns - 2):
                out[plane, :, tile * LANES : (tile + 1) * LANES] = grad[base + 1 + tile, rows, :]
            out[plane, :, (columns - 2) * LANES :] = jnp.where(narrow, grad[right, rows, :], grad[left, rows, :])
        for row in range(margin, tall - margin, margin):
            rows = slice(row, row + margin)
            side_out[plane, row - margin : row] = jnp.where(narrow, grad[right, rows, :], grad[left, rows, :])


def outer_call(plan, window, near_col, far_col, turned, measured, tables, grad, probe_sum):
    size = turned.shape[2]
    margin = size // 2
    columns = window.shape[0] // 2
    row = near((2, margin, (columns - 1) * LANES))
    part = near((size, size))
    return pl.pallas_call(
        outer_kernel,
        out_shape=(near(grad.shape), row, row, near((2, window.shape[1] - size, LANES)), part, part),
        in_specs=[SMEM] + [VMEM] * 8,
        out_specs=(VMEM,) * 6,
        scratch_shapes=[pltpu.VMEM(window.shape, F32), pltpu.VMEM(probe_sum.shape, F32)],
        compiler_params=PARAMS,
        cost_estimate=pl.CostEstimate(flops=10**10, bytes_accessed=2 * 10**7, transcendentals=0),
        name="slots_across",
    )(*in_smem(plan), *in_vmem(window, near_col, far_col, turned, measured, tables, grad, probe_sum))


def side_sum_kernel(side_ref, near_ref, far_ref, near_out, far_out, side):
    margin = near_ref.shape[1]
    height = side_ref.shape[1]
    odd_row, odd_col = parities()
    near_at, far_at = place_of(odd_row, 0, height - margin)
    wide = near_ref.shape[2]
    side[...] = side_ref[...]
    for plane in range(2):
        side[plane, pl.ds(near_at, margin), :] += near_ref[plane, :, wide - LANES :]
        side[plane, pl.ds(far_at, margin), :] += far_ref[plane, :, wide - LANES :]
    for plane in range(2):
        near_out[plane] = folded(side[plane], odd_col == 0)
        far_out[plane] = folded(side[plane], odd_col == 1)


def side_sum_call(side, near_row, far_row):
    shape = near((2, side.shape[1] // 2, LANES))
    return pl.pallas_call(
        side_sum_kernel,
        out_shape=(shape, shape),
        in_specs=[VMEM] * 3,
        out_specs=(VMEM, VMEM),
        scratch_shapes=[pltpu.VMEM(side.shape, F32)],
        compiler_params=PARAMS,
        name="side_sums",
    )(*in_vmem(side, near_row, far_row))


def final_kernel(grad, near_row_ref, far_row_ref, near_col_ref, far_col_ref, out_ref):
    height, width = out_ref.shape[1:]
    columns = grad.shape[0] // 2
    margin = near_row_ref.shape[1]
    half = height // 2
    odd_row, odd_col = parities()
    near_at, far_at = place_of(odd_row, 0, height - margin)
    narrow = lax.broadcasted_iota(jnp.int32, (half, LANES), 1) < LANES // 2
    for plane in range(2):
        for tile in range(columns - 2):
            lanes = slice(tile * LANES, (tile + 1) * LANES)
            out_ref[plane, :, lanes] = grad[plane * columns + 1 + tile, margin : margin + height]
        near = jnp.where(odd_col == 1, near_col_ref[plane], far_col_ref[plane])
        far = jnp.where(odd_col == 1, far_col_ref[plane], near_col_ref[plane])
        for first, left, right in (
            (0, near, far),
            (half, pltpu.roll(near, LANES // 2, axis=1), pltpu.roll(far, LANES // 2, axis=1)),
        ):
            rows = slice(first, first + half)
            out_ref[plane, rows, :LANES] += jnp.where(narrow, left, 0.0)
            out_ref[plane, rows, width - LANES :] += jnp.where(narrow, 0.0, right)
        out_ref[plane, pl.ds(near_at, margin), :] += near_row_ref[plane, :, :width]
        out_ref[plane, pl.ds(far_at, margin), :] += far_row_ref[plane, :, :width]


def final_call(grad, near_row, far_row, near_col, far_col):
    margin = near_row.shape[1]
    shape = (2, grad.shape[1] - 2 * margin, near_row.shape[2] - LANES)
    return pl.pallas_call(
        final_kernel,
        out_shape=jax.ShapeDtypeStruct(shape, F32),
        in_specs=[VMEM] * 5,
        out_specs=VMEM,
        compiler_params=PARAMS,
        name="final_sums",
    )(*in_vmem(grad, near_row, far_row, near_col, far_col))


def near_swap(value, axis):
    return lax.ppermute(value, axis, [(i, i ^ 1) for i in range(lax.axis_size(axis))])


def far_swap(value, axis):
    pairs = [(i, i + 1) for i in range(1, lax.axis_size(axis) - 1, 2)]
    return lax.ppermute(value, axis, pairs + [(j, i) for i, j in pairs])


def doubling_steps(n_row, n_col):
    rest = [(0, 1 << k) for k in range(1, n_col.bit_length() - 1)]
    turned = list(rest)
    for k in range(0, len(rest) - 1, 2):
        turned[k], turned[k + 1] = rest[k + 1], rest[k]
    rows = [(1 << k, 0) for k in range(1, n_row.bit_length() - 1)]
    return list(zip(rows, rows)), list(zip(rest, turned)) + [((0, 1), (0, 1))]


def add_kernel(a_ref, b_ref, out_ref):
    out_ref[...] = a_ref[...] + b_ref[...]


def add_call(a, b):
    return pl.pallas_call(
        add_kernel,
        out_shape=near(a.shape),
        in_specs=[VMEM] * 2,
        out_specs=VMEM,
        compiler_params=PARAMS,
        cost_estimate=pl.CostEstimate(flops=10**9, bytes_accessed=10**5, transcendentals=0),
        name="add",
    )(*in_vmem(a, b))


def add_partner(mine, even, odd, add=jnp.add):
    n_row, n_col = lax.axis_size("trow"), lax.axis_size("tcol")
    pairs = []
    for r in range(n_row):
        for c in range(n_col):
            dr, dc = odd if r % 2 else even
            pairs.append((r * n_col + c, (r ^ dr) * n_col + (c ^ dc)))
    return add(mine, lax.ppermute(mine, ("trow", "tcol"), pairs))


def body(table, object_planes, probe, intensities, row_offsets, col_offsets, counts):
    size = probe.shape[1]
    rows, cols = row_offsets.reshape(-1), col_offsets.reshape(-1)
    measured = intensities.reshape(-1, size, size)
    near_row, far_row = edge_call(object_planes, size // 2)
    far_row = far_swap(far_row, "trow")
    near_row = near_swap(near_row, "trow")
    plan, turned, measured, tables, window = ready_call(rows, cols, counts, probe, measured, table, object_planes)
    window, near_side, far_side = side_call(window, near_row, far_row)
    far_col = far_swap(far_side, "tcol")
    near_col = near_swap(near_side, "tcol")
    grad, probe_sum = inner_call(plan, window, turned, measured, tables)
    grad, near_row, far_row, side, mine, other = outer_call(
        plan, window, near_col, far_col, turned, measured, tables, grad, probe_sum
    )

    along_rows, along_cols = doubling_steps(lax.axis_size("trow"), lax.axis_size("tcol"))
    mine = mine + near_swap(other, "trow")
    mine, near_row, far_row = lax.optimization_barrier((mine, near_row, far_row))
    near_row = near_swap(near_row, "trow")
    far_row = far_swap(far_row, "trow")
    mine = add_partner(mine, *along_cols[-1])
    mine = add_partner(mine, *along_cols[0], add=add_call)
    near_side, far_side = side_sum_call(side, near_row, far_row)
    mine, near_side, far_side = lax.optimization_barrier((mine, near_side, far_side))
    near_col = near_swap(near_side, "tcol")
    far_col = far_swap(far_side, "tcol")
    for step in along_cols[1:-1] + along_rows:
        mine = add_partner(mine, *step)
    object_grad = final_call(grad, near_row, far_row, near_col, far_col)
    other = near_swap(mine, "trow")
    odd_row, _ = parities()
    probe_grad = jnp.where(odd_row == 0, jnp.stack([mine, other]), jnp.stack([other, mine]))
    return (object_grad, probe_grad)


def solution(mesh):
    table = dft_tables(LANES)
    inner = jax.shard_map(
        body,
        mesh=mesh,
        in_specs=(
            P(),
            P(None, "trow", "tcol"),
            P(),
            P("trow", "tcol", None, None, None),
            P("trow", "tcol", None),
            P("trow", "tcol", None),
            P(("trow", "tcol")),
        ),
        out_specs=(P(None, "trow", "tcol"), P()),
        check_vma=False,
    )

    def run(*args):
        return inner(jnp.asarray(table), *args)

    return run
```

```python
import jax
import jax.numpy as jnp
import numpy as np
from jax import lax
from jax.experimental import pallas as pl
from jax.experimental.pallas import tpu as pltpu
from jax.sharding import PartitionSpec as P

LANES = 128
VMEM_BYTES = 24 * 1024 * 1024
GROUP = 8
F32 = jnp.float32
HBM = pl.BlockSpec(memory_space=pltpu.HBM)
VMEM = pl.BlockSpec(memory_space=pltpu.VMEM)
SMEM = pl.BlockSpec(memory_space=pltpu.SMEM)
PARAMS = pltpu.CompilerParams(vmem_limit_bytes=VMEM_BYTES)


def in_hbm(*arrays):
    return [pltpu.with_memory_space_constraint(array, pltpu.HBM) for array in arrays]


def in_vmem(*arrays):
    return [pltpu.with_memory_space_constraint(array, pltpu.VMEM) for array in arrays]


def in_smem(*arrays):
    return [pltpu.with_memory_space_constraint(array, pltpu.SMEM) for array in arrays]


def near(shape, dtype=F32):
    return pltpu.VMEM(tuple(shape), dtype)


def dft_tables(length):
    index = np.arange(length)
    angle = -2.0 * np.pi * (np.outer(index, index) % length) / length
    cosine, sine = np.cos(angle) / np.sqrt(length), np.sin(angle) / np.sqrt(length)
    right = np.block([[cosine, sine], [-sine, cosine]])
    return np.stack([right, right.T]).astype(np.float32)


def split(value):
    high = value.astype(jnp.bfloat16)
    low = (value - high.astype(F32)).astype(jnp.bfloat16)
    return high, low


def dot(a, b):
    return jnp.dot(a, b, preferred_element_type=F32)


def times_table(value, high, low):
    big, small = split(value)
    return dot(jnp.concatenate([big, small, big], axis=1), jnp.concatenate([high, high, low], axis=0))


def table_times(high, low, value):
    big, small = split(value)
    return dot(jnp.concatenate([high, high, low], axis=1), jnp.concatenate([big, small, big], axis=0))


def folded(tall, low_lanes):
    half = tall.shape[0] // 2
    lane = lax.broadcasted_iota(jnp.int32, (half, LANES), 1)
    here = (lane < LANES // 2) == low_lanes
    return jnp.where(here, tall[:half], pltpu.roll(tall[half:], LANES // 2, axis=1))


def parities():
    return lax.axis_index("trow") % 2, lax.axis_index("tcol") % 2


def place_of(odd, low, high):
    near = pl.multiple_of(jnp.where(odd == 1, low, high), 8)
    far = pl.multiple_of(jnp.where(odd == 1, high, low), 8)
    return near, far


def edge_kernel(centre_ref, near_out, far_out, sem):
    margin = near_out.shape[1]
    odd_row, _ = parities()
    near, far = place_of(odd_row, 0, centre_ref.shape[1] - margin)
    copies = [
        pltpu.make_async_copy(centre_ref.at[:, pl.ds(far, margin)], far_out, sem.at[0]),
        pltpu.make_async_copy(centre_ref.at[:, pl.ds(near, margin)], near_out, sem.at[1]),
    ]
    for copy in copies:
        copy.start()
    for copy in copies:
        copy.wait()


def edge_call(centre, margin):
    edge = near((2, margin, centre.shape[2]))
    return pl.pallas_call(
        edge_kernel,
        out_shape=(edge, edge),
        in_specs=[HBM],
        out_specs=(VMEM,) * 2,
        scratch_shapes=[pltpu.SemaphoreType.DMA((2,))],
        compiler_params=PARAMS,
        name="edge_rows",
    )(*in_hbm(centre))


def ready_kernel(
    rows_ref, cols_ref, count_ref, probe_ref, measured_ref, table_ref, centre_ref, plan, turned, measured, tables, window,
    row_list, col_list, probe, table, sem,
):
    slots = measured.shape[0]
    margin = probe.shape[1] // 2
    height, width = centre_ref.shape[1:]
    columns = window.shape[0] // 2
    inner_columns = width - probe.shape[2]
    copies = [(rows_ref, row_list), (cols_ref, col_list), (probe_ref, probe), (table_ref, table)]
    for plane in range(2):
        for tile in range(columns - 2):
            lanes = slice(tile * LANES, (tile + 1) * LANES)
            copies.append((centre_ref.at[plane, :, lanes], window.at[plane * columns + 1 + tile, pl.ds(margin, height)]))
    copies.append((measured_ref, measured))
    copies = [pltpu.make_async_copy(a, b, sem.at[i]) for i, (a, b) in enumerate(copies)]
    for copy in copies:
        copy.start()
    for copy in copies[:3]:
        copy.wait()
    count = count_ref[0, 0]
    inner = jnp.int32(0)
    for slot in range(slots):
        first = col_list[slot]
        live = slot < count
        is_inner = jnp.logical_and(jnp.logical_and(first >= 0, first <= inner_columns), live)
        at = jnp.where(is_inner, inner, slots - 1 - (slot - inner))
        plan[jnp.where(live, at, 5 * slots + 1)] = slot
        inner = inner + is_inner.astype(jnp.int32)
        col = first + LANES
        turn = col & (LANES - 1)
        place = slots + 2 + 3 * slot
        plan[place] = row_list[slot] + margin
        plan[place + 1] = lax.shift_right_logical(col, 7)
        plan[place + 2] = turn
        for plane in range(2):
            turned[slot, plane] = pltpu.roll(probe[plane], turn, axis=1)
    plan[slots] = inner
    plan[slots + 1] = count
    copies[3].wait()
    for index in range(2):
        tables[2 * index], tables[2 * index + 1] = split(table[index])
    for copy in copies[4:]:
        copy.wait()


def ready_call(rows, cols, count, probe, measured, table, centre):
    slots = measured.shape[0]
    height, width = centre.shape[1:]
    tiles = width // LANES
    return pl.pallas_call(
        ready_kernel,
        out_shape=(
            pltpu.SMEM((5 * slots + 2,), jnp.int32),
            near((slots,) + probe.shape),
            near(measured.shape, measured.dtype),
            near((4,) + table.shape[1:], jnp.bfloat16),
            near((2 * (tiles + 2), height + probe.shape[1], LANES)),
        ),
        in_specs=[HBM] * 2 + [VMEM] + [HBM] * 4,
        out_specs=(SMEM,) + (VMEM,) * 4,
        scratch_shapes=[
            pltpu.SMEM(rows.shape, jnp.int32),
            pltpu.SMEM(cols.shape, jnp.int32),
            pltpu.VMEM(probe.shape, F32),
            pltpu.VMEM(table.shape, F32),
            pltpu.SemaphoreType.DMA((5 + 2 * tiles,)),
        ],
        compiler_params=PARAMS,
        name="ready",
    )(*in_hbm(rows, cols), *in_vmem(jnp.broadcast_to(count, (8, LANES))), *in_hbm(probe, measured, table, centre))


def side_kernel(tile_ref, near_ref, far_ref, window, near_out, far_out):
    margin = near_ref.shape[1]
    columns = window.shape[0] // 2
    odd_row, odd_col = parities()
    bottom = window.shape[1] - margin
    near, far = place_of(odd_row, 0, bottom)
    for plane in range(2):
        for tile in range(columns - 2):
            lanes = slice(tile * LANES, (tile + 1) * LANES)
            window[plane * columns + 1 + tile, margin:bottom] = tile_ref[plane * columns + 1 + tile, margin:bottom]
            window[plane * columns + 1 + tile, pl.ds(near, margin), :] = near_ref[plane, :, lanes]
            window[plane * columns + 1 + tile, pl.ds(far, margin), :] = far_ref[plane, :, lanes]
    for plane in range(2):
        near_tile = plane * columns + jnp.where(odd_col == 1, 1, columns - 2)
        far_tile = plane * columns + jnp.where(odd_col == 1, columns - 2, 1)
        near_out[plane] = folded(window[near_tile], odd_col == 1)
        far_out[plane] = folded(window[far_tile], odd_col == 0)


def side_call(window, near_row, far_row):
    shape = near((2, window.shape[1] // 2, LANES))
    return pl.pallas_call(
        side_kernel,
        out_shape=(near(window.shape), shape, shape),
        in_specs=[VMEM] * 3,
        out_specs=(VMEM,) * 3,
        compiler_params=PARAMS,
        name="side_columns",
    )(*in_vmem(window, near_row, far_row))


def run_slots(groups, start, inner, live, plan, window, turned, measured, table, grad, probe_sum):
    slots = measured.shape[0]
    size = turned.shape[2]
    columns = window.shape[0] // 2
    lane = lax.broadcasted_iota(jnp.int32, (size, LANES), 1)

    def find(index):
        at = jnp.where(index < inner, start + index, jnp.maximum(slots - 1 - (index - inner), 0))
        is_live = index < live
        slot = plan[jnp.where(is_live, at, jnp.where(inner > 0, start, slots - 1))]
        place = slots + 2 + 3 * slot
        scale = jnp.where(is_live, 2.0, 0.0).astype(F32)
        return slot, plan[place], plan[place + 1], plan[place + 2], scale

    def load(pair):
        kept, waves = [], []
        for slot, row, tile, turn, _ in pair:
            here = lane >= turn
            patch = [
                jnp.where(
                    here,
                    window[plane * columns + tile, pl.ds(row, size), :],
                    window[plane * columns + tile + 1, pl.ds(row, size), :],
                )
                for plane in range(2)
            ]
            probe = [turned[slot, plane] for plane in range(2)]
            wave_real = probe[0] * patch[0] - probe[1] * patch[1]
            wave_imag = probe[0] * patch[1] + probe[1] * patch[0]
            kept.append(patch)
            waves.append(jnp.concatenate([wave_real, wave_imag], axis=1))
        return kept, jnp.concatenate(waves, axis=0)

    def regroup(pair):
        return jnp.concatenate(
            [
                jnp.concatenate([pair[:size, :size], pair[size:, :size]], axis=1),
                jnp.concatenate([pair[:size, size:], pair[size:, size:]], axis=1),
            ],
            axis=0,
        )

    def weigh(pair, psi):
        real, imag = psi[:size], psi[size:]
        weights = []
        for member, (slot, _, _, _, scale) in enumerate(pair):
            lanes = slice(member * size, (member + 1) * size)
            power = real[:, lanes] * real[:, lanes] + imag[:, lanes] * imag[:, lanes]
            weights.append((power - measured[slot].astype(F32)) * scale)
        weight = jnp.concatenate(weights, axis=1)
        return jnp.concatenate([weight * real, weight * imag], axis=0)

    def add_up(pair, kept, exits):
        for member, (slot, row, tile, turn, _) in enumerate(pair):
            patch = kept[member]
            probe = [turned[slot, plane] for plane in range(2)]
            here = lane >= turn
            exit_real = exits[member * size : (member + 1) * size, :size]
            exit_imag = exits[member * size : (member + 1) * size, size:]
            terms = (patch[0] * exit_real + patch[1] * exit_imag, patch[0] * exit_imag - patch[1] * exit_real)
            adds = (probe[0] * exit_real + probe[1] * exit_imag, probe[0] * exit_imag - probe[1] * exit_real)
            back = (LANES - turn) & (LANES - 1)
            for plane in range(2):
                probe_sum[plane] += pltpu.roll(terms[plane], back, axis=1)
                at = plane * columns + tile
                grad[at, pl.ds(row, size), :] += jnp.where(here, adds[plane], 0.0)
                grad[at + 1, pl.ds(row, size), :] += jnp.where(here, 0.0, adds[plane])

    def step(group, carry):
        slots = [find(group * GROUP + member) for member in range(GROUP)]
        pairs = [slots[member : member + 2] for member in range(0, GROUP, 2)]
        loaded = [load(pair) for pair in pairs]
        waves = [regroup(times_table(wave, table[0], table[1])) for _, wave in loaded]
        waves = [weigh(pair, table_times(table[2], table[3], wave)) for pair, wave in zip(pairs, waves)]
        waves = [regroup(table_times(table[0], table[1], wave)) for wave in waves]
        waves = [times_table(wave, table[2], table[3]) for wave in waves]
        for pair, (kept, _), wave in zip(pairs, loaded, waves):
            add_up(pair, kept, wave)
        return carry

    lax.fori_loop(0, groups, step, 0)


def inner_kernel(plan, window, turned, measured, table, grad, probe_sum):
    grad[...] = jnp.zeros_like(grad)
    probe_sum[...] = jnp.zeros_like(probe_sum)
    groups = plan[measured.shape[0]] // GROUP
    here = groups * GROUP
    run_slots(groups, 0, here, here, plan, window, turned, measured, table, grad, probe_sum)


def inner_call(plan, window, turned, measured, tables):
    return pl.pallas_call(
        inner_kernel,
        out_shape=(near(window.shape), near(turned.shape[1:])),
        in_specs=[SMEM] + [VMEM] * 4,
        out_specs=(VMEM,) * 2,
        compiler_params=PARAMS,
        cost_estimate=pl.CostEstimate(flops=10**10, bytes_accessed=2 * 10**7, transcendentals=0),
        name="slots_inside",
    )(*in_smem(plan), *in_vmem(window, turned, measured, tables))


def outer_kernel(
    plan, window_ref, near_col_ref, far_col_ref, turned, measured, table, grad_ref, probe_ref,
    grad, near_row_out, far_row_out, side_out, mine_out, other_out, window, probe_sum,
):
    slots = measured.shape[0]
    margin = turned.shape[2] // 2
    columns = window.shape[0] // 2
    tall = window.shape[1]
    half = tall // 2
    odd_row, odd_col = parities()
    near, far = place_of(odd_row, 0, tall - margin)
    probe_sum[...] = probe_ref[...]
    grad[...] = grad_ref[...]
    for plane in range(2):
        own = slice(plane * columns + 1, (plane + 1) * columns - 1)
        window[own] = window_ref[own]
        near_tile = plane * columns + jnp.where(odd_col == 1, 0, columns - 1)
        far_tile = plane * columns + jnp.where(odd_col == 1, columns - 1, 0)
        for tile, ref in ((near_tile, near_col_ref), (far_tile, far_col_ref)):
            window[tile, :half] = ref[plane]
            window[tile, half:] = pltpu.roll(ref[plane], margin, axis=1)
    start = plan[slots] // GROUP * GROUP
    inner = plan[slots] - start
    live = plan[slots + 1] - start
    run_slots(
        (live + GROUP - 1) // GROUP, start, inner, live, plan, window, turned, measured, table, grad, probe_sum
    )
    factor = 1.0 / np.sqrt(np.float32(lax.axis_size("trow") * lax.axis_size("tcol") * slots))
    mine_out[...] = probe_sum[odd_row] * factor
    other_out[...] = probe_sum[1 - odd_row] * factor
    narrow = lax.broadcasted_iota(jnp.int32, (margin, LANES), 1) < margin
    for plane in range(2):
        base = plane * columns
        left, right = base, base + columns - 1
        for at, out in ((near, near_row_out), (far, far_row_out)):
            rows = pl.ds(at, margin)
            for tile in range(columns - 2):
                out[plane, :, tile * LANES : (tile + 1) * LANES] = grad[base + 1 + tile, rows, :]
            out[plane, :, (columns - 2) * LANES :] = jnp.where(narrow, grad[right, rows, :], grad[left, rows, :])
        for row in range(margin, tall - margin, margin):
            rows = slice(row, row + margin)
            side_out[plane, row - margin : row] = jnp.where(narrow, grad[right, rows, :], grad[left, rows, :])


def outer_call(plan, window, near_col, far_col, turned, measured, tables, grad, probe_sum):
    size = turned.shape[2]
    margin = size // 2
    columns = window.shape[0] // 2
    row = near((2, margin, (columns - 1) * LANES))
    part = near((size, size))
    return pl.pallas_call(
        outer_kernel,
        out_shape=(near(grad.shape), row, row, near((2, window.shape[1] - size, LANES)), part, part),
        in_specs=[SMEM] + [VMEM] * 8,
        out_specs=(VMEM,) * 6,
        scratch_shapes=[pltpu.VMEM(window.shape, F32), pltpu.VMEM(probe_sum.shape, F32)],
        compiler_params=PARAMS,
        cost_estimate=pl.CostEstimate(flops=10**10, bytes_accessed=2 * 10**7, transcendentals=0),
        name="slots_across",
    )(*in_smem(plan), *in_vmem(window, near_col, far_col, turned, measured, tables, grad, probe_sum))


def side_sum_kernel(side_ref, near_ref, far_ref, near_out, far_out, side):
    margin = near_ref.shape[1]
    height = side_ref.shape[1]
    odd_row, odd_col = parities()
    near_at, far_at = place_of(odd_row, 0, height - margin)
    wide = near_ref.shape[2]
    side[...] = side_ref[...]
    for plane in range(2):
        side[plane, pl.ds(near_at, margin), :] += near_ref[plane, :, wide - LANES :]
        side[plane, pl.ds(far_at, margin), :] += far_ref[plane, :, wide - LANES :]
    for plane in range(2):
        near_out[plane] = folded(side[plane], odd_col == 0)
        far_out[plane] = folded(side[plane], odd_col == 1)


def side_sum_call(side, near_row, far_row):
    shape = near((2, side.shape[1] // 2, LANES))
    return pl.pallas_call(
        side_sum_kernel,
        out_shape=(shape, shape),
        in_specs=[VMEM] * 3,
        out_specs=(VMEM, VMEM),
        scratch_shapes=[pltpu.VMEM(side.shape, F32)],
        compiler_params=PARAMS,
        name="side_sums",
    )(*in_vmem(side, near_row, far_row))


def final_kernel(grad, near_row_ref, far_row_ref, near_col_ref, far_col_ref, out_ref):
    height, width = out_ref.shape[1:]
    columns = grad.shape[0] // 2
    margin = near_row_ref.shape[1]
    half = height // 2
    odd_row, odd_col = parities()
    near_at, far_at = place_of(odd_row, 0, height - margin)
    narrow = lax.broadcasted_iota(jnp.int32, (half, LANES), 1) < LANES // 2
    for plane in range(2):
        for tile in range(columns - 2):
            lanes = slice(tile * LANES, (tile + 1) * LANES)
            out_ref[plane, :, lanes] = grad[plane * columns + 1 + tile, margin : margin + height]
        near = jnp.where(odd_col == 1, near_col_ref[plane], far_col_ref[plane])
        far = jnp.where(odd_col == 1, far_col_ref[plane], near_col_ref[plane])
        for first, left, right in (
            (0, near, far),
            (half, pltpu.roll(near, LANES // 2, axis=1), pltpu.roll(far, LANES // 2, axis=1)),
        ):
            rows = slice(first, first + half)
            out_ref[plane, rows, :LANES] += jnp.where(narrow, left, 0.0)
            out_ref[plane, rows, width - LANES :] += jnp.where(narrow, 0.0, right)
        out_ref[plane, pl.ds(near_at, margin), :] += near_row_ref[plane, :, :width]
        out_ref[plane, pl.ds(far_at, margin), :] += far_row_ref[plane, :, :width]


def final_call(grad, near_row, far_row, near_col, far_col):
    margin = near_row.shape[1]
    shape = (2, grad.shape[1] - 2 * margin, near_row.shape[2] - LANES)
    return pl.pallas_call(
        final_kernel,
        out_shape=jax.ShapeDtypeStruct(shape, F32),
        in_specs=[VMEM] * 5,
        out_specs=VMEM,
        compiler_params=PARAMS,
        name="final_sums",
    )(*in_vmem(grad, near_row, far_row, near_col, far_col))


def near_swap(value, axis):
    return lax.ppermute(value, axis, [(i, i ^ 1) for i in range(lax.axis_size(axis))])


def far_swap(value, axis):
    pairs = [(i, i + 1) for i in range(1, lax.axis_size(axis) - 1, 2)]
    return lax.ppermute(value, axis, pairs + [(j, i) for i, j in pairs])


def doubling_steps(n_row, n_col):
    along_cols = [(0, 1)] + [(0, 1 << k) for k in range(1, n_col.bit_length() - 1)][::-1]
    along_rows = [(1 << k, 0) for k in range(1, n_row.bit_length() - 1)]
    return along_rows, along_cols


def add_kernel(a_ref, b_ref, out_ref):
    out_ref[...] = a_ref[...] + b_ref[...]


def add_call(a, b):
    return pl.pallas_call(
        add_kernel,
        out_shape=near(a.shape),
        in_specs=[VMEM] * 2,
        out_specs=VMEM,
        compiler_params=PARAMS,
        cost_estimate=pl.CostEstimate(flops=10**9, bytes_accessed=10**5, transcendentals=0),
        name="add",
    )(*in_vmem(a, b))


def add_partner(mine, step, add=jnp.add):
    n_row, n_col = lax.axis_size("trow"), lax.axis_size("tcol")
    pairs = [(r * n_col + c, (r ^ step[0]) * n_col + (c ^ step[1])) for r in range(n_row) for c in range(n_col)]
    return add(mine, lax.ppermute(mine, ("trow", "tcol"), pairs))


def body(table, object_planes, probe, intensities, row_offsets, col_offsets, counts):
    size = probe.shape[1]
    rows, cols = row_offsets.reshape(-1), col_offsets.reshape(-1)
    measured = intensities.reshape(-1, size, size)
    near_row, far_row = edge_call(object_planes, size // 2)
    far_row = far_swap(far_row, "trow")
    near_row = near_swap(near_row, "trow")
    plan, turned, measured, tables, window = ready_call(rows, cols, counts, probe, measured, table, object_planes)
    window, near_side, far_side = side_call(window, near_row, far_row)
    far_col = far_swap(far_side, "tcol")
    near_col = near_swap(near_side, "tcol")
    grad, probe_sum = inner_call(plan, window, turned, measured, tables)
    grad, near_row, far_row, side, mine, other = outer_call(
        plan, window, near_col, far_col, turned, measured, tables, grad, probe_sum
    )

    along_rows, along_cols = doubling_steps(lax.axis_size("trow"), lax.axis_size("tcol"))
    mine = mine + near_swap(other, "trow")
    mine, near_row, far_row = lax.optimization_barrier((mine, near_row, far_row))
    near_row = near_swap(near_row, "trow")
    far_row = far_swap(far_row, "trow")
    mine = add_partner(mine, along_cols[0])
    mine = add_partner(mine, along_cols[1], add=add_call)
    near_side, far_side = side_sum_call(side, near_row, far_row)
    mine, near_side, far_side = lax.optimization_barrier((mine, near_side, far_side))
    near_col = near_swap(near_side, "tcol")
    far_col = far_swap(far_side, "tcol")
    for step in along_cols[2:] + along_rows:
        mine = add_partner(mine, step)
    mine, near_col, far_col = lax.optimization_barrier((mine, near_col, far_col))
    object_grad = final_call(grad, near_row, far_row, near_col, far_col)
    other = near_swap(mine, "trow")
    odd_row, _ = parities()
    probe_grad = jnp.where(odd_row == 0, jnp.stack([mine, other]), jnp.stack([other, mine]))
    return (object_grad, probe_grad)


def solution(mesh):
    table = dft_tables(LANES)
    inner = jax.shard_map(
        body,
        mesh=mesh,
        in_specs=(
            P(),
            P(None, "trow", "tcol"),
            P(),
            P("trow", "tcol", None, None, None),
            P("trow", "tcol", None),
            P("trow", "tcol", None),
            P(("trow", "tcol")),
        ),
        out_specs=(P(None, "trow", "tcol"), P()),
        check_vma=False,
    )

    def run(*args):
        return inner(jnp.asarray(table), *args)

    return run
```

```python
import jax
import jax.numpy as jnp
import numpy as np
from jax import lax
from jax.experimental import pallas as pl
from jax.experimental.pallas import tpu as pltpu
from jax.sharding import PartitionSpec as P

LANES = 128
VMEM_BYTES = 24 * 1024 * 1024
GROUP = 8
ADDED = 4
F32 = jnp.float32
HBM = pl.BlockSpec(memory_space=pltpu.HBM)
VMEM = pl.BlockSpec(memory_space=pltpu.VMEM)
SMEM = pl.BlockSpec(memory_space=pltpu.SMEM)
PARAMS = pltpu.CompilerParams(vmem_limit_bytes=VMEM_BYTES)


def in_hbm(*arrays):
    return [pltpu.with_memory_space_constraint(array, pltpu.HBM) for array in arrays]


def in_vmem(*arrays):
    return [pltpu.with_memory_space_constraint(array, pltpu.VMEM) for array in arrays]


def in_smem(*arrays):
    return [pltpu.with_memory_space_constraint(array, pltpu.SMEM) for array in arrays]


def near(shape, dtype=F32):
    return pltpu.VMEM(tuple(shape), dtype)


def dft_tables(length):
    index = np.arange(length)
    angle = -2.0 * np.pi * (np.outer(index, index) % length) / length
    cosine, sine = np.cos(angle) / np.sqrt(length), np.sin(angle) / np.sqrt(length)
    right = np.block([[cosine, sine], [-sine, cosine]])
    return np.stack([right, right.T]).astype(np.float32)


def split(value):
    high = value.astype(jnp.bfloat16)
    low = (value - high.astype(F32)).astype(jnp.bfloat16)
    return high, low


def dot(a, b):
    return jnp.dot(a, b, preferred_element_type=F32)


def times_table(value, high, low):
    big, small = split(value)
    return dot(jnp.concatenate([big, small, big], axis=1), jnp.concatenate([high, high, low], axis=0))


def table_times(high, low, value):
    big, small = split(value)
    return dot(jnp.concatenate([high, high, low], axis=1), jnp.concatenate([big, small, big], axis=0))


def folded(tall, low_lanes):
    half = tall.shape[0] // 2
    lane = lax.broadcasted_iota(jnp.int32, (half, LANES), 1)
    here = (lane < LANES // 2) == low_lanes
    return jnp.where(here, tall[:half], pltpu.roll(tall[half:], LANES // 2, axis=1))


def parities():
    return lax.axis_index("trow") % 2, lax.axis_index("tcol") % 2


def place_of(odd, low, high):
    near = pl.multiple_of(jnp.where(odd == 1, low, high), 8)
    far = pl.multiple_of(jnp.where(odd == 1, high, low), 8)
    return near, far


def edge_kernel(centre_ref, near_out, far_out, sem):
    margin = near_out.shape[1]
    odd_row, _ = parities()
    near, far = place_of(odd_row, 0, centre_ref.shape[1] - margin)
    copies = [
        pltpu.make_async_copy(centre_ref.at[:, pl.ds(far, margin)], far_out, sem.at[0]),
        pltpu.make_async_copy(centre_ref.at[:, pl.ds(near, margin)], near_out, sem.at[1]),
    ]
    for copy in copies:
        copy.start()
    for copy in copies:
        copy.wait()


def edge_call(centre, margin):
    edge = near((2, margin, centre.shape[2]))
    return pl.pallas_call(
        edge_kernel,
        out_shape=(edge, edge),
        in_specs=[HBM],
        out_specs=(VMEM,) * 2,
        scratch_shapes=[pltpu.SemaphoreType.DMA((2,))],
        compiler_params=PARAMS,
        name="edge_rows",
    )(*in_hbm(centre))


def ready_kernel(
    rows_ref, cols_ref, count_ref, probe_ref, measured_ref, table_ref, centre_ref, plan, turned, measured, tables, window,
    row_list, col_list, probe, table, sem,
):
    slots = measured.shape[0]
    margin = probe.shape[1] // 2
    height, width = centre_ref.shape[1:]
    columns = window.shape[0] // 2
    inner_columns = width - probe.shape[2]
    copies = [(rows_ref, row_list), (cols_ref, col_list), (probe_ref, probe), (table_ref, table)]
    for plane in range(2):
        for tile in range(columns - 2):
            lanes = slice(tile * LANES, (tile + 1) * LANES)
            copies.append((centre_ref.at[plane, :, lanes], window.at[plane * columns + 1 + tile, pl.ds(margin, height)]))
    copies.append((measured_ref, measured))
    copies = [pltpu.make_async_copy(a, b, sem.at[i]) for i, (a, b) in enumerate(copies)]
    for copy in copies:
        copy.start()
    for copy in copies[:3]:
        copy.wait()
    count = count_ref[0, 0]
    inner = jnp.int32(0)
    for slot in range(slots):
        first = col_list[slot]
        live = slot < count
        is_inner = jnp.logical_and(jnp.logical_and(first >= 0, first <= inner_columns), live)
        at = jnp.where(is_inner, inner, slots - 1 - (slot - inner))
        plan[jnp.where(live, at, 5 * slots + 1)] = slot
        inner = inner + is_inner.astype(jnp.int32)
        col = first + LANES
        turn = col & (LANES - 1)
        place = slots + 2 + 3 * slot
        plan[place] = row_list[slot] + margin
        plan[place + 1] = lax.shift_right_logical(col, 7)
        plan[place + 2] = turn
        for plane in range(2):
            turned[slot, plane] = pltpu.roll(probe[plane], turn, axis=1)
    plan[slots] = inner
    plan[slots + 1] = count
    copies[3].wait()
    for index in range(2):
        tables[2 * index], tables[2 * index + 1] = split(table[index])
    for copy in copies[4:]:
        copy.wait()


def ready_call(rows, cols, count, probe, measured, table, centre):
    slots = measured.shape[0]
    height, width = centre.shape[1:]
    tiles = width // LANES
    return pl.pallas_call(
        ready_kernel,
        out_shape=(
            pltpu.SMEM((5 * slots + 2,), jnp.int32),
            near((slots,) + probe.shape),
            near(measured.shape, measured.dtype),
            near((4,) + table.shape[1:], jnp.bfloat16),
            near((2 * (tiles + 2), height + probe.shape[1], LANES)),
        ),
        in_specs=[HBM] * 2 + [VMEM] + [HBM] * 4,
        out_specs=(SMEM,) + (VMEM,) * 4,
        scratch_shapes=[
            pltpu.SMEM(rows.shape, jnp.int32),
            pltpu.SMEM(cols.shape, jnp.int32),
            pltpu.VMEM(probe.shape, F32),
            pltpu.VMEM(table.shape, F32),
            pltpu.SemaphoreType.DMA((5 + 2 * tiles,)),
        ],
        compiler_params=PARAMS,
        name="ready",
    )(*in_hbm(rows, cols), *in_vmem(jnp.broadcast_to(count, (8, LANES))), *in_hbm(probe, measured, table, centre))


def side_kernel(tile_ref, near_ref, far_ref, window, near_out, far_out):
    margin = near_ref.shape[1]
    columns = window.shape[0] // 2
    odd_row, odd_col = parities()
    bottom = window.shape[1] - margin
    near, far = place_of(odd_row, 0, bottom)
    for plane in range(2):
        for tile in range(columns - 2):
            lanes = slice(tile * LANES, (tile + 1) * LANES)
            window[plane * columns + 1 + tile, margin:bottom] = tile_ref[plane * columns + 1 + tile, margin:bottom]
            window[plane * columns + 1 + tile, pl.ds(near, margin), :] = near_ref[plane, :, lanes]
            window[plane * columns + 1 + tile, pl.ds(far, margin), :] = far_ref[plane, :, lanes]
    for plane in range(2):
        near_tile = plane * columns + jnp.where(odd_col == 1, 1, columns - 2)
        far_tile = plane * columns + jnp.where(odd_col == 1, columns - 2, 1)
        near_out[plane] = folded(window[near_tile], odd_col == 1)
        far_out[plane] = folded(window[far_tile], odd_col == 0)


def side_call(window, near_row, far_row):
    shape = near((2, window.shape[1] // 2, LANES))
    return pl.pallas_call(
        side_kernel,
        out_shape=(near(window.shape), shape, shape),
        in_specs=[VMEM] * 3,
        out_specs=(VMEM,) * 3,
        compiler_params=PARAMS,
        name="side_columns",
    )(*in_vmem(window, near_row, far_row))


def finder(plan, slots, start, inner, live):
    def find(index):
        at = jnp.where(index < inner, start + index, jnp.maximum(slots - 1 - (index - inner), 0))
        is_live = index < live
        slot = plan[jnp.where(is_live, at, jnp.where(inner > 0, start, slots - 1))]
        place = slots + 2 + 3 * slot
        scale = jnp.where(is_live, 2.0, 0.0).astype(F32)
        return slot, plan[place], plan[place + 1], plan[place + 2], scale, jnp.where(is_live, slot, slots)

    return find


def run_slots(groups, find, window, turned, measured, table, exits, probe_sum):
    size = turned.shape[2]
    columns = window.shape[0] // 2
    lane = lax.broadcasted_iota(jnp.int32, (size, LANES), 1)
    exits[exits.shape[0] - 1] = jnp.zeros(exits.shape[1:], F32)

    def load(pair):
        kept, waves = [], []
        for slot, row, tile, turn, _, _ in pair:
            here = lane >= turn
            patch = [
                jnp.where(
                    here,
                    window[plane * columns + tile, pl.ds(row, size), :],
                    window[plane * columns + tile + 1, pl.ds(row, size), :],
                )
                for plane in range(2)
            ]
            probe = [turned[slot, plane] for plane in range(2)]
            wave_real = probe[0] * patch[0] - probe[1] * patch[1]
            wave_imag = probe[0] * patch[1] + probe[1] * patch[0]
            kept.append(patch)
            waves.append(jnp.concatenate([wave_real, wave_imag], axis=1))
        return kept, jnp.concatenate(waves, axis=0)

    def regroup(pair):
        return jnp.concatenate(
            [
                jnp.concatenate([pair[:size, :size], pair[size:, :size]], axis=1),
                jnp.concatenate([pair[:size, size:], pair[size:, size:]], axis=1),
            ],
            axis=0,
        )

    def weigh(pair, psi):
        real, imag = psi[:size], psi[size:]
        weights = []
        for member, (slot, _, _, _, scale, _) in enumerate(pair):
            lanes = slice(member * size, (member + 1) * size)
            power = real[:, lanes] * real[:, lanes] + imag[:, lanes] * imag[:, lanes]
            weights.append((power - measured[slot].astype(F32)) * scale)
        weight = jnp.concatenate(weights, axis=1)
        return jnp.concatenate([weight * real, weight * imag], axis=0)

    def add_up(pair, kept, pair_exits):
        for member, (_, _, _, turn, _, kept_at) in enumerate(pair):
            patch = kept[member]
            exit_real = pair_exits[member * size : (member + 1) * size, :size]
            exit_imag = pair_exits[member * size : (member + 1) * size, size:]
            exits[kept_at, 0] = exit_real
            exits[kept_at, 1] = exit_imag
            terms = (patch[0] * exit_real + patch[1] * exit_imag, patch[0] * exit_imag - patch[1] * exit_real)
            back = (LANES - turn) & (LANES - 1)
            for plane in range(2):
                probe_sum[plane] += pltpu.roll(terms[plane], back, axis=1)

    def step(group, carry):
        slots = [find(group * GROUP + member) for member in range(GROUP)]
        pairs = [slots[member : member + 2] for member in range(0, GROUP, 2)]
        loaded = [load(pair) for pair in pairs]
        waves = [regroup(times_table(wave, table[0], table[1])) for _, wave in loaded]
        waves = [weigh(pair, table_times(table[2], table[3], wave)) for pair, wave in zip(pairs, waves)]
        waves = [regroup(table_times(table[0], table[1], wave)) for wave in waves]
        waves = [times_table(wave, table[2], table[3]) for wave in waves]
        for pair, (kept, _), wave in zip(pairs, loaded, waves):
            add_up(pair, kept, wave)
        return carry

    lax.fori_loop(0, groups, step, 0)


def inner_kernel(plan, window, turned, measured, table, exits, probe_sum):
    slots = measured.shape[0]
    probe_sum[...] = jnp.zeros_like(probe_sum)
    groups = plan[slots] // GROUP
    find = finder(plan, slots, 0, groups * GROUP, groups * GROUP)
    run_slots(groups, find, window, turned, measured, table, exits, probe_sum)


def inner_call(plan, window, turned, measured, tables):
    slots = measured.shape[0]
    return pl.pallas_call(
        inner_kernel,
        out_shape=(near((slots + 1,) + turned.shape[1:]), near(turned.shape[1:])),
        in_specs=[SMEM] + [VMEM] * 4,
        out_specs=(VMEM,) * 2,
        compiler_params=PARAMS,
        cost_estimate=pl.CostEstimate(flops=10**10, bytes_accessed=2 * 10**7, transcendentals=0),
        name="slots_inside",
    )(*in_smem(plan), *in_vmem(window, turned, measured, tables))


def outer_kernel(
    plan, window_ref, near_col_ref, far_col_ref, turned, measured, table, probe_ref,
    exits, mine_out, other_out, window, probe_sum,
):
    slots = measured.shape[0]
    margin = turned.shape[2] // 2
    columns = window.shape[0] // 2
    half = window.shape[1] // 2
    odd_row, odd_col = parities()
    probe_sum[...] = probe_ref[...]
    for plane in range(2):
        own = slice(plane * columns + 1, (plane + 1) * columns - 1)
        window[own] = window_ref[own]
        near_tile = plane * columns + jnp.where(odd_col == 1, 0, columns - 1)
        far_tile = plane * columns + jnp.where(odd_col == 1, columns - 1, 0)
        for tile, ref in ((near_tile, near_col_ref), (far_tile, far_col_ref)):
            window[tile, :half] = ref[plane]
            window[tile, half:] = pltpu.roll(ref[plane], margin, axis=1)
    start = plan[slots] // GROUP * GROUP
    live = plan[slots + 1] - start
    find = finder(plan, slots, start, plan[slots] - start, live)
    run_slots((live + GROUP - 1) // GROUP, find, window, turned, measured, table, exits, probe_sum)
    factor = 1.0 / np.sqrt(np.float32(lax.axis_size("trow") * lax.axis_size("tcol") * slots))
    mine_out[...] = probe_sum[odd_row] * factor
    other_out[...] = probe_sum[1 - odd_row] * factor


def outer_call(plan, window, near_col, far_col, turned, measured, tables, probe_sum):
    slots = measured.shape[0]
    part = near(probe_sum.shape[1:])
    return pl.pallas_call(
        outer_kernel,
        out_shape=(near((slots + 1,) + turned.shape[1:]), part, part),
        in_specs=[SMEM] + [VMEM] * 7,
        out_specs=(VMEM,) * 3,
        scratch_shapes=[pltpu.VMEM(window.shape, F32), pltpu.VMEM(probe_sum.shape, F32)],
        compiler_params=PARAMS,
        cost_estimate=pl.CostEstimate(flops=10**10, bytes_accessed=2 * 10**7, transcendentals=0),
        name="slots_across",
    )(*in_smem(plan), *in_vmem(window, near_col, far_col, turned, measured, tables, probe_sum))


def object_kernel(plan, turned, inner_exits, outer_exits, grad, near_row_out, far_row_out, side_out):
    slots = turned.shape[0]
    size = turned.shape[2]
    margin = size // 2
    columns = grad.shape[0] // 2
    tall = grad.shape[1]
    odd_row, _ = parities()
    near, far = place_of(odd_row, 0, tall - margin)
    lane = lax.broadcasted_iota(jnp.int32, (size, LANES), 1)
    grad[...] = jnp.zeros_like(grad)

    def add_some(find, exits):
        def step(index, carry):
            for member in range(ADDED):
                slot, row, tile, turn, _, kept_at = find(index * ADDED + member)
                here = lane >= turn
                probe = [turned[slot, plane] for plane in range(2)]
                exit_real, exit_imag = exits[kept_at, 0], exits[kept_at, 1]
                adds = (probe[0] * exit_real + probe[1] * exit_imag, probe[0] * exit_imag - probe[1] * exit_real)
                for plane in range(2):
                    at = plane * columns + tile
                    grad[at, pl.ds(row, size), :] += jnp.where(here, adds[plane], 0.0)
                    grad[at + 1, pl.ds(row, size), :] += jnp.where(here, 0.0, adds[plane])
            return carry

        return step

    start = plan[slots] // GROUP * GROUP
    live = plan[slots + 1] - start
    lax.fori_loop(0, start // ADDED, add_some(finder(plan, slots, 0, start, start), inner_exits), 0)
    lax.fori_loop(
        0, (live + ADDED - 1) // ADDED, add_some(finder(plan, slots, start, plan[slots] - start, live), outer_exits), 0
    )
    narrow = lax.broadcasted_iota(jnp.int32, (margin, LANES), 1) < margin
    for plane in range(2):
        base = plane * columns
        left, right = base, base + columns - 1
        for at, out in ((near, near_row_out), (far, far_row_out)):
            rows = pl.ds(at, margin)
            for tile in range(columns - 2):
                out[plane, :, tile * LANES : (tile + 1) * LANES] = grad[base + 1 + tile, rows, :]
            out[plane, :, (columns - 2) * LANES :] = jnp.where(narrow, grad[right, rows, :], grad[left, rows, :])
        for row in range(margin, tall - margin, margin):
            rows = slice(row, row + margin)
            side_out[plane, row - margin : row] = jnp.where(narrow, grad[right, rows, :], grad[left, rows, :])


def object_call(plan, window, turned, inner_exits, outer_exits):
    size = turned.shape[2]
    row = near((2, size // 2, (window.shape[0] // 2 - 1) * LANES))
    return pl.pallas_call(
        object_kernel,
        out_shape=(near(window.shape), row, row, near((2, window.shape[1] - size, LANES))),
        in_specs=[SMEM] + [VMEM] * 3,
        out_specs=(VMEM,) * 4,
        compiler_params=PARAMS,
        cost_estimate=pl.CostEstimate(flops=2 * 10**9, bytes_accessed=10**6, transcendentals=0),
        name="object_sums",
    )(*in_smem(plan), *in_vmem(turned, inner_exits, outer_exits))


def side_sum_kernel(side_ref, near_ref, far_ref, near_out, far_out, side):
    margin = near_ref.shape[1]
    height = side_ref.shape[1]
    odd_row, odd_col = parities()
    near_at, far_at = place_of(odd_row, 0, height - margin)
    wide = near_ref.shape[2]
    side[...] = side_ref[...]
    for plane in range(2):
        side[plane, pl.ds(near_at, margin), :] += near_ref[plane, :, wide - LANES :]
        side[plane, pl.ds(far_at, margin), :] += far_ref[plane, :, wide - LANES :]
    for plane in range(2):
        near_out[plane] = folded(side[plane], odd_col == 0)
        far_out[plane] = folded(side[plane], odd_col == 1)


def side_sum_call(side, near_row, far_row):
    shape = near((2, side.shape[1] // 2, LANES))
    return pl.pallas_call(
        side_sum_kernel,
        out_shape=(shape, shape),
        in_specs=[VMEM] * 3,
        out_specs=(VMEM, VMEM),
        scratch_shapes=[pltpu.VMEM(side.shape, F32)],
        compiler_params=PARAMS,
        name="side_sums",
    )(*in_vmem(side, near_row, far_row))


def final_kernel(grad, near_row_ref, far_row_ref, near_col_ref, far_col_ref, out_ref):
    height, width = out_ref.shape[1:]
    columns = grad.shape[0] // 2
    margin = near_row_ref.shape[1]
    half = height // 2
    odd_row, odd_col = parities()
    near_at, far_at = place_of(odd_row, 0, height - margin)
    narrow = lax.broadcasted_iota(jnp.int32, (half, LANES), 1) < LANES // 2
    for plane in range(2):
        for tile in range(columns - 2):
            lanes = slice(tile * LANES, (tile + 1) * LANES)
            out_ref[plane, :, lanes] = grad[plane * columns + 1 + tile, margin : margin + height]
        near = jnp.where(odd_col == 1, near_col_ref[plane], far_col_ref[plane])
        far = jnp.where(odd_col == 1, far_col_ref[plane], near_col_ref[plane])
        for first, left, right in (
            (0, near, far),
            (half, pltpu.roll(near, LANES // 2, axis=1), pltpu.roll(far, LANES // 2, axis=1)),
        ):
            rows = slice(first, first + half)
            out_ref[plane, rows, :LANES] += jnp.where(narrow, left, 0.0)
            out_ref[plane, rows, width - LANES :] += jnp.where(narrow, 0.0, right)
        out_ref[plane, pl.ds(near_at, margin), :] += near_row_ref[plane, :, :width]
        out_ref[plane, pl.ds(far_at, margin), :] += far_row_ref[plane, :, :width]


def final_call(grad, near_row, far_row, near_col, far_col):
    margin = near_row.shape[1]
    shape = (2, grad.shape[1] - 2 * margin, near_row.shape[2] - LANES)
    return pl.pallas_call(
        final_kernel,
        out_shape=jax.ShapeDtypeStruct(shape, F32),
        in_specs=[VMEM] * 5,
        out_specs=VMEM,
        compiler_params=PARAMS,
        name="final_sums",
    )(*in_vmem(grad, near_row, far_row, near_col, far_col))


def near_swap(value, axis):
    return lax.ppermute(value, axis, [(i, i ^ 1) for i in range(lax.axis_size(axis))])


def far_swap(value, axis):
    pairs = [(i, i + 1) for i in range(1, lax.axis_size(axis) - 1, 2)]
    return lax.ppermute(value, axis, pairs + [(j, i) for i, j in pairs])


def doubling_steps(n_row, n_col):
    along_cols = [(0, 1)] + [(0, 1 << k) for k in range(1, n_col.bit_length() - 1)][::-1]
    along_rows = [(1 << k, 0) for k in range(1, n_row.bit_length() - 1)]
    return along_rows, along_cols


def add_kernel(a_ref, b_ref, out_ref):
    out_ref[...] = a_ref[...] + b_ref[...]


def add_call(a, b):
    return pl.pallas_call(
        add_kernel,
        out_shape=near(a.shape),
        in_specs=[VMEM] * 2,
        out_specs=VMEM,
        compiler_params=PARAMS,
        cost_estimate=pl.CostEstimate(flops=10**9, bytes_accessed=10**5, transcendentals=0),
        name="add",
    )(*in_vmem(a, b))


def add_partner(mine, step, add=jnp.add):
    n_row, n_col = lax.axis_size("trow"), lax.axis_size("tcol")
    pairs = [(r * n_col + c, (r ^ step[0]) * n_col + (c ^ step[1])) for r in range(n_row) for c in range(n_col)]
    return add(mine, lax.ppermute(mine, ("trow", "tcol"), pairs))


def body(table, object_planes, probe, intensities, row_offsets, col_offsets, counts):
    size = probe.shape[1]
    rows, cols = row_offsets.reshape(-1), col_offsets.reshape(-1)
    measured = intensities.reshape(-1, size, size)
    near_row, far_row = edge_call(object_planes, size // 2)
    far_row = far_swap(far_row, "trow")
    near_row = near_swap(near_row, "trow")
    plan, turned, measured, tables, window = ready_call(rows, cols, counts, probe, measured, table, object_planes)
    window, near_side, far_side = side_call(window, near_row, far_row)
    far_col = far_swap(far_side, "tcol")
    near_col = near_swap(near_side, "tcol")
    inner_exits, probe_sum = inner_call(plan, window, turned, measured, tables)
    outer_exits, mine, other = outer_call(plan, window, near_col, far_col, turned, measured, tables, probe_sum)

    along_rows, along_cols = doubling_steps(lax.axis_size("trow"), lax.axis_size("tcol"))
    mine = mine + near_swap(other, "trow")
    mine, outer_exits = lax.optimization_barrier((mine, outer_exits))
    grad, near_row, far_row, side = object_call(plan, window, turned, inner_exits, outer_exits)
    near_row = near_swap(near_row, "trow")
    far_row = far_swap(far_row, "trow")
    mine = add_partner(mine, along_cols[0])
    mine = add_partner(mine, along_cols[1], add=add_call)
    near_side, far_side = side_sum_call(side, near_row, far_row)
    mine, near_side, far_side = lax.optimization_barrier((mine, near_side, far_side))
    near_col = near_swap(near_side, "tcol")
    far_col = far_swap(far_side, "tcol")
    for step in along_cols[2:] + along_rows:
        mine = add_partner(mine, step)
    mine, near_col, far_col = lax.optimization_barrier((mine, near_col, far_col))
    object_grad = final_call(grad, near_row, far_row, near_col, far_col)
    other = near_swap(mine, "trow")
    odd_row, _ = parities()
    probe_grad = jnp.where(odd_row == 0, jnp.stack([mine, other]), jnp.stack([other, mine]))
    return (object_grad, probe_grad)


def solution(mesh):
    table = dft_tables(LANES)
    inner = jax.shard_map(
        body,
        mesh=mesh,
        in_specs=(
            P(),
            P(None, "trow", "tcol"),
            P(),
            P("trow", "tcol", None, None, None),
            P("trow", "tcol", None),
            P("trow", "tcol", None),
            P(("trow", "tcol")),
        ),
        out_specs=(P(None, "trow", "tcol"), P()),
        check_vma=False,
    )

    def run(*args):
        return inner(jnp.asarray(table), *args)

    return run
```

```python
import jax
import jax.numpy as jnp
import numpy as np
from jax import lax
from jax.experimental import pallas as pl
from jax.experimental.pallas import tpu as pltpu
from jax.sharding import PartitionSpec as P

LANES = 128
VMEM_BYTES = 24 * 1024 * 1024
GROUP = 8
ADDED = 4
F32 = jnp.float32
HBM = pl.BlockSpec(memory_space=pltpu.HBM)
VMEM = pl.BlockSpec(memory_space=pltpu.VMEM)
SMEM = pl.BlockSpec(memory_space=pltpu.SMEM)
PARAMS = pltpu.CompilerParams(vmem_limit_bytes=VMEM_BYTES)


def in_hbm(*arrays):
    return [pltpu.with_memory_space_constraint(array, pltpu.HBM) for array in arrays]


def in_vmem(*arrays):
    return [pltpu.with_memory_space_constraint(array, pltpu.VMEM) for array in arrays]


def in_smem(*arrays):
    return [pltpu.with_memory_space_constraint(array, pltpu.SMEM) for array in arrays]


def near(shape, dtype=F32):
    return pltpu.VMEM(tuple(shape), dtype)


def dft_tables(length):
    index = np.arange(length)
    angle = -2.0 * np.pi * (np.outer(index, index) % length) / length
    cosine, sine = np.cos(angle) / np.sqrt(length), np.sin(angle) / np.sqrt(length)
    right = np.block([[cosine, sine], [-sine, cosine]])
    return np.stack([right, right.T]).astype(np.float32)


def split(value):
    high = value.astype(jnp.bfloat16)
    low = (value - high.astype(F32)).astype(jnp.bfloat16)
    return high, low


def dot(a, b):
    return jnp.dot(a, b, preferred_element_type=F32)


def times_table(value, high, low):
    big, small = split(value)
    return dot(jnp.concatenate([big, small, big], axis=1), jnp.concatenate([high, high, low], axis=0))


def table_times(high, low, value):
    big, small = split(value)
    return dot(jnp.concatenate([high, high, low], axis=1), jnp.concatenate([big, small, big], axis=0))


def folded(tall, low_lanes):
    half = tall.shape[0] // 2
    lane = lax.broadcasted_iota(jnp.int32, (half, LANES), 1)
    here = (lane < LANES // 2) == low_lanes
    return jnp.where(here, tall[:half], pltpu.roll(tall[half:], LANES // 2, axis=1))


def parities():
    return lax.axis_index("trow") % 2, lax.axis_index("tcol") % 2


def place_of(odd, low, high):
    near = pl.multiple_of(jnp.where(odd == 1, low, high), 8)
    far = pl.multiple_of(jnp.where(odd == 1, high, low), 8)
    return near, far


def edge_kernel(centre_ref, near_out, far_out, sem):
    margin = near_out.shape[1]
    odd_row, _ = parities()
    near, far = place_of(odd_row, 0, centre_ref.shape[1] - margin)
    copies = [
        pltpu.make_async_copy(centre_ref.at[:, pl.ds(far, margin)], far_out, sem.at[0]),
        pltpu.make_async_copy(centre_ref.at[:, pl.ds(near, margin)], near_out, sem.at[1]),
    ]
    for copy in copies:
        copy.start()
    for copy in copies:
        copy.wait()


def edge_call(centre, margin):
    edge = near((2, margin, centre.shape[2]))
    return pl.pallas_call(
        edge_kernel,
        out_shape=(edge, edge),
        in_specs=[HBM],
        out_specs=(VMEM,) * 2,
        scratch_shapes=[pltpu.SemaphoreType.DMA((2,))],
        compiler_params=PARAMS,
        name="edge_rows",
    )(*in_hbm(centre))


def ready_kernel(
    rows_ref, cols_ref, count_ref, probe_ref, measured_ref, table_ref, centre_ref, plan, turned, measured, tables, window,
    row_list, col_list, probe, table, sem,
):
    slots = measured.shape[0]
    margin = probe.shape[1] // 2
    height, width = centre_ref.shape[1:]
    columns = window.shape[0] // 2
    inner_columns = width - probe.shape[2]
    copies = [(rows_ref, row_list), (cols_ref, col_list), (probe_ref, probe), (table_ref, table)]
    for plane in range(2):
        for tile in range(columns - 2):
            lanes = slice(tile * LANES, (tile + 1) * LANES)
            copies.append((centre_ref.at[plane, :, lanes], window.at[plane * columns + 1 + tile, pl.ds(margin, height)]))
    copies.append((measured_ref, measured))
    copies = [pltpu.make_async_copy(a, b, sem.at[i]) for i, (a, b) in enumerate(copies)]
    for copy in copies:
        copy.start()
    for copy in copies[:3]:
        copy.wait()
    count = count_ref[0, 0]
    inner = jnp.int32(0)
    for slot in range(slots):
        first = col_list[slot]
        live = slot < count
        is_inner = jnp.logical_and(jnp.logical_and(first >= 0, first <= inner_columns), live)
        at = jnp.where(is_inner, inner, slots - 1 - (slot - inner))
        plan[jnp.where(live, at, 5 * slots + 1)] = slot
        inner = inner + is_inner.astype(jnp.int32)
        col = first + LANES
        turn = col & (LANES - 1)
        place = slots + 2 + 3 * slot
        plan[place] = row_list[slot] + margin
        plan[place + 1] = lax.shift_right_logical(col, 7)
        plan[place + 2] = turn
        for plane in range(2):
            turned[slot, plane] = pltpu.roll(probe[plane], turn, axis=1)
    plan[slots] = inner
    plan[slots + 1] = count
    copies[3].wait()
    for index in range(2):
        tables[2 * index], tables[2 * index + 1] = split(table[index])
    for copy in copies[4:]:
        copy.wait()


def ready_call(rows, cols, count, probe, measured, table, centre):
    slots = measured.shape[0]
    height, width = centre.shape[1:]
    tiles = width // LANES
    return pl.pallas_call(
        ready_kernel,
        out_shape=(
            pltpu.SMEM((5 * slots + 2,), jnp.int32),
            near((slots,) + probe.shape),
            near(measured.shape, measured.dtype),
            near((4,) + table.shape[1:], jnp.bfloat16),
            near((2 * (tiles + 2), height + probe.shape[1], LANES)),
        ),
        in_specs=[HBM] * 2 + [VMEM] + [HBM] * 4,
        out_specs=(SMEM,) + (VMEM,) * 4,
        scratch_shapes=[
            pltpu.SMEM(rows.shape, jnp.int32),
            pltpu.SMEM(cols.shape, jnp.int32),
            pltpu.VMEM(probe.shape, F32),
            pltpu.VMEM(table.shape, F32),
            pltpu.SemaphoreType.DMA((5 + 2 * tiles,)),
        ],
        compiler_params=PARAMS,
        name="ready",
    )(*in_hbm(rows, cols), *in_vmem(jnp.broadcast_to(count, (8, LANES))), *in_hbm(probe, measured, table, centre))


def side_kernel(tile_ref, near_ref, far_ref, window, near_out, far_out):
    margin = near_ref.shape[1]
    columns = window.shape[0] // 2
    odd_row, odd_col = parities()
    bottom = window.shape[1] - margin
    near, far = place_of(odd_row, 0, bottom)
    for plane in range(2):
        for tile in range(columns - 2):
            lanes = slice(tile * LANES, (tile + 1) * LANES)
            window[plane * columns + 1 + tile, margin:bottom] = tile_ref[plane * columns + 1 + tile, margin:bottom]
            window[plane * columns + 1 + tile, pl.ds(near, margin), :] = near_ref[plane, :, lanes]
            window[plane * columns + 1 + tile, pl.ds(far, margin), :] = far_ref[plane, :, lanes]
    for plane in range(2):
        near_tile = plane * columns + jnp.where(odd_col == 1, 1, columns - 2)
        far_tile = plane * columns + jnp.where(odd_col == 1, columns - 2, 1)
        near_out[plane] = folded(window[near_tile], odd_col == 1)
        far_out[plane] = folded(window[far_tile], odd_col == 0)


def side_call(window, near_row, far_row):
    shape = near((2, window.shape[1] // 2, LANES))
    return pl.pallas_call(
        side_kernel,
        out_shape=(near(window.shape), shape, shape),
        in_specs=[VMEM] * 3,
        out_specs=(VMEM,) * 3,
        compiler_params=PARAMS,
        name="side_columns",
    )(*in_vmem(window, near_row, far_row))


def finder(plan, slots, start, inner, live):
    def find(index):
        at = jnp.where(index < inner, start + index, jnp.maximum(slots - 1 - (index - inner), 0))
        is_live = index < live
        slot = plan[jnp.where(is_live, at, jnp.where(inner > 0, start, slots - 1))]
        place = slots + 2 + 3 * slot
        scale = jnp.where(is_live, 2.0, 0.0).astype(F32)
        return slot, plan[place], plan[place + 1], plan[place + 2], scale, jnp.where(is_live, slot, slots)

    return find


def run_slots(groups, size_of, first, find, window, turned, measured, table, exits, probe_sum):
    size = turned.shape[2]
    columns = window.shape[0] // 2
    lane = lax.broadcasted_iota(jnp.int32, (size, LANES), 1)
    exits[exits.shape[0] - 1] = jnp.zeros(exits.shape[1:], F32)

    def load(pair):
        kept, waves = [], []
        for slot, row, tile, turn, _, _ in pair:
            here = lane >= turn
            patch = [
                jnp.where(
                    here,
                    window[plane * columns + tile, pl.ds(row, size), :],
                    window[plane * columns + tile + 1, pl.ds(row, size), :],
                )
                for plane in range(2)
            ]
            probe = [turned[slot, plane] for plane in range(2)]
            wave_real = probe[0] * patch[0] - probe[1] * patch[1]
            wave_imag = probe[0] * patch[1] + probe[1] * patch[0]
            kept.append(patch)
            waves.append(jnp.concatenate([wave_real, wave_imag], axis=1))
        return kept, jnp.concatenate(waves, axis=0)

    def regroup(pair):
        return jnp.concatenate(
            [
                jnp.concatenate([pair[:size, :size], pair[size:, :size]], axis=1),
                jnp.concatenate([pair[:size, size:], pair[size:, size:]], axis=1),
            ],
            axis=0,
        )

    def weigh(pair, psi):
        real, imag = psi[:size], psi[size:]
        weights = []
        for member, (slot, _, _, _, scale, _) in enumerate(pair):
            lanes = slice(member * size, (member + 1) * size)
            power = real[:, lanes] * real[:, lanes] + imag[:, lanes] * imag[:, lanes]
            weights.append((power - measured[slot].astype(F32)) * scale)
        weight = jnp.concatenate(weights, axis=1)
        return jnp.concatenate([weight * real, weight * imag], axis=0)

    def add_up(pair, kept, pair_exits):
        for member, (_, _, _, turn, _, kept_at) in enumerate(pair):
            patch = kept[member]
            exit_real = pair_exits[member * size : (member + 1) * size, :size]
            exit_imag = pair_exits[member * size : (member + 1) * size, size:]
            exits[kept_at, 0] = exit_real
            exits[kept_at, 1] = exit_imag
            terms = (patch[0] * exit_real + patch[1] * exit_imag, patch[0] * exit_imag - patch[1] * exit_real)
            back = (LANES - turn) & (LANES - 1)
            for plane in range(2):
                probe_sum[plane] += pltpu.roll(terms[plane], back, axis=1)

    def step(group, carry):
        slots = [find(first + group * size_of + member) for member in range(size_of)]
        pairs = [slots[member : member + 2] for member in range(0, size_of, 2)]
        loaded = [load(pair) for pair in pairs]
        waves = [regroup(times_table(wave, table[0], table[1])) for _, wave in loaded]
        waves = [weigh(pair, table_times(table[2], table[3], wave)) for pair, wave in zip(pairs, waves)]
        waves = [regroup(table_times(table[0], table[1], wave)) for wave in waves]
        waves = [times_table(wave, table[2], table[3]) for wave in waves]
        for pair, (kept, _), wave in zip(pairs, loaded, waves):
            add_up(pair, kept, wave)
        return carry

    lax.fori_loop(0, groups, step, 0)


def inner_kernel(plan, window, turned, measured, table, exits, probe_sum):
    slots = measured.shape[0]
    probe_sum[...] = jnp.zeros_like(probe_sum)
    groups = plan[slots] // GROUP
    find = finder(plan, slots, 0, groups * GROUP, groups * GROUP)
    run_slots(groups, GROUP, 0, find, window, turned, measured, table, exits, probe_sum)


def inner_call(plan, window, turned, measured, tables):
    slots = measured.shape[0]
    return pl.pallas_call(
        inner_kernel,
        out_shape=(near((slots + 1,) + turned.shape[1:]), near(turned.shape[1:])),
        in_specs=[SMEM] + [VMEM] * 4,
        out_specs=(VMEM,) * 2,
        compiler_params=PARAMS,
        cost_estimate=pl.CostEstimate(flops=10**10, bytes_accessed=2 * 10**7, transcendentals=0),
        name="slots_inside",
    )(*in_smem(plan), *in_vmem(window, turned, measured, tables))


def outer_kernel(
    plan, window_ref, near_col_ref, far_col_ref, turned, measured, table, probe_ref,
    exits, mine_out, other_out, window, probe_sum,
):
    slots = measured.shape[0]
    margin = turned.shape[2] // 2
    columns = window.shape[0] // 2
    half = window.shape[1] // 2
    odd_row, odd_col = parities()
    probe_sum[...] = probe_ref[...]
    for plane in range(2):
        own = slice(plane * columns + 1, (plane + 1) * columns - 1)
        window[own] = window_ref[own]
        near_tile = plane * columns + jnp.where(odd_col == 1, 0, columns - 1)
        far_tile = plane * columns + jnp.where(odd_col == 1, columns - 1, 0)
        for tile, ref in ((near_tile, near_col_ref), (far_tile, far_col_ref)):
            window[tile, :half] = ref[plane]
            window[tile, half:] = pltpu.roll(ref[plane], margin, axis=1)
    start = plan[slots] // GROUP * GROUP
    live = plan[slots + 1] - start
    find = finder(plan, slots, start, plan[slots] - start, live)
    large = live // (2 * GROUP)
    run_slots(large, 2 * GROUP, 0, find, window, turned, measured, table, exits, probe_sum)
    first = large * 2 * GROUP
    run_slots((live - first + GROUP - 1) // GROUP, GROUP, first, find, window, turned, measured, table, exits, probe_sum)
    factor = 1.0 / np.sqrt(np.float32(lax.axis_size("trow") * lax.axis_size("tcol") * slots))
    mine_out[...] = probe_sum[odd_row] * factor
    other_out[...] = probe_sum[1 - odd_row] * factor


def outer_call(plan, window, near_col, far_col, turned, measured, tables, probe_sum):
    slots = measured.shape[0]
    part = near(probe_sum.shape[1:])
    return pl.pallas_call(
        outer_kernel,
        out_shape=(near((slots + 1,) + turned.shape[1:]), part, part),
        in_specs=[SMEM] + [VMEM] * 7,
        out_specs=(VMEM,) * 3,
        scratch_shapes=[pltpu.VMEM(window.shape, F32), pltpu.VMEM(probe_sum.shape, F32)],
        compiler_params=PARAMS,
        cost_estimate=pl.CostEstimate(flops=10**10, bytes_accessed=2 * 10**7, transcendentals=0),
        name="slots_across",
    )(*in_smem(plan), *in_vmem(window, near_col, far_col, turned, measured, tables, probe_sum))


def object_kernel(plan, turned, inner_exits, outer_exits, grad, near_row_out, far_row_out, side_out):
    slots = turned.shape[0]
    size = turned.shape[2]
    margin = size // 2
    columns = grad.shape[0] // 2
    tall = grad.shape[1]
    odd_row, _ = parities()
    near, far = place_of(odd_row, 0, tall - margin)
    lane = lax.broadcasted_iota(jnp.int32, (size, LANES), 1)
    grad[...] = jnp.zeros_like(grad)

    def add_some(find, exits):
        def step(index, carry):
            for member in range(ADDED):
                slot, row, tile, turn, _, kept_at = find(index * ADDED + member)
                here = lane >= turn
                probe = [turned[slot, plane] for plane in range(2)]
                exit_real, exit_imag = exits[kept_at, 0], exits[kept_at, 1]
                adds = (probe[0] * exit_real + probe[1] * exit_imag, probe[0] * exit_imag - probe[1] * exit_real)
                for plane in range(2):
                    at = plane * columns + tile
                    grad[at, pl.ds(row, size), :] += jnp.where(here, adds[plane], 0.0)
                    grad[at + 1, pl.ds(row, size), :] += jnp.where(here, 0.0, adds[plane])
            return carry

        return step

    start = plan[slots] // GROUP * GROUP
    live = plan[slots + 1] - start
    lax.fori_loop(0, start // ADDED, add_some(finder(plan, slots, 0, start, start), inner_exits), 0)
    lax.fori_loop(
        0, (live + ADDED - 1) // ADDED, add_some(finder(plan, slots, start, plan[slots] - start, live), outer_exits), 0
    )
    narrow = lax.broadcasted_iota(jnp.int32, (margin, LANES), 1) < margin
    for plane in range(2):
        base = plane * columns
        left, right = base, base + columns - 1
        for at, out in ((near, near_row_out), (far, far_row_out)):
            rows = pl.ds(at, margin)
            for tile in range(columns - 2):
                out[plane, :, tile * LANES : (tile + 1) * LANES] = grad[base + 1 + tile, rows, :]
            out[plane, :, (columns - 2) * LANES :] = jnp.where(narrow, grad[right, rows, :], grad[left, rows, :])
        for row in range(margin, tall - margin, margin):
            rows = slice(row, row + margin)
            side_out[plane, row - margin : row] = jnp.where(narrow, grad[right, rows, :], grad[left, rows, :])


def object_call(plan, window, turned, inner_exits, outer_exits):
    size = turned.shape[2]
    row = near((2, size // 2, (window.shape[0] // 2 - 1) * LANES))
    return pl.pallas_call(
        object_kernel,
        out_shape=(near(window.shape), row, row, near((2, window.shape[1] - size, LANES))),
        in_specs=[SMEM] + [VMEM] * 3,
        out_specs=(VMEM,) * 4,
        compiler_params=PARAMS,
        cost_estimate=pl.CostEstimate(flops=2 * 10**9, bytes_accessed=10**6, transcendentals=0),
        name="object_sums",
    )(*in_smem(plan), *in_vmem(turned, inner_exits, outer_exits))


def side_sum_kernel(side_ref, near_ref, far_ref, near_out, far_out, side):
    margin = near_ref.shape[1]
    height = side_ref.shape[1]
    odd_row, odd_col = parities()
    near_at, far_at = place_of(odd_row, 0, height - margin)
    wide = near_ref.shape[2]
    side[...] = side_ref[...]
    for plane in range(2):
        side[plane, pl.ds(near_at, margin), :] += near_ref[plane, :, wide - LANES :]
        side[plane, pl.ds(far_at, margin), :] += far_ref[plane, :, wide - LANES :]
    for plane in range(2):
        near_out[plane] = folded(side[plane], odd_col == 0)
        far_out[plane] = folded(side[plane], odd_col == 1)


def side_sum_call(side, near_row, far_row):
    shape = near((2, side.shape[1] // 2, LANES))
    return pl.pallas_call(
        side_sum_kernel,
        out_shape=(shape, shape),
        in_specs=[VMEM] * 3,
        out_specs=(VMEM, VMEM),
        scratch_shapes=[pltpu.VMEM(side.shape, F32)],
        compiler_params=PARAMS,
        name="side_sums",
    )(*in_vmem(side, near_row, far_row))


def final_kernel(grad, near_row_ref, far_row_ref, near_col_ref, far_col_ref, out_ref):
    height, width = out_ref.shape[1:]
    columns = grad.shape[0] // 2
    margin = near_row_ref.shape[1]
    half = height // 2
    odd_row, odd_col = parities()
    near_at, far_at = place_of(odd_row, 0, height - margin)
    narrow = lax.broadcasted_iota(jnp.int32, (half, LANES), 1) < LANES // 2
    for plane in range(2):
        for tile in range(columns - 2):
            lanes = slice(tile * LANES, (tile + 1) * LANES)
            out_ref[plane, :, lanes] = grad[plane * columns + 1 + tile, margin : margin + height]
        near = jnp.where(odd_col == 1, near_col_ref[plane], far_col_ref[plane])
        far = jnp.where(odd_col == 1, far_col_ref[plane], near_col_ref[plane])
        for first, left, right in (
            (0, near, far),
            (half, pltpu.roll(near, LANES // 2, axis=1), pltpu.roll(far, LANES // 2, axis=1)),
        ):
            rows = slice(first, first + half)
            out_ref[plane, rows, :LANES] += jnp.where(narrow, left, 0.0)
            out_ref[plane, rows, width - LANES :] += jnp.where(narrow, 0.0, right)
        out_ref[plane, pl.ds(near_at, margin), :] += near_row_ref[plane, :, :width]
        out_ref[plane, pl.ds(far_at, margin), :] += far_row_ref[plane, :, :width]


def final_call(grad, near_row, far_row, near_col, far_col):
    margin = near_row.shape[1]
    shape = (2, grad.shape[1] - 2 * margin, near_row.shape[2] - LANES)
    return pl.pallas_call(
        final_kernel,
        out_shape=jax.ShapeDtypeStruct(shape, F32),
        in_specs=[VMEM] * 5,
        out_specs=VMEM,
        compiler_params=PARAMS,
        name="final_sums",
    )(*in_vmem(grad, near_row, far_row, near_col, far_col))


def near_swap(value, axis):
    return lax.ppermute(value, axis, [(i, i ^ 1) for i in range(lax.axis_size(axis))])


def far_swap(value, axis):
    pairs = [(i, i + 1) for i in range(1, lax.axis_size(axis) - 1, 2)]
    return lax.ppermute(value, axis, pairs + [(j, i) for i, j in pairs])


def doubling_steps(n_row, n_col):
    along_cols = [(0, 1)] + [(0, 1 << k) for k in range(1, n_col.bit_length() - 1)][::-1]
    along_rows = [(1 << k, 0) for k in range(1, n_row.bit_length() - 1)]
    return along_rows, along_cols


def add_kernel(a_ref, b_ref, out_ref):
    out_ref[...] = a_ref[...] + b_ref[...]


def add_call(a, b):
    return pl.pallas_call(
        add_kernel,
        out_shape=near(a.shape),
        in_specs=[VMEM] * 2,
        out_specs=VMEM,
        compiler_params=PARAMS,
        cost_estimate=pl.CostEstimate(flops=10**9, bytes_accessed=10**5, transcendentals=0),
        name="add",
    )(*in_vmem(a, b))


def add_partner(mine, step, add=jnp.add):
    n_row, n_col = lax.axis_size("trow"), lax.axis_size("tcol")
    pairs = [(r * n_col + c, (r ^ step[0]) * n_col + (c ^ step[1])) for r in range(n_row) for c in range(n_col)]
    return add(mine, lax.ppermute(mine, ("trow", "tcol"), pairs))


def body(table, object_planes, probe, intensities, row_offsets, col_offsets, counts):
    size = probe.shape[1]
    rows, cols = row_offsets.reshape(-1), col_offsets.reshape(-1)
    measured = intensities.reshape(-1, size, size)
    near_row, far_row = edge_call(object_planes, size // 2)
    far_row = far_swap(far_row, "trow")
    near_row = near_swap(near_row, "trow")
    plan, turned, measured, tables, window = ready_call(rows, cols, counts, probe, measured, table, object_planes)
    window, near_side, far_side = side_call(window, near_row, far_row)
    far_col = far_swap(far_side, "tcol")
    near_col = near_swap(near_side, "tcol")
    inner_exits, probe_sum = inner_call(plan, window, turned, measured, tables)
    outer_exits, mine, other = outer_call(plan, window, near_col, far_col, turned, measured, tables, probe_sum)

    along_rows, along_cols = doubling_steps(lax.axis_size("trow"), lax.axis_size("tcol"))
    mine = mine + near_swap(other, "trow")
    mine, outer_exits = lax.optimization_barrier((mine, outer_exits))
    grad, near_row, far_row, side = object_call(plan, window, turned, inner_exits, outer_exits)
    near_row = near_swap(near_row, "trow")
    far_row = far_swap(far_row, "trow")
    mine = add_partner(mine, along_cols[0])
    mine = add_partner(mine, along_cols[1], add=add_call)
    near_side, far_side = side_sum_call(side, near_row, far_row)
    mine, near_side, far_side = lax.optimization_barrier((mine, near_side, far_side))
    near_col = near_swap(near_side, "tcol")
    far_col = far_swap(far_side, "tcol")
    for step in along_cols[2:] + along_rows:
        mine = add_partner(mine, step)
    mine, near_col, far_col = lax.optimization_barrier((mine, near_col, far_col))
    object_grad = final_call(grad, near_row, far_row, near_col, far_col)
    other = near_swap(mine, "trow")
    odd_row, _ = parities()
    probe_grad = jnp.where(odd_row == 0, jnp.stack([mine, other]), jnp.stack([other, mine]))
    return (object_grad, probe_grad)


def solution(mesh):
    table = dft_tables(LANES)
    inner = jax.shard_map(
        body,
        mesh=mesh,
        in_specs=(
            P(),
            P(None, "trow", "tcol"),
            P(),
            P("trow", "tcol", None, None, None),
            P("trow", "tcol", None),
            P("trow", "tcol", None),
            P(("trow", "tcol")),
        ),
        out_specs=(P(None, "trow", "tcol"), P()),
        check_vma=False,
    )

    def run(*args):
        return inner(jnp.asarray(table), *args)

    return run
```

```python
import jax
import jax.numpy as jnp
import numpy as np
from jax import lax
from jax.experimental import pallas as pl
from jax.experimental.pallas import tpu as pltpu
from jax.sharding import PartitionSpec as P

LANES = 128
VMEM_BYTES = 24 * 1024 * 1024
GROUP = 8
ADDED = 4
F32 = jnp.float32
HBM = pl.BlockSpec(memory_space=pltpu.HBM)
VMEM = pl.BlockSpec(memory_space=pltpu.VMEM)
SMEM = pl.BlockSpec(memory_space=pltpu.SMEM)
PARAMS = pltpu.CompilerParams(vmem_limit_bytes=VMEM_BYTES)


def in_hbm(*arrays):
    return [pltpu.with_memory_space_constraint(array, pltpu.HBM) for array in arrays]


def in_vmem(*arrays):
    return [pltpu.with_memory_space_constraint(array, pltpu.VMEM) for array in arrays]


def in_smem(*arrays):
    return [pltpu.with_memory_space_constraint(array, pltpu.SMEM) for array in arrays]


def near(shape, dtype=F32):
    return pltpu.VMEM(tuple(shape), dtype)


def dft_tables(length):
    index = np.arange(length)
    angle = -2.0 * np.pi * (np.outer(index, index) % length) / length
    cosine, sine = np.cos(angle) / np.sqrt(length), np.sin(angle) / np.sqrt(length)
    right = np.block([[cosine, sine], [-sine, cosine]])
    return np.stack([right, right.T]).astype(np.float32)


def split(value):
    high = value.astype(jnp.bfloat16)
    low = (value - high.astype(F32)).astype(jnp.bfloat16)
    return high, low


def dot(a, b):
    return jnp.dot(a, b, preferred_element_type=F32)


def times_table(value, high, low):
    big, small = split(value)
    return dot(jnp.concatenate([big, small, big], axis=1), jnp.concatenate([high, high, low], axis=0))


def table_times(high, low, value):
    big, small = split(value)
    return dot(jnp.concatenate([high, high, low], axis=1), jnp.concatenate([big, small, big], axis=0))


def folded(tall, low_lanes):
    half = tall.shape[0] // 2
    lane = lax.broadcasted_iota(jnp.int32, (half, LANES), 1)
    here = (lane < LANES // 2) == low_lanes
    return jnp.where(here, tall[:half], pltpu.roll(tall[half:], LANES // 2, axis=1))


def parities():
    return lax.axis_index("trow") % 2, lax.axis_index("tcol") % 2


def place_of(odd, low, high):
    near = pl.multiple_of(jnp.where(odd == 1, low, high), 8)
    far = pl.multiple_of(jnp.where(odd == 1, high, low), 8)
    return near, far


def edge_kernel(centre_ref, near_out, far_out, sem):
    margin = near_out.shape[1]
    odd_row, _ = parities()
    near, far = place_of(odd_row, 0, centre_ref.shape[1] - margin)
    copies = [
        pltpu.make_async_copy(centre_ref.at[:, pl.ds(far, margin)], far_out, sem.at[0]),
        pltpu.make_async_copy(centre_ref.at[:, pl.ds(near, margin)], near_out, sem.at[1]),
    ]
    for copy in copies:
        copy.start()
    for copy in copies:
        copy.wait()


def edge_call(centre, margin):
    edge = near((2, margin, centre.shape[2]))
    return pl.pallas_call(
        edge_kernel,
        out_shape=(edge, edge),
        in_specs=[HBM],
        out_specs=(VMEM,) * 2,
        scratch_shapes=[pltpu.SemaphoreType.DMA((2,))],
        compiler_params=PARAMS,
        name="edge_rows",
    )(*in_hbm(centre))


def ready_kernel(
    rows_ref, cols_ref, count_ref, probe_ref, measured_ref, table_ref, centre_ref, plan, turned, measured, tables, window,
    row_list, col_list, probe, table, sem,
):
    slots = measured.shape[0]
    margin = probe.shape[1] // 2
    height, width = centre_ref.shape[1:]
    columns = window.shape[0] // 2
    inner_columns = width - probe.shape[2]
    copies = [(rows_ref, row_list), (cols_ref, col_list), (probe_ref, probe), (table_ref, table)]
    for plane in range(2):
        for tile in range(columns - 2):
            lanes = slice(tile * LANES, (tile + 1) * LANES)
            copies.append((centre_ref.at[plane, :, lanes], window.at[plane * columns + 1 + tile, pl.ds(margin, height)]))
    copies.append((measured_ref, measured))
    copies = [pltpu.make_async_copy(a, b, sem.at[i]) for i, (a, b) in enumerate(copies)]
    for copy in copies:
        copy.start()
    for copy in copies[:3]:
        copy.wait()
    count = count_ref[0, 0]
    inner = jnp.int32(0)
    for slot in range(slots):
        first = col_list[slot]
        live = slot < count
        is_inner = jnp.logical_and(jnp.logical_and(first >= 0, first <= inner_columns), live)
        at = jnp.where(is_inner, inner, slots - 1 - (slot - inner))
        plan[jnp.where(live, at, 5 * slots + 1)] = slot
        inner = inner + is_inner.astype(jnp.int32)
        col = first + LANES
        turn = col & (LANES - 1)
        place = slots + 2 + 3 * slot
        plan[place] = row_list[slot] + margin
        plan[place + 1] = lax.shift_right_logical(col, 7)
        plan[place + 2] = turn
        for plane in range(2):
            turned[slot, plane] = pltpu.roll(probe[plane], turn, axis=1)
    plan[slots] = inner
    plan[slots + 1] = count
    copies[3].wait()
    for index in range(2):
        tables[2 * index], tables[2 * index + 1] = split(table[index])
    for copy in copies[4:]:
        copy.wait()


def ready_call(rows, cols, count, probe, measured, table, centre):
    slots = measured.shape[0]
    height, width = centre.shape[1:]
    tiles = width // LANES
    return pl.pallas_call(
        ready_kernel,
        out_shape=(
            pltpu.SMEM((5 * slots + 2,), jnp.int32),
            near((slots,) + probe.shape),
            near(measured.shape, measured.dtype),
            near((4,) + table.shape[1:], jnp.bfloat16),
            near((2 * (tiles + 2), height + probe.shape[1], LANES)),
        ),
        in_specs=[HBM] * 2 + [VMEM] + [HBM] * 4,
        out_specs=(SMEM,) + (VMEM,) * 4,
        scratch_shapes=[
            pltpu.SMEM(rows.shape, jnp.int32),
            pltpu.SMEM(cols.shape, jnp.int32),
            pltpu.VMEM(probe.shape, F32),
            pltpu.VMEM(table.shape, F32),
            pltpu.SemaphoreType.DMA((5 + 2 * tiles,)),
        ],
        compiler_params=PARAMS,
        name="ready",
    )(*in_hbm(rows, cols), *in_vmem(jnp.broadcast_to(count, (8, LANES))), *in_hbm(probe, measured, table, centre))


def side_kernel(tile_ref, near_ref, far_ref, window, near_out, far_out):
    margin = near_ref.shape[1]
    columns = window.shape[0] // 2
    odd_row, odd_col = parities()
    bottom = window.shape[1] - margin
    near, far = place_of(odd_row, 0, bottom)
    for plane in range(2):
        for tile in range(columns - 2):
            lanes = slice(tile * LANES, (tile + 1) * LANES)
            window[plane * columns + 1 + tile, margin:bottom] = tile_ref[plane * columns + 1 + tile, margin:bottom]
            window[plane * columns + 1 + tile, pl.ds(near, margin), :] = near_ref[plane, :, lanes]
            window[plane * columns + 1 + tile, pl.ds(far, margin), :] = far_ref[plane, :, lanes]
    for plane in range(2):
        near_tile = plane * columns + jnp.where(odd_col == 1, 1, columns - 2)
        far_tile = plane * columns + jnp.where(odd_col == 1, columns - 2, 1)
        near_out[plane] = folded(window[near_tile], odd_col == 1)
        far_out[plane] = folded(window[far_tile], odd_col == 0)


def side_call(window, near_row, far_row):
    shape = near((2, window.shape[1] // 2, LANES))
    return pl.pallas_call(
        side_kernel,
        out_shape=(near(window.shape), shape, shape),
        in_specs=[VMEM] * 3,
        out_specs=(VMEM,) * 3,
        compiler_params=PARAMS,
        name="side_columns",
    )(*in_vmem(window, near_row, far_row))


def finder(plan, slots, start, inner, live):
    def find(index):
        at = jnp.where(index < inner, start + index, jnp.maximum(slots - 1 - (index - inner), 0))
        is_live = index < live
        slot = plan[jnp.where(is_live, at, jnp.where(inner > 0, start, slots - 1))]
        place = slots + 2 + 3 * slot
        scale = jnp.where(is_live, 2.0, 0.0).astype(F32)
        return slot, plan[place], plan[place + 1], plan[place + 2], scale, jnp.where(is_live, slot, slots)

    return find


def run_slots(groups, size_of, first, find, window, turned, measured, table, exits, probe_sum):
    size = turned.shape[2]
    columns = window.shape[0] // 2
    lane = lax.broadcasted_iota(jnp.int32, (size, LANES), 1)
    exits[exits.shape[0] - 1] = jnp.zeros(exits.shape[1:], F32)

    def load(pair):
        kept, waves = [], []
        for slot, row, tile, turn, _, _ in pair:
            here = lane >= turn
            patch = [
                jnp.where(
                    here,
                    window[plane * columns + tile, pl.ds(row, size), :],
                    window[plane * columns + tile + 1, pl.ds(row, size), :],
                )
                for plane in range(2)
            ]
            probe = [turned[slot, plane] for plane in range(2)]
            wave_real = probe[0] * patch[0] - probe[1] * patch[1]
            wave_imag = probe[0] * patch[1] + probe[1] * patch[0]
            kept.append(patch)
            waves.append(jnp.concatenate([wave_real, wave_imag], axis=1))
        return kept, jnp.concatenate(waves, axis=0)

    def regroup(pair):
        return jnp.concatenate(
            [
                jnp.concatenate([pair[:size, :size], pair[size:, :size]], axis=1),
                jnp.concatenate([pair[:size, size:], pair[size:, size:]], axis=1),
            ],
            axis=0,
        )

    def weigh(pair, psi):
        real, imag = psi[:size], psi[size:]
        weights = []
        for member, (slot, _, _, _, scale, _) in enumerate(pair):
            lanes = slice(member * size, (member + 1) * size)
            power = real[:, lanes] * real[:, lanes] + imag[:, lanes] * imag[:, lanes]
            weights.append((power - measured[slot].astype(F32)) * scale)
        weight = jnp.concatenate(weights, axis=1)
        return jnp.concatenate([weight * real, weight * imag], axis=0)

    def add_up(pair, kept, pair_exits):
        for member, (_, _, _, turn, _, kept_at) in enumerate(pair):
            patch = kept[member]
            exit_real = pair_exits[member * size : (member + 1) * size, :size]
            exit_imag = pair_exits[member * size : (member + 1) * size, size:]
            exits[kept_at, 0] = exit_real
            exits[kept_at, 1] = exit_imag
            terms = (patch[0] * exit_real + patch[1] * exit_imag, patch[0] * exit_imag - patch[1] * exit_real)
            back = (LANES - turn) & (LANES - 1)
            for plane in range(2):
                probe_sum[plane] += pltpu.roll(terms[plane], back, axis=1)

    def step(group, carry):
        slots = [find(first + group * size_of + member) for member in range(size_of)]
        pairs = [slots[member : member + 2] for member in range(0, size_of, 2)]
        loaded = [load(pair) for pair in pairs]
        waves = [regroup(times_table(wave, table[0], table[1])) for _, wave in loaded]
        waves = [weigh(pair, table_times(table[2], table[3], wave)) for pair, wave in zip(pairs, waves)]
        waves = [regroup(table_times(table[0], table[1], wave)) for wave in waves]
        waves = [times_table(wave, table[2], table[3]) for wave in waves]
        for pair, (kept, _), wave in zip(pairs, loaded, waves):
            add_up(pair, kept, wave)
        return carry

    lax.fori_loop(0, groups, step, 0)


def inner_kernel(plan, window, turned, measured, table, exits, probe_sum):
    slots = measured.shape[0]
    probe_sum[...] = jnp.zeros_like(probe_sum)
    groups = plan[slots] // GROUP
    find = finder(plan, slots, 0, groups * GROUP, groups * GROUP)
    run_slots(groups, GROUP, 0, find, window, turned, measured, table, exits, probe_sum)


def inner_call(plan, window, turned, measured, tables):
    slots = measured.shape[0]
    return pl.pallas_call(
        inner_kernel,
        out_shape=(near((slots + 1,) + turned.shape[1:]), near(turned.shape[1:])),
        in_specs=[SMEM] + [VMEM] * 4,
        out_specs=(VMEM,) * 2,
        compiler_params=PARAMS,
        cost_estimate=pl.CostEstimate(flops=10**10, bytes_accessed=2 * 10**7, transcendentals=0),
        name="slots_inside",
    )(*in_smem(plan), *in_vmem(window, turned, measured, tables))


def outer_kernel(
    plan, window_ref, near_col_ref, far_col_ref, turned, measured, table, probe_ref,
    exits, mine_out, other_out, window, probe_sum,
):
    slots = measured.shape[0]
    margin = turned.shape[2] // 2
    columns = window.shape[0] // 2
    half = window.shape[1] // 2
    odd_row, odd_col = parities()
    probe_sum[...] = probe_ref[...]
    for plane in range(2):
        own = slice(plane * columns + 1, (plane + 1) * columns - 1)
        window[own] = window_ref[own]
        near_tile = plane * columns + jnp.where(odd_col == 1, 0, columns - 1)
        far_tile = plane * columns + jnp.where(odd_col == 1, columns - 1, 0)
        for tile, ref in ((near_tile, near_col_ref), (far_tile, far_col_ref)):
            window[tile, :half] = ref[plane]
            window[tile, half:] = pltpu.roll(ref[plane], margin, axis=1)
    start = plan[slots] // GROUP * GROUP
    live = plan[slots + 1] - start
    find = finder(plan, slots, start, plan[slots] - start, live)
    large = live // (2 * GROUP)
    run_slots(large, 2 * GROUP, 0, find, window, turned, measured, table, exits, probe_sum)
    first = large * 2 * GROUP
    run_slots((live - first + GROUP - 1) // GROUP, GROUP, first, find, window, turned, measured, table, exits, probe_sum)
    factor = 1.0 / np.sqrt(np.float32(lax.axis_size("trow") * lax.axis_size("tcol") * slots))
    mine_out[...] = probe_sum[odd_row] * factor
    other_out[...] = probe_sum[1 - odd_row] * factor


def outer_call(plan, window, near_col, far_col, turned, measured, tables, probe_sum):
    slots = measured.shape[0]
    part = near(probe_sum.shape[1:])
    return pl.pallas_call(
        outer_kernel,
        out_shape=(near((slots + 1,) + turned.shape[1:]), part, part),
        in_specs=[SMEM] + [VMEM] * 7,
        out_specs=(VMEM,) * 3,
        scratch_shapes=[pltpu.VMEM(window.shape, F32), pltpu.VMEM(probe_sum.shape, F32)],
        compiler_params=PARAMS,
        cost_estimate=pl.CostEstimate(flops=10**10, bytes_accessed=2 * 10**7, transcendentals=0),
        name="slots_across",
    )(*in_smem(plan), *in_vmem(window, near_col, far_col, turned, measured, tables, probe_sum))


def add_objects(groups, find, turned, exits, grad):
    size = turned.shape[2]
    columns = grad.shape[0] // 2
    lane = lax.broadcasted_iota(jnp.int32, (size, LANES), 1)

    def step(index, carry):
        for member in range(ADDED):
            slot, row, tile, turn, _, kept_at = find(index * ADDED + member)
            here = lane >= turn
            probe = [turned[slot, plane] for plane in range(2)]
            exit_real, exit_imag = exits[kept_at, 0], exits[kept_at, 1]
            adds = (probe[0] * exit_real + probe[1] * exit_imag, probe[0] * exit_imag - probe[1] * exit_real)
            for plane in range(2):
                at = plane * columns + tile
                grad[at, pl.ds(row, size), :] += jnp.where(here, adds[plane], 0.0)
                grad[at + 1, pl.ds(row, size), :] += jnp.where(here, 0.0, adds[plane])
        return carry

    lax.fori_loop(0, groups, step, 0)


def first_object_kernel(plan, turned, exits, grad):
    slots = turned.shape[0]
    grad[...] = jnp.zeros_like(grad)
    start = plan[slots] // GROUP * GROUP
    add_objects(start // ADDED, finder(plan, slots, 0, start, start), turned, exits, grad)


def first_object_call(plan, window, turned, exits):
    return pl.pallas_call(
        first_object_kernel,
        out_shape=near(window.shape),
        in_specs=[SMEM] + [VMEM] * 2,
        out_specs=VMEM,
        compiler_params=PARAMS,
        cost_estimate=pl.CostEstimate(flops=10**9, bytes_accessed=10**5, transcendentals=0),
        name="object_inside",
    )(*in_smem(plan), *in_vmem(turned, exits))


def object_kernel(plan, turned, exits, grad_ref, grad, near_row_out, far_row_out, side_out):
    slots = turned.shape[0]
    margin = turned.shape[2] // 2
    columns = grad.shape[0] // 2
    tall = grad.shape[1]
    odd_row, _ = parities()
    near, far = place_of(odd_row, 0, tall - margin)
    grad[...] = grad_ref[...]
    start = plan[slots] // GROUP * GROUP
    live = plan[slots + 1] - start
    find = finder(plan, slots, start, plan[slots] - start, live)
    add_objects((live + ADDED - 1) // ADDED, find, turned, exits, grad)
    narrow = lax.broadcasted_iota(jnp.int32, (margin, LANES), 1) < margin
    for plane in range(2):
        base = plane * columns
        left, right = base, base + columns - 1
        for at, out in ((near, near_row_out), (far, far_row_out)):
            rows = pl.ds(at, margin)
            for tile in range(columns - 2):
                out[plane, :, tile * LANES : (tile + 1) * LANES] = grad[base + 1 + tile, rows, :]
            out[plane, :, (columns - 2) * LANES :] = jnp.where(narrow, grad[right, rows, :], grad[left, rows, :])
        for row in range(margin, tall - margin, margin):
            rows = slice(row, row + margin)
            side_out[plane, row - margin : row] = jnp.where(narrow, grad[right, rows, :], grad[left, rows, :])


def object_call(plan, turned, exits, grad):
    size = turned.shape[2]
    row = near((2, size // 2, (grad.shape[0] // 2 - 1) * LANES))
    return pl.pallas_call(
        object_kernel,
        out_shape=(near(grad.shape), row, row, near((2, grad.shape[1] - size, LANES))),
        in_specs=[SMEM] + [VMEM] * 3,
        out_specs=(VMEM,) * 4,
        compiler_params=PARAMS,
        cost_estimate=pl.CostEstimate(flops=10**9, bytes_accessed=10**5, transcendentals=0),
        name="object_across",
    )(*in_smem(plan), *in_vmem(turned, exits, grad))


def side_sum_kernel(side_ref, near_ref, far_ref, near_out, far_out, side):
    margin = near_ref.shape[1]
    height = side_ref.shape[1]
    odd_row, odd_col = parities()
    near_at, far_at = place_of(odd_row, 0, height - margin)
    wide = near_ref.shape[2]
    side[...] = side_ref[...]
    for plane in range(2):
        side[plane, pl.ds(near_at, margin), :] += near_ref[plane, :, wide - LANES :]
        side[plane, pl.ds(far_at, margin), :] += far_ref[plane, :, wide - LANES :]
    for plane in range(2):
        near_out[plane] = folded(side[plane], odd_col == 0)
        far_out[plane] = folded(side[plane], odd_col == 1)


def side_sum_call(side, near_row, far_row):
    shape = near((2, side.shape[1] // 2, LANES))
    return pl.pallas_call(
        side_sum_kernel,
        out_shape=(shape, shape),
        in_specs=[VMEM] * 3,
        out_specs=(VMEM, VMEM),
        scratch_shapes=[pltpu.VMEM(side.shape, F32)],
        compiler_params=PARAMS,
        name="side_sums",
    )(*in_vmem(side, near_row, far_row))


def final_kernel(grad, near_row_ref, far_row_ref, near_col_ref, far_col_ref, out_ref):
    height, width = out_ref.shape[1:]
    columns = grad.shape[0] // 2
    margin = near_row_ref.shape[1]
    half = height // 2
    odd_row, odd_col = parities()
    near_at, far_at = place_of(odd_row, 0, height - margin)
    narrow = lax.broadcasted_iota(jnp.int32, (half, LANES), 1) < LANES // 2
    for plane in range(2):
        for tile in range(columns - 2):
            lanes = slice(tile * LANES, (tile + 1) * LANES)
            out_ref[plane, :, lanes] = grad[plane * columns + 1 + tile, margin : margin + height]
        near = jnp.where(odd_col == 1, near_col_ref[plane], far_col_ref[plane])
        far = jnp.where(odd_col == 1, far_col_ref[plane], near_col_ref[plane])
        for first, left, right in (
            (0, near, far),
            (half, pltpu.roll(near, LANES // 2, axis=1), pltpu.roll(far, LANES // 2, axis=1)),
        ):
            rows = slice(first, first + half)
            out_ref[plane, rows, :LANES] += jnp.where(narrow, left, 0.0)
            out_ref[plane, rows, width - LANES :] += jnp.where(narrow, 0.0, right)
        out_ref[plane, pl.ds(near_at, margin), :] += near_row_ref[plane, :, :width]
        out_ref[plane, pl.ds(far_at, margin), :] += far_row_ref[plane, :, :width]


def final_call(grad, near_row, far_row, near_col, far_col):
    margin = near_row.shape[1]
    shape = (2, grad.shape[1] - 2 * margin, near_row.shape[2] - LANES)
    return pl.pallas_call(
        final_kernel,
        out_shape=jax.ShapeDtypeStruct(shape, F32),
        in_specs=[VMEM] * 5,
        out_specs=VMEM,
        compiler_params=PARAMS,
        name="final_sums",
    )(*in_vmem(grad, near_row, far_row, near_col, far_col))


def near_swap(value, axis):
    return lax.ppermute(value, axis, [(i, i ^ 1) for i in range(lax.axis_size(axis))])


def far_swap(value, axis):
    pairs = [(i, i + 1) for i in range(1, lax.axis_size(axis) - 1, 2)]
    return lax.ppermute(value, axis, pairs + [(j, i) for i, j in pairs])


def doubling_steps(n_row, n_col):
    along_cols = [(0, 1)] + [(0, 1 << k) for k in range(1, n_col.bit_length() - 1)][::-1]
    along_rows = [(1 << k, 0) for k in range(1, n_row.bit_length() - 1)]
    return along_rows, along_cols


def add_kernel(a_ref, b_ref, out_ref):
    out_ref[...] = a_ref[...] + b_ref[...]


def add_call(a, b):
    return pl.pallas_call(
        add_kernel,
        out_shape=near(a.shape),
        in_specs=[VMEM] * 2,
        out_specs=VMEM,
        compiler_params=PARAMS,
        cost_estimate=pl.CostEstimate(flops=10**9, bytes_accessed=10**5, transcendentals=0),
        name="add",
    )(*in_vmem(a, b))


def add_partner(mine, step, add=jnp.add):
    n_row, n_col = lax.axis_size("trow"), lax.axis_size("tcol")
    pairs = [(r * n_col + c, (r ^ step[0]) * n_col + (c ^ step[1])) for r in range(n_row) for c in range(n_col)]
    return add(mine, lax.ppermute(mine, ("trow", "tcol"), pairs))


def body(table, object_planes, probe, intensities, row_offsets, col_offsets, counts):
    size = probe.shape[1]
    rows, cols = row_offsets.reshape(-1), col_offsets.reshape(-1)
    measured = intensities.reshape(-1, size, size)
    near_row, far_row = edge_call(object_planes, size // 2)
    far_row = far_swap(far_row, "trow")
    near_row = near_swap(near_row, "trow")
    plan, turned, measured, tables, window = ready_call(rows, cols, counts, probe, measured, table, object_planes)
    window, near_side, far_side = side_call(window, near_row, far_row)
    far_col = far_swap(far_side, "tcol")
    near_col = near_swap(near_side, "tcol")
    inner_exits, probe_sum = inner_call(plan, window, turned, measured, tables)
    outer_exits, mine, other = outer_call(plan, window, near_col, far_col, turned, measured, tables, probe_sum)

    along_rows, along_cols = doubling_steps(lax.axis_size("trow"), lax.axis_size("tcol"))
    other, inner_exits = lax.optimization_barrier((other, inner_exits))
    grad = first_object_call(plan, window, turned, inner_exits)
    mine = mine + near_swap(other, "trow")
    mine, outer_exits = lax.optimization_barrier((mine, outer_exits))
    grad, near_row, far_row, side = object_call(plan, turned, outer_exits, grad)
    near_row = near_swap(near_row, "trow")
    far_row = far_swap(far_row, "trow")
    mine = add_partner(mine, along_cols[0])
    mine = add_partner(mine, along_cols[1], add=add_call)
    near_side, far_side = side_sum_call(side, near_row, far_row)
    mine, near_side, far_side = lax.optimization_barrier((mine, near_side, far_side))
    near_col = near_swap(near_side, "tcol")
    far_col = far_swap(far_side, "tcol")
    for step in along_cols[2:] + along_rows:
        mine = add_partner(mine, step)
    mine, near_col, far_col = lax.optimization_barrier((mine, near_col, far_col))
    object_grad = final_call(grad, near_row, far_row, near_col, far_col)
    other = near_swap(mine, "trow")
    odd_row, _ = parities()
    probe_grad = jnp.where(odd_row == 0, jnp.stack([mine, other]), jnp.stack([other, mine]))
    return (object_grad, probe_grad)


def solution(mesh):
    table = dft_tables(LANES)
    inner = jax.shard_map(
        body,
        mesh=mesh,
        in_specs=(
            P(),
            P(None, "trow", "tcol"),
            P(),
            P("trow", "tcol", None, None, None),
            P("trow", "tcol", None),
            P("trow", "tcol", None),
            P(("trow", "tcol")),
        ),
        out_specs=(P(None, "trow", "tcol"), P()),
        check_vma=False,
    )

    def run(*args):
        return inner(jnp.asarray(table), *args)

    return run
```

```python
import jax
import jax.numpy as jnp
import numpy as np
from jax import lax
from jax.experimental import pallas as pl
from jax.experimental.pallas import tpu as pltpu
from jax.sharding import PartitionSpec as P

LANES = 128
VMEM_BYTES = 24 * 1024 * 1024
GROUP = 8
ADDED = 4
F32 = jnp.float32
HBM = pl.BlockSpec(memory_space=pltpu.HBM)
VMEM = pl.BlockSpec(memory_space=pltpu.VMEM)
SMEM = pl.BlockSpec(memory_space=pltpu.SMEM)
PARAMS = pltpu.CompilerParams(vmem_limit_bytes=VMEM_BYTES)


def in_hbm(*arrays):
    return [pltpu.with_memory_space_constraint(array, pltpu.HBM) for array in arrays]


def in_vmem(*arrays):
    return [pltpu.with_memory_space_constraint(array, pltpu.VMEM) for array in arrays]


def in_smem(*arrays):
    return [pltpu.with_memory_space_constraint(array, pltpu.SMEM) for array in arrays]


def near(shape, dtype=F32):
    return pltpu.VMEM(tuple(shape), dtype)


def dft_tables(length):
    index = np.arange(length)
    angle = -2.0 * np.pi * (np.outer(index, index) % length) / length
    cosine, sine = np.cos(angle) / np.sqrt(length), np.sin(angle) / np.sqrt(length)
    right = np.block([[cosine, sine], [-sine, cosine]])
    return np.stack([right, right.T]).astype(np.float32)


def split(value):
    high = value.astype(jnp.bfloat16)
    low = (value - high.astype(F32)).astype(jnp.bfloat16)
    return high, low


def dot(a, b):
    return jnp.dot(a, b, preferred_element_type=F32)


def times_table(value, high, low):
    big, small = split(value)
    return dot(jnp.concatenate([big, small, big], axis=1), jnp.concatenate([high, high, low], axis=0))


def table_times(high, low, value):
    big, small = split(value)
    return dot(jnp.concatenate([high, high, low], axis=1), jnp.concatenate([big, small, big], axis=0))


def folded(tall, low_lanes):
    half = tall.shape[0] // 2
    lane = lax.broadcasted_iota(jnp.int32, (half, LANES), 1)
    here = (lane < LANES // 2) == low_lanes
    return jnp.where(here, tall[:half], pltpu.roll(tall[half:], LANES // 2, axis=1))


def parities():
    return lax.axis_index("trow") % 2, lax.axis_index("tcol") % 2


def place_of(odd, low, high):
    near = pl.multiple_of(jnp.where(odd == 1, low, high), 8)
    far = pl.multiple_of(jnp.where(odd == 1, high, low), 8)
    return near, far


def edge_kernel(centre_ref, near_out, far_out, sem):
    margin = near_out.shape[1]
    odd_row, _ = parities()
    near, far = place_of(odd_row, 0, centre_ref.shape[1] - margin)
    copies = [
        pltpu.make_async_copy(centre_ref.at[:, pl.ds(far, margin)], far_out, sem.at[0]),
        pltpu.make_async_copy(centre_ref.at[:, pl.ds(near, margin)], near_out, sem.at[1]),
    ]
    for copy in copies:
        copy.start()
    for copy in copies:
        copy.wait()


def edge_call(centre, margin):
    edge = near((2, margin, centre.shape[2]))
    return pl.pallas_call(
        edge_kernel,
        out_shape=(edge, edge),
        in_specs=[HBM],
        out_specs=(VMEM,) * 2,
        scratch_shapes=[pltpu.SemaphoreType.DMA((2,))],
        compiler_params=PARAMS,
        name="edge_rows",
    )(*in_hbm(centre))


def ready_kernel(
    rows_ref, cols_ref, count_ref, probe_ref, measured_ref, table_ref, centre_ref, plan, turned, measured, tables, window,
    row_list, col_list, probe, table, sem,
):
    slots = measured.shape[0]
    margin = probe.shape[1] // 2
    height, width = centre_ref.shape[1:]
    columns = window.shape[0] // 2
    inner_columns = width - probe.shape[2]
    copies = [(rows_ref, row_list), (cols_ref, col_list), (probe_ref, probe), (table_ref, table)]
    for plane in range(2):
        for tile in range(columns - 2):
            lanes = slice(tile * LANES, (tile + 1) * LANES)
            copies.append((centre_ref.at[plane, :, lanes], window.at[plane * columns + 1 + tile, pl.ds(margin, height)]))
    copies.append((measured_ref, measured))
    copies = [pltpu.make_async_copy(a, b, sem.at[i]) for i, (a, b) in enumerate(copies)]
    for copy in copies:
        copy.start()
    for copy in copies[:3]:
        copy.wait()
    count = count_ref[0, 0]
    inner = jnp.int32(0)
    for slot in range(slots):
        first = col_list[slot]
        live = slot < count
        is_inner = jnp.logical_and(jnp.logical_and(first >= 0, first <= inner_columns), live)
        at = jnp.where(is_inner, inner, slots - 1 - (slot - inner))
        plan[jnp.where(live, at, 5 * slots + 1)] = slot
        inner = inner + is_inner.astype(jnp.int32)
        col = first + LANES
        turn = col & (LANES - 1)
        place = slots + 2 + 3 * slot
        plan[place] = row_list[slot] + margin
        plan[place + 1] = lax.shift_right_logical(col, 7)
        plan[place + 2] = turn
        for plane in range(2):
            turned[slot, plane] = pltpu.roll(probe[plane], turn, axis=1)
    plan[slots] = inner
    plan[slots + 1] = count
    copies[3].wait()
    for index in range(2):
        tables[2 * index], tables[2 * index + 1] = split(table[index])
    for copy in copies[4:]:
        copy.wait()


def ready_call(rows, cols, count, probe, measured, table, centre):
    slots = measured.shape[0]
    height, width = centre.shape[1:]
    tiles = width // LANES
    return pl.pallas_call(
        ready_kernel,
        out_shape=(
            pltpu.SMEM((5 * slots + 2,), jnp.int32),
            near((slots,) + probe.shape),
            near(measured.shape, measured.dtype),
            near((4,) + table.shape[1:], jnp.bfloat16),
            near((2 * (tiles + 2), height + probe.shape[1], LANES)),
        ),
        in_specs=[HBM] * 2 + [VMEM] + [HBM] * 4,
        out_specs=(SMEM,) + (VMEM,) * 4,
        scratch_shapes=[
            pltpu.SMEM(rows.shape, jnp.int32),
            pltpu.SMEM(cols.shape, jnp.int32),
            pltpu.VMEM(probe.shape, F32),
            pltpu.VMEM(table.shape, F32),
            pltpu.SemaphoreType.DMA((5 + 2 * tiles,)),
        ],
        compiler_params=PARAMS,
        name="ready",
    )(*in_hbm(rows, cols), *in_vmem(jnp.broadcast_to(count, (8, LANES))), *in_hbm(probe, measured, table, centre))


def side_kernel(tile_ref, near_ref, far_ref, window, near_out, far_out):
    margin = near_ref.shape[1]
    columns = window.shape[0] // 2
    odd_row, odd_col = parities()
    bottom = window.shape[1] - margin
    near, far = place_of(odd_row, 0, bottom)
    for plane in range(2):
        for tile in range(columns - 2):
            lanes = slice(tile * LANES, (tile + 1) * LANES)
            window[plane * columns + 1 + tile, margin:bottom] = tile_ref[plane * columns + 1 + tile, margin:bottom]
            window[plane * columns + 1 + tile, pl.ds(near, margin), :] = near_ref[plane, :, lanes]
            window[plane * columns + 1 + tile, pl.ds(far, margin), :] = far_ref[plane, :, lanes]
    for plane in range(2):
        near_tile = plane * columns + jnp.where(odd_col == 1, 1, columns - 2)
        far_tile = plane * columns + jnp.where(odd_col == 1, columns - 2, 1)
        near_out[plane] = folded(window[near_tile], odd_col == 1)
        far_out[plane] = folded(window[far_tile], odd_col == 0)


def side_call(window, near_row, far_row):
    shape = near((2, window.shape[1] // 2, LANES))
    return pl.pallas_call(
        side_kernel,
        out_shape=(near(window.shape), shape, shape),
        in_specs=[VMEM] * 3,
        out_specs=(VMEM,) * 3,
        compiler_params=PARAMS,
        name="side_columns",
    )(*in_vmem(window, near_row, far_row))


def finder(plan, slots, start, inner, live):
    def find(index):
        at = jnp.where(index < inner, start + index, jnp.maximum(slots - 1 - (index - inner), 0))
        is_live = index < live
        slot = plan[jnp.where(is_live, at, jnp.where(inner > 0, start, slots - 1))]
        place = slots + 2 + 3 * slot
        scale = jnp.where(is_live, 2.0, 0.0).astype(F32)
        return slot, plan[place], plan[place + 1], plan[place + 2], scale, jnp.where(is_live, slot, slots)

    return find


def run_slots(groups, size_of, first, find, window, turned, measured, table, exits, probe_sum):
    size = turned.shape[2]
    columns = window.shape[0] // 2
    lane = lax.broadcasted_iota(jnp.int32, (size, LANES), 1)
    exits[exits.shape[0] - 1] = jnp.zeros(exits.shape[1:], F32)

    def load(pair):
        kept, waves = [], []
        for slot, row, tile, turn, _, _ in pair:
            here = lane >= turn
            patch = [
                jnp.where(
                    here,
                    window[plane * columns + tile, pl.ds(row, size), :],
                    window[plane * columns + tile + 1, pl.ds(row, size), :],
                )
                for plane in range(2)
            ]
            probe = [turned[slot, plane] for plane in range(2)]
            wave_real = probe[0] * patch[0] - probe[1] * patch[1]
            wave_imag = probe[0] * patch[1] + probe[1] * patch[0]
            kept.append(patch)
            waves.append(jnp.concatenate([wave_real, wave_imag], axis=1))
        return kept, jnp.concatenate(waves, axis=0)

    def regroup(pair):
        return jnp.concatenate(
            [
                jnp.concatenate([pair[:size, :size], pair[size:, :size]], axis=1),
                jnp.concatenate([pair[:size, size:], pair[size:, size:]], axis=1),
            ],
            axis=0,
        )

    def weigh(pair, psi):
        real, imag = psi[:size], psi[size:]
        weights = []
        for member, (slot, _, _, _, scale, _) in enumerate(pair):
            lanes = slice(member * size, (member + 1) * size)
            power = real[:, lanes] * real[:, lanes] + imag[:, lanes] * imag[:, lanes]
            weights.append((power - measured[slot].astype(F32)) * scale)
        weight = jnp.concatenate(weights, axis=1)
        return jnp.concatenate([weight * real, weight * imag], axis=0)

    def add_up(pair, kept, pair_exits):
        for member, (_, _, _, turn, _, kept_at) in enumerate(pair):
            patch = kept[member]
            exit_real = pair_exits[member * size : (member + 1) * size, :size]
            exit_imag = pair_exits[member * size : (member + 1) * size, size:]
            exits[kept_at, 0] = exit_real
            exits[kept_at, 1] = exit_imag
            terms = (patch[0] * exit_real + patch[1] * exit_imag, patch[0] * exit_imag - patch[1] * exit_real)
            back = (LANES - turn) & (LANES - 1)
            for plane in range(2):
                probe_sum[plane] += pltpu.roll(terms[plane], back, axis=1)

    def step(group, carry):
        slots = [find(first + group * size_of + member) for member in range(size_of)]
        pairs = [slots[member : member + 2] for member in range(0, size_of, 2)]
        loaded = [load(pair) for pair in pairs]
        waves = [regroup(times_table(wave, table[0], table[1])) for _, wave in loaded]
        waves = [weigh(pair, table_times(table[2], table[3], wave)) for pair, wave in zip(pairs, waves)]
        waves = [regroup(table_times(table[0], table[1], wave)) for wave in waves]
        waves = [times_table(wave, table[2], table[3]) for wave in waves]
        for pair, (kept, _), wave in zip(pairs, loaded, waves):
            add_up(pair, kept, wave)
        return carry

    lax.fori_loop(0, groups, step, 0)


def inner_kernel(plan, window, turned, measured, table, exits, probe_sum):
    slots = measured.shape[0]
    probe_sum[...] = jnp.zeros_like(probe_sum)
    groups = plan[slots] // GROUP
    find = finder(plan, slots, 0, groups * GROUP, groups * GROUP)
    run_slots(groups, GROUP, 0, find, window, turned, measured, table, exits, probe_sum)


def inner_call(plan, window, turned, measured, tables):
    slots = measured.shape[0]
    return pl.pallas_call(
        inner_kernel,
        out_shape=(near((slots + 1,) + turned.shape[1:]), near(turned.shape[1:])),
        in_specs=[SMEM] + [VMEM] * 4,
        out_specs=(VMEM,) * 2,
        compiler_params=PARAMS,
        cost_estimate=pl.CostEstimate(flops=10**10, bytes_accessed=2 * 10**7, transcendentals=0),
        name="slots_inside",
    )(*in_smem(plan), *in_vmem(window, turned, measured, tables))


def outer_kernel(
    plan, window_ref, near_col_ref, far_col_ref, turned, measured, table, probe_ref,
    exits, mine_out, other_out, window, probe_sum,
):
    slots = measured.shape[0]
    margin = turned.shape[2] // 2
    columns = window.shape[0] // 2
    half = window.shape[1] // 2
    odd_row, odd_col = parities()
    probe_sum[...] = probe_ref[...]
    for plane in range(2):
        own = slice(plane * columns + 1, (plane + 1) * columns - 1)
        window[own] = window_ref[own]
        near_tile = plane * columns + jnp.where(odd_col == 1, 0, columns - 1)
        far_tile = plane * columns + jnp.where(odd_col == 1, columns - 1, 0)
        for tile, ref in ((near_tile, near_col_ref), (far_tile, far_col_ref)):
            window[tile, :half] = ref[plane]
            window[tile, half:] = pltpu.roll(ref[plane], margin, axis=1)
    start = plan[slots] // GROUP * GROUP
    live = plan[slots + 1] - start
    find = finder(plan, slots, start, plan[slots] - start, live)
    large = live // (2 * GROUP)
    run_slots(large, 2 * GROUP, 0, find, window, turned, measured, table, exits, probe_sum)
    first = large * 2 * GROUP
    groups = (live - first + GROUP // 2 - 1) // GROUP
    run_slots(groups, GROUP, first, find, window, turned, measured, table, exits, probe_sum)
    first = first + groups * GROUP
    few = (live > first).astype(jnp.int32)
    run_slots(few, GROUP // 2, first, find, window, turned, measured, table, exits, probe_sum)
    factor = 1.0 / np.sqrt(np.float32(lax.axis_size("trow") * lax.axis_size("tcol") * slots))
    mine_out[...] = probe_sum[odd_row] * factor
    other_out[...] = probe_sum[1 - odd_row] * factor


def outer_call(plan, window, near_col, far_col, turned, measured, tables, probe_sum):
    slots = measured.shape[0]
    part = near(probe_sum.shape[1:])
    return pl.pallas_call(
        outer_kernel,
        out_shape=(near((slots + 1,) + turned.shape[1:]), part, part),
        in_specs=[SMEM] + [VMEM] * 7,
        out_specs=(VMEM,) * 3,
        scratch_shapes=[pltpu.VMEM(window.shape, F32), pltpu.VMEM(probe_sum.shape, F32)],
        compiler_params=PARAMS,
        cost_estimate=pl.CostEstimate(flops=10**10, bytes_accessed=2 * 10**7, transcendentals=0),
        name="slots_across",
    )(*in_smem(plan), *in_vmem(window, near_col, far_col, turned, measured, tables, probe_sum))


def add_objects(groups, find, turned, exits, grad):
    size = turned.shape[2]
    columns = grad.shape[0] // 2
    lane = lax.broadcasted_iota(jnp.int32, (size, LANES), 1)

    def step(index, carry):
        for member in range(ADDED):
            slot, row, tile, turn, _, kept_at = find(index * ADDED + member)
            here = lane >= turn
            probe = [turned[slot, plane] for plane in range(2)]
            exit_real, exit_imag = exits[kept_at, 0], exits[kept_at, 1]
            adds = (probe[0] * exit_real + probe[1] * exit_imag, probe[0] * exit_imag - probe[1] * exit_real)
            for plane in range(2):
                at = plane * columns + tile
                grad[at, pl.ds(row, size), :] += jnp.where(here, adds[plane], 0.0)
                grad[at + 1, pl.ds(row, size), :] += jnp.where(here, 0.0, adds[plane])
        return carry

    lax.fori_loop(0, groups, step, 0)


def first_object_kernel(plan, turned, exits, grad):
    slots = turned.shape[0]
    grad[...] = jnp.zeros_like(grad)
    start = plan[slots] // GROUP * GROUP
    add_objects(start // ADDED, finder(plan, slots, 0, start, start), turned, exits, grad)


def first_object_call(plan, window, turned, exits):
    return pl.pallas_call(
        first_object_kernel,
        out_shape=near(window.shape),
        in_specs=[SMEM] + [VMEM] * 2,
        out_specs=VMEM,
        compiler_params=PARAMS,
        cost_estimate=pl.CostEstimate(flops=10**9, bytes_accessed=10**5, transcendentals=0),
        name="object_inside",
    )(*in_smem(plan), *in_vmem(turned, exits))


def object_kernel(plan, turned, exits, grad_ref, grad, near_row_out, far_row_out, side_out):
    slots = turned.shape[0]
    margin = turned.shape[2] // 2
    columns = grad.shape[0] // 2
    tall = grad.shape[1]
    odd_row, _ = parities()
    near, far = place_of(odd_row, 0, tall - margin)
    grad[...] = grad_ref[...]
    start = plan[slots] // GROUP * GROUP
    live = plan[slots + 1] - start
    find = finder(plan, slots, start, plan[slots] - start, live)
    add_objects((live + ADDED - 1) // ADDED, find, turned, exits, grad)
    narrow = lax.broadcasted_iota(jnp.int32, (margin, LANES), 1) < margin
    for plane in range(2):
        base = plane * columns
        left, right = base, base + columns - 1
        for at, out in ((near, near_row_out), (far, far_row_out)):
            rows = pl.ds(at, margin)
            for tile in range(columns - 2):
                out[plane, :, tile * LANES : (tile + 1) * LANES] = grad[base + 1 + tile, rows, :]
            out[plane, :, (columns - 2) * LANES :] = jnp.where(narrow, grad[right, rows, :], grad[left, rows, :])
        for row in range(margin, tall - margin, margin):
            rows = slice(row, row + margin)
            side_out[plane, row - margin : row] = jnp.where(narrow, grad[right, rows, :], grad[left, rows, :])


def object_call(plan, turned, exits, grad):
    size = turned.shape[2]
    row = near((2, size // 2, (grad.shape[0] // 2 - 1) * LANES))
    return pl.pallas_call(
        object_kernel,
        out_shape=(near(grad.shape), row, row, near((2, grad.shape[1] - size, LANES))),
        in_specs=[SMEM] + [VMEM] * 3,
        out_specs=(VMEM,) * 4,
        compiler_params=PARAMS,
        cost_estimate=pl.CostEstimate(flops=10**9, bytes_accessed=10**5, transcendentals=0),
        name="object_across",
    )(*in_smem(plan), *in_vmem(turned, exits, grad))


def side_sum_kernel(side_ref, near_ref, far_ref, near_out, far_out, side):
    margin = near_ref.shape[1]
    height = side_ref.shape[1]
    odd_row, odd_col = parities()
    near_at, far_at = place_of(odd_row, 0, height - margin)
    wide = near_ref.shape[2]
    side[...] = side_ref[...]
    for plane in range(2):
        side[plane, pl.ds(near_at, margin), :] += near_ref[plane, :, wide - LANES :]
        side[plane, pl.ds(far_at, margin), :] += far_ref[plane, :, wide - LANES :]
    for plane in range(2):
        near_out[plane] = folded(side[plane], odd_col == 0)
        far_out[plane] = folded(side[plane], odd_col == 1)


def side_sum_call(side, near_row, far_row):
    shape = near((2, side.shape[1] // 2, LANES))
    return pl.pallas_call(
        side_sum_kernel,
        out_shape=(shape, shape),
        in_specs=[VMEM] * 3,
        out_specs=(VMEM, VMEM),
        scratch_shapes=[pltpu.VMEM(side.shape, F32)],
        compiler_params=PARAMS,
        name="side_sums",
    )(*in_vmem(side, near_row, far_row))


def final_kernel(grad, near_row_ref, far_row_ref, near_col_ref, far_col_ref, out_ref):
    height, width = out_ref.shape[1:]
    columns = grad.shape[0] // 2
    margin = near_row_ref.shape[1]
    half = height // 2
    odd_row, odd_col = parities()
    near_at, far_at = place_of(odd_row, 0, height - margin)
    narrow = lax.broadcasted_iota(jnp.int32, (half, LANES), 1) < LANES // 2
    for plane in range(2):
        for tile in range(columns - 2):
            lanes = slice(tile * LANES, (tile + 1) * LANES)
            out_ref[plane, :, lanes] = grad[plane * columns + 1 + tile, margin : margin + height]
        near = jnp.where(odd_col == 1, near_col_ref[plane], far_col_ref[plane])
        far = jnp.where(odd_col == 1, far_col_ref[plane], near_col_ref[plane])
        for first, left, right in (
            (0, near, far),
            (half, pltpu.roll(near, LANES // 2, axis=1), pltpu.roll(far, LANES // 2, axis=1)),
        ):
            rows = slice(first, first + half)
            out_ref[plane, rows, :LANES] += jnp.where(narrow, left, 0.0)
            out_ref[plane, rows, width - LANES :] += jnp.where(narrow, 0.0, right)
        out_ref[plane, pl.ds(near_at, margin), :] += near_row_ref[plane, :, :width]
        out_ref[plane, pl.ds(far_at, margin), :] += far_row_ref[plane, :, :width]


def final_call(grad, near_row, far_row, near_col, far_col):
    margin = near_row.shape[1]
    shape = (2, grad.shape[1] - 2 * margin, near_row.shape[2] - LANES)
    return pl.pallas_call(
        final_kernel,
        out_shape=jax.ShapeDtypeStruct(shape, F32),
        in_specs=[VMEM] * 5,
        out_specs=VMEM,
        compiler_params=PARAMS,
        name="final_sums",
    )(*in_vmem(grad, near_row, far_row, near_col, far_col))


def near_swap(value, axis):
    return lax.ppermute(value, axis, [(i, i ^ 1) for i in range(lax.axis_size(axis))])


def far_swap(value, axis):
    pairs = [(i, i + 1) for i in range(1, lax.axis_size(axis) - 1, 2)]
    return lax.ppermute(value, axis, pairs + [(j, i) for i, j in pairs])


def doubling_steps(n_row, n_col):
    along_cols = [(0, 1)] + [(0, 1 << k) for k in range(1, n_col.bit_length() - 1)][::-1]
    along_rows = [(1 << k, 0) for k in range(1, n_row.bit_length() - 1)]
    return along_rows, along_cols


def add_kernel(a_ref, b_ref, out_ref):
    out_ref[...] = a_ref[...] + b_ref[...]


def add_call(a, b):
    return pl.pallas_call(
        add_kernel,
        out_shape=near(a.shape),
        in_specs=[VMEM] * 2,
        out_specs=VMEM,
        compiler_params=PARAMS,
        cost_estimate=pl.CostEstimate(flops=10**9, bytes_accessed=10**5, transcendentals=0),
        name="add",
    )(*in_vmem(a, b))


def add_partner(mine, step, add=jnp.add):
    n_row, n_col = lax.axis_size("trow"), lax.axis_size("tcol")
    pairs = [(r * n_col + c, (r ^ step[0]) * n_col + (c ^ step[1])) for r in range(n_row) for c in range(n_col)]
    return add(mine, lax.ppermute(mine, ("trow", "tcol"), pairs))


def body(table, object_planes, probe, intensities, row_offsets, col_offsets, counts):
    size = probe.shape[1]
    rows, cols = row_offsets.reshape(-1), col_offsets.reshape(-1)
    measured = intensities.reshape(-1, size, size)
    near_row, far_row = edge_call(object_planes, size // 2)
    far_row = far_swap(far_row, "trow")
    near_row = near_swap(near_row, "trow")
    plan, turned, measured, tables, window = ready_call(rows, cols, counts, probe, measured, table, object_planes)
    window, near_side, far_side = side_call(window, near_row, far_row)
    far_col = far_swap(far_side, "tcol")
    near_col = near_swap(near_side, "tcol")
    inner_exits, probe_sum = inner_call(plan, window, turned, measured, tables)
    outer_exits, mine, other = outer_call(plan, window, near_col, far_col, turned, measured, tables, probe_sum)

    along_rows, along_cols = doubling_steps(lax.axis_size("trow"), lax.axis_size("tcol"))
    other, inner_exits = lax.optimization_barrier((other, inner_exits))
    grad = first_object_call(plan, window, turned, inner_exits)
    mine = mine + near_swap(other, "trow")
    mine, outer_exits = lax.optimization_barrier((mine, outer_exits))
    grad, near_row, far_row, side = object_call(plan, turned, outer_exits, grad)
    near_row = near_swap(near_row, "trow")
    far_row = far_swap(far_row, "trow")
    mine = add_partner(mine, along_cols[0])
    mine = add_partner(mine, along_cols[1], add=add_call)
    near_side, far_side = side_sum_call(side, near_row, far_row)
    mine, near_side, far_side = lax.optimization_barrier((mine, near_side, far_side))
    near_col = near_swap(near_side, "tcol")
    far_col = far_swap(far_side, "tcol")
    for step in along_cols[2:] + along_rows:
        mine = add_partner(mine, step)
    mine, near_col, far_col = lax.optimization_barrier((mine, near_col, far_col))
    object_grad = final_call(grad, near_row, far_row, near_col, far_col)
    other = near_swap(mine, "trow")
    odd_row, _ = parities()
    probe_grad = jnp.where(odd_row == 0, jnp.stack([mine, other]), jnp.stack([other, mine]))
    return (object_grad, probe_grad)


def solution(mesh):
    table = dft_tables(LANES)
    inner = jax.shard_map(
        body,
        mesh=mesh,
        in_specs=(
            P(),
            P(None, "trow", "tcol"),
            P(),
            P("trow", "tcol", None, None, None),
            P("trow", "tcol", None),
            P("trow", "tcol", None),
            P(("trow", "tcol")),
        ),
        out_specs=(P(None, "trow", "tcol"), P()),
        check_vma=False,
    )

    def run(*args):
        return inner(jnp.asarray(table), *args)

    return run
```

```python
import jax
import jax.numpy as jnp
import numpy as np
from jax import lax
from jax.experimental import pallas as pl
from jax.experimental.pallas import tpu as pltpu
from jax.sharding import PartitionSpec as P

LANES = 128
VMEM_BYTES = 24 * 1024 * 1024
GROUP = 8
ADDED = 4
F32 = jnp.float32
HBM = pl.BlockSpec(memory_space=pltpu.HBM)
VMEM = pl.BlockSpec(memory_space=pltpu.VMEM)
SMEM = pl.BlockSpec(memory_space=pltpu.SMEM)
PARAMS = pltpu.CompilerParams(vmem_limit_bytes=VMEM_BYTES)


def in_hbm(*arrays):
    return [pltpu.with_memory_space_constraint(array, pltpu.HBM) for array in arrays]


def in_vmem(*arrays):
    return [pltpu.with_memory_space_constraint(array, pltpu.VMEM) for array in arrays]


def in_smem(*arrays):
    return [pltpu.with_memory_space_constraint(array, pltpu.SMEM) for array in arrays]


def near(shape, dtype=F32):
    return pltpu.VMEM(tuple(shape), dtype)


def dft_tables(length):
    index = np.arange(length)
    angle = -2.0 * np.pi * (np.outer(index, index) % length) / length
    cosine, sine = np.cos(angle) / np.sqrt(length), np.sin(angle) / np.sqrt(length)
    right = np.block([[cosine, sine], [-sine, cosine]])
    return np.stack([right, right.T]).astype(np.float32)


def split(value):
    high = value.astype(jnp.bfloat16)
    low = (value - high.astype(F32)).astype(jnp.bfloat16)
    return high, low


def dot(a, b):
    return jnp.dot(a, b, preferred_element_type=F32)


def times_table(value, high, low):
    big, small = split(value)
    rows = value.shape[0]
    both = dot(jnp.concatenate([big, small], axis=0), high)
    return both[:rows] + (both[rows:] + dot(big, low))


def table_times(high, low, value):
    big, small = split(value)
    return dot(jnp.concatenate([high, high, low], axis=1), jnp.concatenate([big, small, big], axis=0))


def folded(tall, low_lanes):
    half = tall.shape[0] // 2
    lane = lax.broadcasted_iota(jnp.int32, (half, LANES), 1)
    here = (lane < LANES // 2) == low_lanes
    return jnp.where(here, tall[:half], pltpu.roll(tall[half:], LANES // 2, axis=1))


def parities():
    return lax.axis_index("trow") % 2, lax.axis_index("tcol") % 2


def place_of(odd, low, high):
    near = pl.multiple_of(jnp.where(odd == 1, low, high), 8)
    far = pl.multiple_of(jnp.where(odd == 1, high, low), 8)
    return near, far


def edge_kernel(centre_ref, near_out, far_out, sem):
    margin = near_out.shape[1]
    odd_row, _ = parities()
    near, far = place_of(odd_row, 0, centre_ref.shape[1] - margin)
    copies = [
        pltpu.make_async_copy(centre_ref.at[:, pl.ds(far, margin)], far_out, sem.at[0]),
        pltpu.make_async_copy(centre_ref.at[:, pl.ds(near, margin)], near_out, sem.at[1]),
    ]
    for copy in copies:
        copy.start()
    for copy in copies:
        copy.wait()


def edge_call(centre, margin):
    edge = near((2, margin, centre.shape[2]))
    return pl.pallas_call(
        edge_kernel,
        out_shape=(edge, edge),
        in_specs=[HBM],
        out_specs=(VMEM,) * 2,
        scratch_shapes=[pltpu.SemaphoreType.DMA((2,))],
        compiler_params=PARAMS,
        name="edge_rows",
    )(*in_hbm(centre))


def ready_kernel(
    rows_ref, cols_ref, count_ref, probe_ref, measured_ref, table_ref, centre_ref, plan, turned, measured, tables, window,
    row_list, col_list, probe, table, sem,
):
    slots = measured.shape[0]
    margin = probe.shape[1] // 2
    height, width = centre_ref.shape[1:]
    columns = window.shape[0] // 2
    inner_columns = width - probe.shape[2]
    copies = [(rows_ref, row_list), (cols_ref, col_list), (probe_ref, probe), (table_ref, table)]
    for plane in range(2):
        for tile in range(columns - 2):
            lanes = slice(tile * LANES, (tile + 1) * LANES)
            copies.append((centre_ref.at[plane, :, lanes], window.at[plane * columns + 1 + tile, pl.ds(margin, height)]))
    copies.append((measured_ref, measured))
    copies = [pltpu.make_async_copy(a, b, sem.at[i]) for i, (a, b) in enumerate(copies)]
    for copy in copies:
        copy.start()
    for copy in copies[:3]:
        copy.wait()
    count = count_ref[0, 0]
    inner = jnp.int32(0)
    for slot in range(slots):
        first = col_list[slot]
        live = slot < count
        is_inner = jnp.logical_and(jnp.logical_and(first >= 0, first <= inner_columns), live)
        at = jnp.where(is_inner, inner, slots - 1 - (slot - inner))
        plan[jnp.where(live, at, 5 * slots + 1)] = slot
        inner = inner + is_inner.astype(jnp.int32)
        col = first + LANES
        turn = col & (LANES - 1)
        place = slots + 2 + 3 * slot
        plan[place] = row_list[slot] + margin
        plan[place + 1] = lax.shift_right_logical(col, 7)
        plan[place + 2] = turn
        for plane in range(2):
            turned[slot, plane] = pltpu.roll(probe[plane], turn, axis=1)
    plan[slots] = inner
    plan[slots + 1] = count
    copies[3].wait()
    for index in range(2):
        tables[2 * index], tables[2 * index + 1] = split(table[index])
    for copy in copies[4:]:
        copy.wait()


def ready_call(rows, cols, count, probe, measured, table, centre):
    slots = measured.shape[0]
    height, width = centre.shape[1:]
    tiles = width // LANES
    return pl.pallas_call(
        ready_kernel,
        out_shape=(
            pltpu.SMEM((5 * slots + 2,), jnp.int32),
            near((slots,) + probe.shape),
            near(measured.shape, measured.dtype),
            near((4,) + table.shape[1:], jnp.bfloat16),
            near((2 * (tiles + 2), height + probe.shape[1], LANES)),
        ),
        in_specs=[HBM] * 2 + [VMEM] + [HBM] * 4,
        out_specs=(SMEM,) + (VMEM,) * 4,
        scratch_shapes=[
            pltpu.SMEM(rows.shape, jnp.int32),
            pltpu.SMEM(cols.shape, jnp.int32),
            pltpu.VMEM(probe.shape, F32),
            pltpu.VMEM(table.shape, F32),
            pltpu.SemaphoreType.DMA((5 + 2 * tiles,)),
        ],
        compiler_params=PARAMS,
        name="ready",
    )(*in_hbm(rows, cols), *in_vmem(jnp.broadcast_to(count, (8, LANES))), *in_hbm(probe, measured, table, centre))


def side_kernel(tile_ref, near_ref, far_ref, window, near_out, far_out):
    margin = near_ref.shape[1]
    columns = window.shape[0] // 2
    odd_row, odd_col = parities()
    bottom = window.shape[1] - margin
    near, far = place_of(odd_row, 0, bottom)
    for plane in range(2):
        for tile in range(columns - 2):
            lanes = slice(tile * LANES, (tile + 1) * LANES)
            window[plane * columns + 1 + tile, margin:bottom] = tile_ref[plane * columns + 1 + tile, margin:bottom]
            window[plane * columns + 1 + tile, pl.ds(near, margin), :] = near_ref[plane, :, lanes]
            window[plane * columns + 1 + tile, pl.ds(far, margin), :] = far_ref[plane, :, lanes]
    for plane in range(2):
        near_tile = plane * columns + jnp.where(odd_col == 1, 1, columns - 2)
        far_tile = plane * columns + jnp.where(odd_col == 1, columns - 2, 1)
        near_out[plane] = folded(window[near_tile], odd_col == 1)
        far_out[plane] = folded(window[far_tile], odd_col == 0)


def side_call(window, near_row, far_row):
    shape = near((2, window.shape[1] // 2, LANES))
    return pl.pallas_call(
        side_kernel,
        out_shape=(near(window.shape), shape, shape),
        in_specs=[VMEM] * 3,
        out_specs=(VMEM,) * 3,
        compiler_params=PARAMS,
        name="side_columns",
    )(*in_vmem(window, near_row, far_row))


def finder(plan, slots, start, inner, live):
    def find(index):
        at = jnp.where(index < inner, start + index, jnp.maximum(slots - 1 - (index - inner), 0))
        is_live = index < live
        slot = plan[jnp.where(is_live, at, jnp.where(inner > 0, start, slots - 1))]
        place = slots + 2 + 3 * slot
        scale = jnp.where(is_live, 2.0, 0.0).astype(F32)
        return slot, plan[place], plan[place + 1], plan[place + 2], scale, jnp.where(is_live, slot, slots)

    return find


def run_slots(groups, size_of, first, find, window, turned, measured, table, exits, probe_sum):
    size = turned.shape[2]
    columns = window.shape[0] // 2
    lane = lax.broadcasted_iota(jnp.int32, (size, LANES), 1)
    exits[exits.shape[0] - 1] = jnp.zeros(exits.shape[1:], F32)

    def load(pair):
        kept, waves = [], []
        for slot, row, tile, turn, _, _ in pair:
            here = lane >= turn
            patch = [
                jnp.where(
                    here,
                    window[plane * columns + tile, pl.ds(row, size), :],
                    window[plane * columns + tile + 1, pl.ds(row, size), :],
                )
                for plane in range(2)
            ]
            probe = [turned[slot, plane] for plane in range(2)]
            wave_real = probe[0] * patch[0] - probe[1] * patch[1]
            wave_imag = probe[0] * patch[1] + probe[1] * patch[0]
            kept.append(patch)
            waves.append(jnp.concatenate([wave_real, wave_imag], axis=1))
        return kept, jnp.concatenate(waves, axis=0)

    def regroup(pair):
        return jnp.concatenate(
            [
                jnp.concatenate([pair[:size, :size], pair[size:, :size]], axis=1),
                jnp.concatenate([pair[:size, size:], pair[size:, size:]], axis=1),
            ],
            axis=0,
        )

    def weigh(pair, psi):
        real, imag = psi[:size], psi[size:]
        weights = []
        for member, (slot, _, _, _, scale, _) in enumerate(pair):
            lanes = slice(member * size, (member + 1) * size)
            power = real[:, lanes] * real[:, lanes] + imag[:, lanes] * imag[:, lanes]
            weights.append((power - measured[slot].astype(F32)) * scale)
        weight = jnp.concatenate(weights, axis=1)
        return jnp.concatenate([weight * real, weight * imag], axis=0)

    def add_up(pair, kept, pair_exits):
        for member, (_, _, _, turn, _, kept_at) in enumerate(pair):
            patch = kept[member]
            exit_real = pair_exits[member * size : (member + 1) * size, :size]
            exit_imag = pair_exits[member * size : (member + 1) * size, size:]
            exits[kept_at, 0] = exit_real
            exits[kept_at, 1] = exit_imag
            terms = (patch[0] * exit_real + patch[1] * exit_imag, patch[0] * exit_imag - patch[1] * exit_real)
            back = (LANES - turn) & (LANES - 1)
            for plane in range(2):
                probe_sum[plane] += pltpu.roll(terms[plane], back, axis=1)

    def step(group, carry):
        slots = [find(first + group * size_of + member) for member in range(size_of)]
        pairs = [slots[member : member + 2] for member in range(0, size_of, 2)]
        loaded = [load(pair) for pair in pairs]
        waves = [regroup(times_table(wave, table[0], table[1])) for _, wave in loaded]
        waves = [weigh(pair, table_times(table[2], table[3], wave)) for pair, wave in zip(pairs, waves)]
        waves = [regroup(table_times(table[0], table[1], wave)) for wave in waves]
        waves = [times_table(wave, table[2], table[3]) for wave in waves]
        for pair, (kept, _), wave in zip(pairs, loaded, waves):
            add_up(pair, kept, wave)
        return carry

    lax.fori_loop(0, groups, step, 0)


def inner_kernel(plan, window, turned, measured, table, exits, probe_sum):
    slots = measured.shape[0]
    probe_sum[...] = jnp.zeros_like(probe_sum)
    groups = plan[slots] // GROUP
    find = finder(plan, slots, 0, groups * GROUP, groups * GROUP)
    run_slots(groups, GROUP, 0, find, window, turned, measured, table, exits, probe_sum)


def inner_call(plan, window, turned, measured, tables):
    slots = measured.shape[0]
    return pl.pallas_call(
        inner_kernel,
        out_shape=(near((slots + 1,) + turned.shape[1:]), near(turned.shape[1:])),
        in_specs=[SMEM] + [VMEM] * 4,
        out_specs=(VMEM,) * 2,
        compiler_params=PARAMS,
        cost_estimate=pl.CostEstimate(flops=10**10, bytes_accessed=2 * 10**7, transcendentals=0),
        name="slots_inside",
    )(*in_smem(plan), *in_vmem(window, turned, measured, tables))


def outer_kernel(
    plan, window_ref, near_col_ref, far_col_ref, turned, measured, table, probe_ref,
    exits, mine_out, other_out, window, probe_sum,
):
    slots = measured.shape[0]
    margin = turned.shape[2] // 2
    columns = window.shape[0] // 2
    half = window.shape[1] // 2
    odd_row, odd_col = parities()
    probe_sum[...] = probe_ref[...]
    for plane in range(2):
        own = slice(plane * columns + 1, (plane + 1) * columns - 1)
        window[own] = window_ref[own]
        near_tile = plane * columns + jnp.where(odd_col == 1, 0, columns - 1)
        far_tile = plane * columns + jnp.where(odd_col == 1, columns - 1, 0)
        for tile, ref in ((near_tile, near_col_ref), (far_tile, far_col_ref)):
            window[tile, :half] = ref[plane]
            window[tile, half:] = pltpu.roll(ref[plane], margin, axis=1)
    start = plan[slots] // GROUP * GROUP
    live = plan[slots + 1] - start
    find = finder(plan, slots, start, plan[slots] - start, live)
    large = live // (2 * GROUP)
    run_slots(large, 2 * GROUP, 0, find, window, turned, measured, table, exits, probe_sum)
    first = large * 2 * GROUP
    run_slots((live - first + GROUP - 1) // GROUP, GROUP, first, find, window, turned, measured, table, exits, probe_sum)
    factor = 1.0 / np.sqrt(np.float32(lax.axis_size("trow") * lax.axis_size("tcol") * slots))
    mine_out[...] = probe_sum[odd_row] * factor
    other_out[...] = probe_sum[1 - odd_row] * factor


def outer_call(plan, window, near_col, far_col, turned, measured, tables, probe_sum):
    slots = measured.shape[0]
    part = near(probe_sum.shape[1:])
    return pl.pallas_call(
        outer_kernel,
        out_shape=(near((slots + 1,) + turned.shape[1:]), part, part),
        in_specs=[SMEM] + [VMEM] * 7,
        out_specs=(VMEM,) * 3,
        scratch_shapes=[pltpu.VMEM(window.shape, F32), pltpu.VMEM(probe_sum.shape, F32)],
        compiler_params=PARAMS,
        cost_estimate=pl.CostEstimate(flops=10**10, bytes_accessed=2 * 10**7, transcendentals=0),
        name="slots_across",
    )(*in_smem(plan), *in_vmem(window, near_col, far_col, turned, measured, tables, probe_sum))


def add_objects(groups, find, turned, exits, grad):
    size = turned.shape[2]
    columns = grad.shape[0] // 2
    lane = lax.broadcasted_iota(jnp.int32, (size, LANES), 1)

    def step(index, carry):
        for member in range(ADDED):
            slot, row, tile, turn, _, kept_at = find(index * ADDED + member)
            here = lane >= turn
            probe = [turned[slot, plane] for plane in range(2)]
            exit_real, exit_imag = exits[kept_at, 0], exits[kept_at, 1]
            adds = (probe[0] * exit_real + probe[1] * exit_imag, probe[0] * exit_imag - probe[1] * exit_real)
            for plane in range(2):
                at = plane * columns + tile
                grad[at, pl.ds(row, size), :] += jnp.where(here, adds[plane], 0.0)
                grad[at + 1, pl.ds(row, size), :] += jnp.where(here, 0.0, adds[plane])
        return carry

    lax.fori_loop(0, groups, step, 0)


def first_object_kernel(plan, turned, exits, grad):
    slots = turned.shape[0]
    grad[...] = jnp.zeros_like(grad)
    start = plan[slots] // GROUP * GROUP
    add_objects(start // ADDED, finder(plan, slots, 0, start, start), turned, exits, grad)


def first_object_call(plan, window, turned, exits):
    return pl.pallas_call(
        first_object_kernel,
        out_shape=near(window.shape),
        in_specs=[SMEM] + [VMEM] * 2,
        out_specs=VMEM,
        compiler_params=PARAMS,
        cost_estimate=pl.CostEstimate(flops=10**9, bytes_accessed=10**5, transcendentals=0),
        name="object_inside",
    )(*in_smem(plan), *in_vmem(turned, exits))


def object_kernel(plan, turned, exits, grad_ref, grad, near_row_out, far_row_out, side_out):
    slots = turned.shape[0]
    margin = turned.shape[2] // 2
    columns = grad.shape[0] // 2
    tall = grad.shape[1]
    odd_row, _ = parities()
    near, far = place_of(odd_row, 0, tall - margin)
    grad[...] = grad_ref[...]
    start = plan[slots] // GROUP * GROUP
    live = plan[slots + 1] - start
    find = finder(plan, slots, start, plan[slots] - start, live)
    add_objects((live + ADDED - 1) // ADDED, find, turned, exits, grad)
    narrow = lax.broadcasted_iota(jnp.int32, (margin, LANES), 1) < margin
    for plane in range(2):
        base = plane * columns
        left, right = base, base + columns - 1
        for at, out in ((near, near_row_out), (far, far_row_out)):
            rows = pl.ds(at, margin)
            for tile in range(columns - 2):
                out[plane, :, tile * LANES : (tile + 1) * LANES] = grad[base + 1 + tile, rows, :]
            out[plane, :, (columns - 2) * LANES :] = jnp.where(narrow, grad[right, rows, :], grad[left, rows, :])
        for row in range(margin, tall - margin, margin):
            rows = slice(row, row + margin)
            side_out[plane, row - margin : row] = jnp.where(narrow, grad[right, rows, :], grad[left, rows, :])


def object_call(plan, turned, exits, grad):
    size = turned.shape[2]
    row = near((2, size // 2, (grad.shape[0] // 2 - 1) * LANES))
    return pl.pallas_call(
        object_kernel,
        out_shape=(near(grad.shape), row, row, near((2, grad.shape[1] - size, LANES))),
        in_specs=[SMEM] + [VMEM] * 3,
        out_specs=(VMEM,) * 4,
        compiler_params=PARAMS,
        cost_estimate=pl.CostEstimate(flops=10**9, bytes_accessed=10**5, transcendentals=0),
        name="object_across",
    )(*in_smem(plan), *in_vmem(turned, exits, grad))


def side_sum_kernel(side_ref, near_ref, far_ref, near_out, far_out, side):
    margin = near_ref.shape[1]
    height = side_ref.shape[1]
    odd_row, odd_col = parities()
    near_at, far_at = place_of(odd_row, 0, height - margin)
    wide = near_ref.shape[2]
    side[...] = side_ref[...]
    for plane in range(2):
        side[plane, pl.ds(near_at, margin), :] += near_ref[plane, :, wide - LANES :]
        side[plane, pl.ds(far_at, margin), :] += far_ref[plane, :, wide - LANES :]
    for plane in range(2):
        near_out[plane] = folded(side[plane], odd_col == 0)
        far_out[plane] = folded(side[plane], odd_col == 1)


def side_sum_call(side, near_row, far_row):
    shape = near((2, side.shape[1] // 2, LANES))
    return pl.pallas_call(
        side_sum_kernel,
        out_shape=(shape, shape),
        in_specs=[VMEM] * 3,
        out_specs=(VMEM, VMEM),
        scratch_shapes=[pltpu.VMEM(side.shape, F32)],
        compiler_params=PARAMS,
        name="side_sums",
    )(*in_vmem(side, near_row, far_row))


def final_kernel(grad, near_row_ref, far_row_ref, near_col_ref, far_col_ref, out_ref):
    height, width = out_ref.shape[1:]
    columns = grad.shape[0] // 2
    margin = near_row_ref.shape[1]
    half = height // 2
    odd_row, odd_col = parities()
    near_at, far_at = place_of(odd_row, 0, height - margin)
    narrow = lax.broadcasted_iota(jnp.int32, (half, LANES), 1) < LANES // 2
    for plane in range(2):
        for tile in range(columns - 2):
            lanes = slice(tile * LANES, (tile + 1) * LANES)
            out_ref[plane, :, lanes] = grad[plane * columns + 1 + tile, margin : margin + height]
        near = jnp.where(odd_col == 1, near_col_ref[plane], far_col_ref[plane])
        far = jnp.where(odd_col == 1, far_col_ref[plane], near_col_ref[plane])
        for first, left, right in (
            (0, near, far),
            (half, pltpu.roll(near, LANES // 2, axis=1), pltpu.roll(far, LANES // 2, axis=1)),
        ):
            rows = slice(first, first + half)
            out_ref[plane, rows, :LANES] += jnp.where(narrow, left, 0.0)
            out_ref[plane, rows, width - LANES :] += jnp.where(narrow, 0.0, right)
        out_ref[plane, pl.ds(near_at, margin), :] += near_row_ref[plane, :, :width]
        out_ref[plane, pl.ds(far_at, margin), :] += far_row_ref[plane, :, :width]


def final_call(grad, near_row, far_row, near_col, far_col):
    margin = near_row.shape[1]
    shape = (2, grad.shape[1] - 2 * margin, near_row.shape[2] - LANES)
    return pl.pallas_call(
        final_kernel,
        out_shape=jax.ShapeDtypeStruct(shape, F32),
        in_specs=[VMEM] * 5,
        out_specs=VMEM,
        compiler_params=PARAMS,
        name="final_sums",
    )(*in_vmem(grad, near_row, far_row, near_col, far_col))


def near_swap(value, axis):
    return lax.ppermute(value, axis, [(i, i ^ 1) for i in range(lax.axis_size(axis))])


def far_swap(value, axis):
    pairs = [(i, i + 1) for i in range(1, lax.axis_size(axis) - 1, 2)]
    return lax.ppermute(value, axis, pairs + [(j, i) for i, j in pairs])


def doubling_steps(n_row, n_col):
    along_cols = [(0, 1)] + [(0, 1 << k) for k in range(1, n_col.bit_length() - 1)][::-1]
    along_rows = [(1 << k, 0) for k in range(1, n_row.bit_length() - 1)]
    return along_rows, along_cols


def add_kernel(a_ref, b_ref, out_ref):
    out_ref[...] = a_ref[...] + b_ref[...]


def add_call(a, b):
    return pl.pallas_call(
        add_kernel,
        out_shape=near(a.shape),
        in_specs=[VMEM] * 2,
        out_specs=VMEM,
        compiler_params=PARAMS,
        cost_estimate=pl.CostEstimate(flops=10**9, bytes_accessed=10**5, transcendentals=0),
        name="add",
    )(*in_vmem(a, b))


def add_partner(mine, step, add=jnp.add):
    n_row, n_col = lax.axis_size("trow"), lax.axis_size("tcol")
    pairs = [(r * n_col + c, (r ^ step[0]) * n_col + (c ^ step[1])) for r in range(n_row) for c in range(n_col)]
    return add(mine, lax.ppermute(mine, ("trow", "tcol"), pairs))


def body(table, object_planes, probe, intensities, row_offsets, col_offsets, counts):
    size = probe.shape[1]
    rows, cols = row_offsets.reshape(-1), col_offsets.reshape(-1)
    measured = intensities.reshape(-1, size, size)
    near_row, far_row = edge_call(object_planes, size // 2)
    far_row = far_swap(far_row, "trow")
    near_row = near_swap(near_row, "trow")
    plan, turned, measured, tables, window = ready_call(rows, cols, counts, probe, measured, table, object_planes)
    window, near_side, far_side = side_call(window, near_row, far_row)
    far_col = far_swap(far_side, "tcol")
    near_col = near_swap(near_side, "tcol")
    inner_exits, probe_sum = inner_call(plan, window, turned, measured, tables)
    outer_exits, mine, other = outer_call(plan, window, near_col, far_col, turned, measured, tables, probe_sum)

    along_rows, along_cols = doubling_steps(lax.axis_size("trow"), lax.axis_size("tcol"))
    other, inner_exits = lax.optimization_barrier((other, inner_exits))
    grad = first_object_call(plan, window, turned, inner_exits)
    mine = mine + near_swap(other, "trow")
    mine, outer_exits = lax.optimization_barrier((mine, outer_exits))
    grad, near_row, far_row, side = object_call(plan, turned, outer_exits, grad)
    near_row = near_swap(near_row, "trow")
    far_row = far_swap(far_row, "trow")
    mine = add_partner(mine, along_cols[0])
    mine = add_partner(mine, along_cols[1], add=add_call)
    near_side, far_side = side_sum_call(side, near_row, far_row)
    mine, near_side, far_side = lax.optimization_barrier((mine, near_side, far_side))
    near_col = near_swap(near_side, "tcol")
    far_col = far_swap(far_side, "tcol")
    for step in along_cols[2:] + along_rows:
        mine = add_partner(mine, step)
    mine, near_col, far_col = lax.optimization_barrier((mine, near_col, far_col))
    object_grad = final_call(grad, near_row, far_row, near_col, far_col)
    other = near_swap(mine, "trow")
    odd_row, _ = parities()
    probe_grad = jnp.where(odd_row == 0, jnp.stack([mine, other]), jnp.stack([other, mine]))
    return (object_grad, probe_grad)


def solution(mesh):
    table = dft_tables(LANES)
    inner = jax.shard_map(
        body,
        mesh=mesh,
        in_specs=(
            P(),
            P(None, "trow", "tcol"),
            P(),
            P("trow", "tcol", None, None, None),
            P("trow", "tcol", None),
            P("trow", "tcol", None),
            P(("trow", "tcol")),
        ),
        out_specs=(P(None, "trow", "tcol"), P()),
        check_vma=False,
    )

    def run(*args):
        return inner(jnp.asarray(table), *args)

    return run
```
